32 devices in a mesh: lon: 32 (over z, y, x, core), lat: 1.
Axes of the slice: x: 2, y: 2, z: 4, core: 2. Of those that a mesh axis runs over, the one named last changes fastest.
Arguments:
- inputs: bfloat16 [32, 1024, 192], P('lat', 'lon'), may hold values from -6 to 6
- cotangent: bfloat16 [32, 1024, 192], P('lat', 'lon'), may hold values from -6 to 6
- first_weight: bfloat16 [3, 3, 192, 192], replicated, may hold values from -0.15625 to 0.15625
- second_weight: bfloat16 [3, 3, 192, 192], replicated, may hold values from -0.15625 to 0.15625
Outputs:
- input_gradient: bfloat16 [32, 1024, 192], P('lat', 'lon')
- first_kernel_gradient: float32 [3, 3, 192, 192], replicated
- second_kernel_gradient: float32 [3, 3, 192, 192], replicated
The draws below stay inside these ranges and needn't reach their ends.
All inputs are finite; a program needn't handle non-finite values.
Results may differ from the reference program's by a relative error of at most 0.0049.
Values may be sent and summed in bfloat16 or wider, within the bound.
No kernel may reach another device: no remote copies, remote signals or barrier semaphores. Data moves between devices by JAX's collectives and lax.ppermute only.
A program may use at most 128 MiB of HBM per device.

```python
import math
import jax
import jax.numpy as jnp

C = 192
FIRST_SPREAD = 32
SECOND_SPREAD = 64
LAT = 32
LON = 1024


def block_scale(own_key, dims, pieces, least, high):
    factor_of = 1.0
    for dim, shards_of in pieces:
        draws = jax.random.uniform(jax.random.fold_in(jax.random.fold_in(own_key, 6), dim), (shards_of,), jnp.float32, least / len(pieces), high / len(pieces))
        factor_of = factor_of * jnp.repeat(jnp.exp(draws), dims[dim] // shards_of).reshape((-1,) + (1,) * (len(dims) - 1 - dim))
    return factor_of


def noise(stream_key, shape, deviation, reach, shards=(), dtype=jnp.bfloat16):
    values = deviation * jax.random.normal(stream_key, shape, jnp.float32)
    if shards:
        values = values * block_scale(stream_key, shape, shards, -0.22, 0.18)
    return jnp.clip(values, -reach, reach).astype(dtype)


def setup_inputs(seed: int = 0) -> dict:
    streams_of = jax.random.split(jax.random.key(seed), 5)
    inputs = noise(streams_of[0], (LAT, LON, C), 1.0, 6.0, ((1, 32),))
    cotangent = noise(streams_of[1], (LAT, LON, C), 1.0, 6.0, ((1, 32),))
    first_weight = noise(streams_of[2], (3, 3, C, C), (9 * C) ** -0.5, 0.15625)
    second_weight = noise(streams_of[3], (3, 3, C, C), (9 * C) ** -0.5, 0.15625)
    return dict(inputs=inputs, cotangent=cotangent, first_weight=first_weight, second_weight=second_weight)


def shifted_taps(field, dilation):
    padded = jnp.pad(field, ((1, 1), (0, 0), (0, 0)))
    height = field.shape[0]
    result = []
    for row_off in (-1, 0, 1):
        band = padded[1 + row_off:1 + row_off + height]
        for col_off in (-1, 0, 1):
            result.append(jnp.roll(band, -col_off * dilation, axis=1))
    return result

def apply_convolution(field, weight, dilation):
    channels = field.shape[2]
    shape = (field.shape[0], field.shape[1], weight.shape[3])
    total = jnp.zeros(shape, jnp.float32)
    for index, tapped in enumerate(shifted_taps(field, dilation)):
        product = jnp.dot(tapped.reshape(-1, channels), weight[index // 3, index % 3], preferred_element_type=jnp.float32)
        total = total + product.reshape(shape)
    return total

def cross_correlate(field, other, dilation):
    channels = field.shape[2]
    flat_other = other.reshape(-1, channels)
    blocks = []
    for tapped in shifted_taps(field, dilation):
        blocks.append(jnp.dot(tapped.reshape(-1, channels).T, flat_other, preferred_element_type=jnp.float32))
    return jnp.stack(blocks).reshape(3, 3, channels, channels)

def flipped_kernel(weight):
    return jnp.transpose(weight[::-1, ::-1], (0, 1, 3, 2))

def reference(inputs, cotangent, first_weight, second_weight):
    gradient_scale = 1.0 / math.sqrt(LAT * LON)
    pre_activation = apply_convolution(inputs, first_weight, FIRST_SPREAD)
    hidden_state = jax.nn.silu(pre_activation).astype(jnp.bfloat16)
    hidden_gradient = apply_convolution(cotangent, flipped_kernel(second_weight), SECOND_SPREAD)
    second_kernel_gradient = cross_correlate(hidden_state, cotangent, SECOND_SPREAD) * gradient_scale
    sigma = jax.nn.sigmoid(pre_activation)
    pre_activation_gradient = (hidden_gradient * sigma * (1.0 + pre_activation * (1.0 - sigma))).astype(jnp.bfloat16)
    input_gradient = apply_convolution(pre_activation_gradient, flipped_kernel(first_weight), FIRST_SPREAD).astype(jnp.bfloat16)
    first_kernel_gradient = cross_correlate(inputs, pre_activation_gradient, FIRST_SPREAD) * gradient_scale
    return (input_gradient, first_kernel_gradient, second_kernel_gradient)
```

```python
import math

import jax
import jax.numpy as jnp
from jax import lax
from jax.experimental import pallas as pl
from jax.experimental.pallas import tpu as pltpu
from jax.sharding import PartitionSpec as P

FIRST_SPREAD = 32
SECOND_SPREAD = 64
LANES = 128
ROW_TILE = 16
VMEM_LIMIT = 48 * 1024 * 1024


def call(body, outs, args, scratch=(), flops=0, name=None):
    moved = sum(a.size * a.dtype.itemsize for a in list(args) + list(outs))
    return pl.pallas_call(
        body,
        out_shape=list(outs),
        in_specs=[pl.BlockSpec(memory_space=pltpu.VMEM)] * len(args),
        out_specs=[pl.BlockSpec(memory_space=pltpu.VMEM)] * len(outs),
        scratch_shapes=list(scratch),
        compiler_params=pltpu.CompilerParams(vmem_limit_bytes=VMEM_LIMIT),
        cost_estimate=pl.CostEstimate(flops=flops, bytes_accessed=moved, transcendentals=0),
        name=name,
    )(*args)


def shape_of(shape, dtype):
    return jax.ShapeDtypeStruct(shape, dtype)


def packs(rows, channels):
    return channels % LANES * 2 == LANES and rows % (2 * ROW_TILE) == 0


def packed_shape(rows, channels):
    if not packs(rows, channels):
        return (rows, channels)
    full = channels // LANES
    return (rows * full + rows // 2, LANES)


def pack_into(ref, value):
    rows, channels = value.shape
    if not packs(rows, channels):
        ref[...] = value
        return
    full = channels // LANES
    for tile in range(full):
        ref[tile * rows : (tile + 1) * rows, :] = value[:, tile * LANES : (tile + 1) * LANES]
    rest = value[:, full * LANES :]
    half = rows // 2
    ref[full * rows :, :] = jnp.concatenate([rest[:half], rest[half:]], axis=1)


def unpacked(ref, rows, channels):
    if not packs(rows, channels):
        return ref[...]
    full = channels // LANES
    rest = ref[full * rows :, :]
    width = channels - full * LANES
    tail = jnp.concatenate([rest[:, :width], rest[:, width:]], axis=0)
    return jnp.concatenate([ref[t * rows : (t + 1) * rows, :] for t in range(full)] + [tail], axis=1)


def extend(scratch, value, rim, width):
    rows = value.shape[0]
    scratch[width : width + rows, :] = value
    if rim is None:
        blank = jnp.zeros((width, value.shape[1]), value.dtype)
        scratch[:width, :] = blank
        scratch[width + rows :, :] = blank
    else:
        scratch[:width, :] = rim[:width, :]
        scratch[width + rows :, :] = rim[width:, :]


def row_blocks(rows):
    size = rows
    while size > 256 and size % 2 == 0 and size // 2 % ROW_TILE == 0:
        size //= 2
    return [(start, size) for start in range(0, rows, size)]


NT = (((1,), (1,)), ((), ()))
NN = (((1,), (0,)), ((), ()))


def conv_block(terms, start, size, width):
    total = None
    for ext, weight, b, flipped in terms:
        for a in (-1, 0, 1):
            tap = ext[start + (1 + a) * width : start + (1 + a) * width + size, :]
            kernel = weight[1 - a, 1 - b] if flipped else weight[1 + a, 1 + b]
            part = lax.dot_general(tap, kernel, NT if flipped else NN, preferred_element_type=jnp.float32)
            total = part if total is None else total + part
    return total


def flat_rows(channels, pieces):
    if channels % LANES * 2 != LANES:
        rows = 9 * channels * (-(-channels // LANES))
    else:
        rows = 9 * channels * channels // LANES
    unit = pieces * ROW_TILE
    return -(-rows // unit) * unit


def store_flat(ref, lead, blocks):
    channels = blocks[0].shape[0]
    full = channels // LANES
    row = 0
    for block in blocks:
        for tile in range(full):
            ref[lead, row : row + channels, :] = block[:, tile * LANES : (tile + 1) * LANES]
            row += channels
    width = channels - full * LANES
    if width == 0:
        return
    rests = [block[:, full * LANES :] for block in blocks]
    if width * 2 != LANES:
        for rest in rests:
            ref[lead, row : row + channels, :width] = rest
            row += channels
        return
    for pair in range(0, 8, 2):
        ref[lead, row : row + channels, :] = jnp.concatenate([rests[pair], rests[pair + 1]], axis=1)
        row += channels
    half = channels // 2
    ref[lead, row : row + half, :] = jnp.concatenate([rests[8][:half], rests[8][half:]], axis=1)


def load_flat(ref, lead, channels):
    full = channels // LANES
    row = 0
    parts = []
    for _ in range(9):
        tiles = []
        for _ in range(full):
            tiles.append(ref[lead, row : row + channels, :])
            row += channels
        parts.append(tiles)
    width = channels - full * LANES
    if width == 0:
        pass
    elif width * 2 != LANES:
        for tap in range(9):
            parts[tap].append(ref[lead, row : row + channels, :width])
            row += channels
    else:
        for pair in range(0, 8, 2):
            both = ref[lead, row : row + channels, :]
            parts[pair].append(both[:, :width])
            parts[pair + 1].append(both[:, width:])
            row += channels
        both = ref[lead, row : row + channels // 2, :]
        parts[8].append(jnp.concatenate([both[:, :width], both[:, width:]], axis=0))
    return [jnp.concatenate(p, axis=1) if len(p) > 1 else p[0] for p in parts]


def radices(count):
    found = []
    if count % 2 == 0:
        found.append(2)
        count //= 2
    while count % 4 == 0:
        found.append(4)
        count //= 4
    while count % 2 == 0:
        found.append(2)
        count //= 2
    return found if count == 1 else None


def swapped(value, count, stride, k):
    return lax.ppermute(value, "lon", [(i, i ^ (k * stride)) for i in range(count)])


def moved(value, steps):
    count = lax.axis_size("lon")
    if steps % count == 0:
        return value
    return lax.ppermute(value, "lon", [(i, (i + steps) % count) for i in range(count)])


def lat_rim(field):
    count = lax.axis_size("lat")
    if count == 1:
        return None
    north = lax.ppermute(field[-1], "lat", [(i, i + 1) for i in range(count - 1)])
    south = lax.ppermute(field[0], "lat", [(i + 1, i) for i in range(count - 1)])
    return jnp.stack([north, south])


def beside(field, packed, spread, pack):
    width = field.shape[1]
    steps, rest = divmod(spread, width)
    if rest == 0:
        return moved(packed, steps), moved(packed, -steps)
    cut = width - rest
    west = jnp.concatenate([moved(field[:, cut:], steps + 1), moved(field[:, :cut], steps)], axis=1)
    east = jnp.concatenate([moved(field[:, rest:], -steps), moved(field[:, :rest], -steps - 1)], axis=1)
    return pack(west), pack(east)


def shards(inputs, cotangent, first_weight, second_weight):
    height, width, channels = inputs.shape
    rows = height * width
    count = lax.axis_size("lon")
    scale = 1.0 / math.sqrt(rows * lax.axis_size("lat") * count)
    bf16, f32 = jnp.bfloat16, jnp.float32
    pshape = packed_shape(rows, channels)
    ext_shape = (rows + 2 * width, channels)
    ext = pltpu.VMEM(ext_shape, bf16)
    tap_flops = 2 * rows * channels * channels
    blocks = row_blocks(rows)

    def pack_body(*refs):
        half = len(refs) // 2
        for source, target in zip(refs[:half], refs[half:]):
            pack_into(target, source[...])

    def pack(*fields):
        flat = [f.reshape(rows, channels) for f in fields]
        return call(pack_body, [shape_of(pshape, bf16)] * len(flat), flat, name="pack")

    def pack_one(field):
        return pack(field)[0]

    def rims_of(field, spread):
        rim = lat_rim(field)
        if rim is None:
            return []
        west, east = beside(rim, rim, spread, lambda r: r)
        return [r.reshape(2 * width, channels) for r in (rim, west, east)]

    x = inputs.reshape(rows, channels)
    g = cotangent.reshape(rows, channels)
    x_rims = rims_of(inputs, FIRST_SPREAD)
    g_rims = rims_of(cotangent, SECOND_SPREAD)
    rimmed = bool(x_rims)

    x_packed, g_packed = pack(inputs, cotangent)
    x_west, x_east = beside(inputs, x_packed, FIRST_SPREAD, pack_one)
    g_west, g_east = beside(cotangent, g_packed, SECOND_SPREAD, pack_one)

    def own_body(x_ref, g_ref, w1_ref, w2_ref, *rest):
        rims, (part1, part2, xe, ge) = (rest[:2], rest[2:]) if rimmed else ((None, None), rest)
        extend(xe, x_ref[...], rims[0], width)
        extend(ge, g_ref[...], rims[1], width)
        for start, size in blocks:
            part1[start : start + size, :] = conv_block([(xe, w1_ref, 0, False)], start, size, width)
        for start, size in blocks:
            part2[start : start + size, :] = conv_block([(ge, w2_ref, 0, True)], start, size, width)

    part1, part2 = call(
        own_body,
        [shape_of((rows, channels), f32)] * 2,
        [x, g, first_weight, second_weight] + x_rims[:1] + g_rims[:1],
        [ext, ext],
        flops=6 * tap_flops,
        name="own_columns",
    )

    def hidden_body(part_ref, west_ref, east_ref, w_ref, *rest):
        rims, (hidden_t, slope, we, ee, hid) = (rest[:2], rest[2:]) if rimmed else ((None, None), rest)
        extend(we, unpacked(west_ref, rows, channels), rims[0], width)
        extend(ee, unpacked(east_ref, rows, channels), rims[1], width)
        for start, size in blocks:
            act = part_ref[start : start + size, :] + conv_block(
                [(we, w_ref, -1, False), (ee, w_ref, 1, False)], start, size, width
            )
            sigma = jax.nn.sigmoid(act)
            slope[start : start + size, :] = sigma * (1.0 + act * (1.0 - sigma))
            hid[start : start + size, :] = (act * sigma).astype(bf16).astype(f32)
        hidden_t[...] = hid[...].T.astype(bf16)

    hidden_t, slope = call(
        hidden_body,
        [shape_of((channels, rows), bf16), shape_of((rows, channels), f32)],
        [part1, x_west, x_east, first_weight] + x_rims[1:],
        [ext, ext, pltpu.VMEM((rows, channels), f32)],
        flops=6 * tap_flops,
        name="hidden",
    )

    def grad_body(part_ref, slope_ref, west_ref, east_ref, w_ref, *rest):
        rims, (pre_grad, packed, we, ee) = (rest[:2], rest[2:]) if rimmed else ((None, None), rest)
        extend(we, unpacked(west_ref, rows, channels), rims[0], width)
        extend(ee, unpacked(east_ref, rows, channels), rims[1], width)
        for start, size in blocks:
            grad = part_ref[start : start + size, :] + conv_block(
                [(we, w_ref, -1, True), (ee, w_ref, 1, True)], start, size, width
            )
            pre_grad[start : start + size, :] = (grad * slope_ref[start : start + size, :]).astype(bf16)
        pack_into(packed, pre_grad[...])

    pre_grad, pre_packed = call(
        grad_body,
        [shape_of((rows, channels), bf16), shape_of(pshape, bf16)],
        [part2, slope, g_west, g_east, second_weight] + g_rims[1:],
        [ext, ext],
        flops=6 * tap_flops,
        name="pre_grad",
    )
    pre_field = pre_grad.reshape(height, width, channels)
    p_west, p_east = beside(pre_field, pre_packed, FIRST_SPREAD, pack_one)
    p_rims = rims_of(pre_field, FIRST_SPREAD)

    stages = radices(count)
    pieces = count // 2 if stages else 1
    flat = flat_rows(channels, pieces)

    def kernels_body(hidden_t, pre_ref, x_ref, xw_ref, xe_ref, g_ref, gw_ref, ge_ref, *rest):
        rims, rest = (rest[:6], rest[6:]) if rimmed else ((None,) * 6, rest)
        own, send, both, e0, e1, e2, f0, f1, f2 = rest
        extend(e0, unpacked(gw_ref, rows, channels), rims[4], width)
        extend(e1, g_ref[...], rims[3], width)
        extend(e2, unpacked(ge_ref, rows, channels), rims[5], width)
        extend(f0, unpacked(xw_ref, rows, channels), rims[1], width)
        extend(f1, x_ref[...], rims[0], width)
        extend(f2, unpacked(xe_ref, rows, channels), rims[2], width)

        def window(field, a):
            return field[(1 + a) * width : (1 + a) * width + rows, :]

        second = []
        for a in (-1, 0, 1):
            for b in (-1, 0, 1):
                tap = window((e0, e1, e2)[1 - b], -a)
                second.append(jnp.dot(hidden_t[...], tap, preferred_element_type=f32))
        used = flat_rows(channels, 1) // ROW_TILE * ROW_TILE
        if used < flat:
            both[:, used - ROW_TILE :, :] = jnp.zeros((2, flat - used + ROW_TILE, LANES), f32)
        store_flat(both, 0, second)
        pre_t = pre_ref[...].astype(f32).T.astype(bf16)
        first = []
        for a in (-1, 0, 1):
            for b in (-1, 0, 1):
                first.append(jnp.dot(pre_t, window((f0, f1, f2)[1 + b], a), preferred_element_type=f32))
        store_flat(both, 1, first)
        mine = lax.rem(lax.axis_index("lon"), 2)
        own[...] = both[mine]
        send[...] = both[1 - mine].astype(bf16)

    own, send = call(
        kernels_body,
        [shape_of((flat, LANES), f32), shape_of((flat, LANES), bf16)],
        [hidden_t, pre_grad, x, x_west, x_east, g, g_west, g_east] + x_rims + g_rims,
        [pltpu.VMEM((2, flat, LANES), f32)] + [ext] * 6,
        flops=18 * tap_flops,
        name="kernel_gradients",
    )

    index = lax.axis_index("lon")
    total = own + swapped(send, count, 1, 1).astype(f32)
    stride = 2
    for radix in stages[1:]:
        digit = index // stride % radix
        split = total.reshape(radix, -1, LANES)
        parts = [
            swapped(
                lax.dynamic_index_in_dim(split, digit ^ k, 0, keepdims=False).astype(bf16), count, stride, k
            )
            for k in range(1, radix)
        ]
        total = lax.dynamic_index_in_dim(split, digit, 0, keepdims=False)
        for part in parts:
            total = total + part.astype(f32)
        stride *= radix
    if lax.axis_size("lat") > 1:
        total = lax.psum(total, "lat")
    held = total.astype(bf16)
    for radix in reversed(stages[2:]):
        stride //= radix
        held = jnp.concatenate([held] + [swapped(held, count, stride, k) for k in range(1, radix)], axis=0)
    group = stages[1]
    quarter = [held] + [swapped(held, count, 2, k) for k in range(1, group)]
    sibling = [swapped(q, count, 1, 1) for q in quarter]

    def own_grad_body(p_ref, w_ref, *rest):
        rim, (part, pe) = (rest[0], rest[1:]) if rimmed else (None, rest)
        extend(pe, p_ref[...], rim, width)
        for start, size in blocks:
            part[start : start + size, :] = conv_block([(pe, w_ref, 0, True)], start, size, width)

    (part3,) = call(
        own_grad_body,
        [shape_of((rows, channels), f32)],
        [pre_grad, first_weight] + p_rims[:1],
        [ext],
        flops=3 * tap_flops,
        name="own_input_gradient",
    )

    def input_body(part_ref, west_ref, east_ref, w_ref, *rest):
        rims, (out, we, ee) = (rest[:2], rest[2:]) if rimmed else ((None, None), rest)
        extend(we, unpacked(west_ref, rows, channels), rims[0], width)
        extend(ee, unpacked(east_ref, rows, channels), rims[1], width)
        for start, size in blocks:
            grad = part_ref[start : start + size, :] + conv_block(
                [(we, w_ref, -1, True), (ee, w_ref, 1, True)], start, size, width
            )
            out[start : start + size, :] = grad.astype(bf16)

    (input_gradient,) = call(
        input_body,
        [shape_of((rows, channels), bf16)],
        [part3, p_west, p_east, first_weight] + p_rims[1:],
        [ext, ext],
        flops=6 * tap_flops,
        name="input_gradient",
    )

    rest_radices = stages[2:]
    unit = flat // pieces

    def final_body(*refs):
        quarters, (first_out, second_out, both) = refs[: 2 * group], refs[2 * group :]
        place = lax.axis_index("lon")
        mine = lax.rem(place, 2)
        for side in range(2):
            lead = mine if side == 0 else 1 - mine
            for k in range(group):
                begin = (lax.rem(place // 2, group) ^ k) * (pieces // group)
                parts = [(begin, 0)]
                stride, span = 2 * group, pieces // group
                offset_parts = [(begin, 0, span)]
                walk = [(begin, 0)]
                for radix in rest_radices:
                    digit = lax.rem(place // stride, radix)
                    span //= radix
                    walk = [
                        (at + (digit ^ j) * span, order + j * span) for at, order in walk for j in range(radix)
                    ]
                    stride *= radix
                for at, order in walk:
                    both[lead, pl.ds(pl.multiple_of(at * unit, unit), unit), :] = quarters[side * group + k][
                        order * unit : (order + 1) * unit, :
                    ].astype(f32)
        second = load_flat(both, 0, channels)
        first = load_flat(both, 1, channels)
        for tap in range(9):
            second_out[tap // 3, tap % 3] = second[tap] * scale
            first_out[tap // 3, tap % 3] = first[tap].T * scale

    first_gradient, second_gradient = call(
        final_body,
        [shape_of((3, 3, channels, channels), f32)] * 2,
        quarter + sibling,
        [pltpu.VMEM((2, flat, LANES), f32)],
        name="unpack_gradients",
    )
    return (input_gradient.reshape(height, width, channels), first_gradient, second_gradient)


def solution(mesh):
    placed = (P("lat", "lon", None), P("lat", "lon", None), P(), P())
    return jax.shard_map(
        shards,
        mesh=mesh,
        in_specs=placed,
        out_specs=(P("lat", "lon", None), P(), P()),
        check_vma=False,
    )
```

```python
import math

import jax
import jax.numpy as jnp
from jax import lax
from jax.experimental import pallas as pl
from jax.experimental.pallas import tpu as pltpu
from jax.sharding import PartitionSpec as P

FIRST_SPREAD = 32
SECOND_SPREAD = 64
LANES = 128
ROW_TILE = 16
VMEM_LIMIT = 48 * 1024 * 1024


def call(body, outs, args, scratch=(), flops=0, name=None):
    moved = sum(a.size * a.dtype.itemsize for a in list(args) + list(outs))
    return pl.pallas_call(
        body,
        out_shape=list(outs),
        in_specs=[pl.BlockSpec(memory_space=pltpu.VMEM)] * len(args),
        out_specs=[pl.BlockSpec(memory_space=pltpu.VMEM)] * len(outs),
        scratch_shapes=list(scratch),
        compiler_params=pltpu.CompilerParams(vmem_limit_bytes=VMEM_LIMIT),
        cost_estimate=pl.CostEstimate(flops=flops, bytes_accessed=moved, transcendentals=0),
        name=name,
    )(*args)


def shape_of(shape, dtype):
    return jax.ShapeDtypeStruct(shape, dtype)


def packs(rows, channels):
    return channels % LANES * 2 == LANES and rows % (2 * ROW_TILE) == 0


def packed_shape(rows, channels):
    if not packs(rows, channels):
        return (rows, channels)
    full = channels // LANES
    return (rows * full + rows // 2, LANES)


def pack_into(ref, value):
    rows, channels = value.shape
    if not packs(rows, channels):
        ref[...] = value
        return
    full = channels // LANES
    for tile in range(full):
        ref[tile * rows : (tile + 1) * rows, :] = value[:, tile * LANES : (tile + 1) * LANES]
    rest = value[:, full * LANES :]
    half = rows // 2
    ref[full * rows :, :] = jnp.concatenate([rest[:half], rest[half:]], axis=1)


def unpacked(ref, rows, channels):
    if not packs(rows, channels):
        return ref[...]
    full = channels // LANES
    rest = ref[full * rows :, :]
    width = channels - full * LANES
    tail = jnp.concatenate([rest[:, :width], rest[:, width:]], axis=0)
    return jnp.concatenate([ref[t * rows : (t + 1) * rows, :] for t in range(full)] + [tail], axis=1)


def extend(scratch, value, rim, width):
    rows = value.shape[0]
    scratch[width : width + rows, :] = value
    if rim is None:
        blank = jnp.zeros((width, value.shape[1]), value.dtype)
        scratch[:width, :] = blank
        scratch[width + rows :, :] = blank
    else:
        scratch[:width, :] = rim[:width, :]
        scratch[width + rows :, :] = rim[width:, :]


def row_blocks(rows):
    size = rows
    while size > 256 and size % 2 == 0 and size // 2 % ROW_TILE == 0:
        size //= 2
    return [(start, size) for start in range(0, rows, size)]


NT = (((1,), (1,)), ((), ()))
NN = (((1,), (0,)), ((), ()))


def conv_block(terms, start, size, width):
    total = None
    for ext, weight, b, flipped in terms:
        for a in (-1, 0, 1):
            tap = ext[start + (1 + a) * width : start + (1 + a) * width + size, :]
            kernel = weight[1 - a, 1 - b] if flipped else weight[1 + a, 1 + b]
            part = lax.dot_general(tap, kernel, NT if flipped else NN, preferred_element_type=jnp.float32)
            total = part if total is None else total + part
    return total


def flat_rows(channels, pieces):
    if channels % LANES * 2 != LANES:
        rows = 9 * channels * (-(-channels // LANES))
    else:
        rows = 9 * channels * channels // LANES
    unit = pieces * ROW_TILE
    return -(-rows // unit) * unit


def store_flat(ref, lead, blocks):
    channels = blocks[0].shape[0]
    full = channels // LANES
    row = 0
    for block in blocks:
        for tile in range(full):
            ref[lead, row : row + channels, :] = block[:, tile * LANES : (tile + 1) * LANES]
            row += channels
    width = channels - full * LANES
    if width == 0:
        return
    rests = [block[:, full * LANES :] for block in blocks]
    if width * 2 != LANES:
        for rest in rests:
            ref[lead, row : row + channels, :width] = rest
            row += channels
        return
    for pair in range(0, 8, 2):
        ref[lead, row : row + channels, :] = jnp.concatenate([rests[pair], rests[pair + 1]], axis=1)
        row += channels
    half = channels // 2
    ref[lead, row : row + half, :] = jnp.concatenate([rests[8][:half], rests[8][half:]], axis=1)


def load_flat(ref, lead, channels):
    full = channels // LANES
    row = 0
    parts = []
    for _ in range(9):
        tiles = []
        for _ in range(full):
            tiles.append(ref[lead, row : row + channels, :])
            row += channels
        parts.append(tiles)
    width = channels - full * LANES
    if width == 0:
        pass
    elif width * 2 != LANES:
        for tap in range(9):
            parts[tap].append(ref[lead, row : row + channels, :width])
            row += channels
    else:
        for pair in range(0, 8, 2):
            both = ref[lead, row : row + channels, :]
            parts[pair].append(both[:, :width])
            parts[pair + 1].append(both[:, width:])
            row += channels
        both = ref[lead, row : row + channels // 2, :]
        parts[8].append(jnp.concatenate([both[:, :width], both[:, width:]], axis=0))
    return [jnp.concatenate(p, axis=1) if len(p) > 1 else p[0] for p in parts]


def radices(count):
    found = []
    if count % 2 == 0:
        found.append(2)
        count //= 2
    while count % 4 == 0:
        found.append(4)
        count //= 4
    while count % 2 == 0:
        found.append(2)
        count //= 2
    return found if count == 1 else None


def swapped(value, count, stride, k):
    return lax.ppermute(value, "lon", [(i, i ^ (k * stride)) for i in range(count)])


def moved(value, steps):
    count = lax.axis_size("lon")
    if steps % count == 0:
        return value
    return lax.ppermute(value, "lon", [(i, (i + steps) % count) for i in range(count)])


def lat_rim(field):
    count = lax.axis_size("lat")
    if count == 1:
        return None
    north = lax.ppermute(field[-1], "lat", [(i, i + 1) for i in range(count - 1)])
    south = lax.ppermute(field[0], "lat", [(i + 1, i) for i in range(count - 1)])
    return jnp.stack([north, south])


def paired(spread, width):
    steps, rest = divmod(spread, width)
    return rest == 0 and lax.axis_size("lon") % (2 * steps) == 0


def side_of(spread, width):
    if not paired(spread, width):
        return 0
    return lax.rem(lax.axis_index("lon") // (spread // width), 2)


def inner_pairs(steps):
    return [(i, i + steps if i // steps % 2 == 0 else i - steps) for i in range(lax.axis_size("lon"))]


def outer_pairs(steps):
    count = lax.axis_size("lon")
    return [(i, (i - steps if i // steps % 2 == 0 else i + steps) % count) for i in range(count)]


def beside(field, packed, spread, pack):
    width = field.shape[1]
    steps, rest = divmod(spread, width)
    if paired(spread, width):
        return (
            lax.ppermute(packed, "lon", inner_pairs(steps)),
            lax.ppermute(packed, "lon", outer_pairs(steps)),
        )
    if rest == 0:
        return moved(packed, -steps), moved(packed, steps)
    cut = width - rest
    west = jnp.concatenate([moved(field[:, cut:], steps + 1), moved(field[:, :cut], steps)], axis=1)
    east = jnp.concatenate([moved(field[:, rest:], -steps), moved(field[:, :rest], -steps - 1)], axis=1)
    return pack(east), pack(west)


def shards(inputs, cotangent, first_weight, second_weight):
    height, width, channels = inputs.shape
    rows = height * width
    count = lax.axis_size("lon")
    scale = 1.0 / math.sqrt(rows * lax.axis_size("lat") * count)
    bf16, f32 = jnp.bfloat16, jnp.float32
    pshape = packed_shape(rows, channels)
    ext_rows = rows + 2 * width
    ext = pltpu.VMEM((ext_rows, channels), bf16)
    sides = pltpu.VMEM((3, ext_rows, channels), bf16)
    tap_flops = 2 * rows * channels * channels
    blocks = row_blocks(rows)

    def pack_body(source, target):
        pack_into(target, source[...])

    def pack_one(field):
        return call(pack_body, [shape_of(pshape, bf16)], [field.reshape(rows, channels)], name="pack")[0]

    def rims_of(field, spread):
        rim = lat_rim(field)
        if rim is None:
            return []
        inner, outer = beside(rim, rim, spread, lambda r: r)
        return [r.reshape(2 * width, channels) for r in (rim, inner, outer)]

    def place_sides(scratch, inner_ref, outer_ref, rims, spread):
        side = side_of(spread, width)
        extend(scratch.at[2 - 2 * side], unpacked(inner_ref, rows, channels), rims[0], width)
        extend(scratch.at[2 * side], unpacked(outer_ref, rows, channels), rims[1], width)

    x = inputs.reshape(rows, channels)
    g = cotangent.reshape(rows, channels)
    x_rims = rims_of(inputs, FIRST_SPREAD)
    g_rims = rims_of(cotangent, SECOND_SPREAD)
    rimmed = bool(x_rims)

    x_inner, x_outer = beside(inputs, pack_one(inputs), FIRST_SPREAD, pack_one)
    g_inner, g_outer = beside(cotangent, pack_one(cotangent), SECOND_SPREAD, pack_one)

    def own_body(x_ref, g_ref, w1_ref, w2_ref, *rest):
        rims, (part1, part2, xe, ge) = (rest[:2], rest[2:]) if rimmed else ((None, None), rest)
        extend(xe, x_ref[...], rims[0], width)
        extend(ge, g_ref[...], rims[1], width)
        for start, size in blocks:
            part1[start : start + size, :] = conv_block([(xe, w1_ref, 0, False)], start, size, width)
        for start, size in blocks:
            part2[start : start + size, :] = conv_block([(ge, w2_ref, 0, True)], start, size, width)

    part1, part2 = call(
        own_body,
        [shape_of((rows, channels), f32)] * 2,
        [x, g, first_weight, second_weight] + x_rims[:1] + g_rims[:1],
        [ext, ext],
        flops=6 * tap_flops,
        name="own_columns",
    )

    def hidden_body(part_ref, inner_ref, outer_ref, w_ref, *rest):
        rims, (hidden_t, slope, se, hid) = (rest[:2], rest[2:]) if rimmed else ((None, None), rest)
        place_sides(se, inner_ref, outer_ref, rims, FIRST_SPREAD)
        for start, size in blocks:
            act = part_ref[start : start + size, :] + conv_block(
                [(se.at[0], w_ref, -1, False), (se.at[2], w_ref, 1, False)], start, size, width
            )
            sigma = jax.nn.sigmoid(act)
            slope[start : start + size, :] = sigma * (1.0 + act * (1.0 - sigma))
            hid[start : start + size, :] = (act * sigma).astype(bf16).astype(f32)
        hidden_t[...] = hid[...].T.astype(bf16)

    hidden_t, slope = call(
        hidden_body,
        [shape_of((channels, rows), bf16), shape_of((rows, channels), f32)],
        [part1, x_inner, x_outer, first_weight] + x_rims[1:],
        [sides, pltpu.VMEM((rows, channels), f32)],
        flops=6 * tap_flops,
        name="hidden",
    )

    def grad_body(part_ref, slope_ref, inner_ref, outer_ref, w_ref, *rest):
        rims, (pre_grad, packed, pre_t, se, pre) = (rest[:2], rest[2:]) if rimmed else ((None, None), rest)
        place_sides(se, inner_ref, outer_ref, rims, SECOND_SPREAD)
        for start, size in blocks:
            grad = part_ref[start : start + size, :] + conv_block(
                [(se.at[0], w_ref, -1, True), (se.at[2], w_ref, 1, True)], start, size, width
            )
            value = (grad * slope_ref[start : start + size, :]).astype(bf16)
            pre_grad[start : start + size, :] = value
            pre[start : start + size, :] = value.astype(f32)
        pack_into(packed, pre_grad[...])
        pre_t[...] = pre[...].T.astype(bf16)

    pre_grad, pre_packed, pre_t = call(
        grad_body,
        [shape_of((rows, channels), bf16), shape_of(pshape, bf16), shape_of((channels, rows), bf16)],
        [part2, slope, g_inner, g_outer, second_weight] + g_rims[1:],
        [sides, pltpu.VMEM((rows, channels), f32)],
        flops=6 * tap_flops,
        name="pre_grad",
    )

    stages = radices(count)
    pieces = count // 2
    flat = flat_rows(channels, pieces)
    used = flat_rows(channels, 1)
    index = lax.axis_index("lon")

    def kernel_gradient(which):
        def body(hid_ref, pre_ref, x_ref, xi_ref, xo_ref, g_ref, gi_ref, go_ref, *rest):
            rims, (out, flat_ref, se) = (rest[:6], rest[6:]) if rimmed else ((None,) * 6, rest)

            def window(b, a):
                return se[1 + b, (1 + a) * width : (1 + a) * width + rows, :]

            if used < flat:
                flat_ref[0, used - ROW_TILE :, :] = jnp.zeros((flat - used + ROW_TILE, LANES), f32)
            chosen = which(lax.rem(lax.axis_index("lon"), 2))

            @pl.when(chosen == 0)
            def _():
                place_sides(se, gi_ref, go_ref, rims[4:6], SECOND_SPREAD)
                extend(se.at[1], g_ref[...], rims[3], width)
                store_flat(
                    flat_ref,
                    0,
                    [
                        jnp.dot(hid_ref[...], window(-b, -a), preferred_element_type=f32)
                        for a in (-1, 0, 1)
                        for b in (-1, 0, 1)
                    ],
                )

            @pl.when(chosen == 1)
            def _():
                place_sides(se, xi_ref, xo_ref, rims[1:3], FIRST_SPREAD)
                extend(se.at[1], x_ref[...], rims[0], width)
                store_flat(
                    flat_ref,
                    0,
                    [
                        jnp.dot(pre_ref[...], window(b, a), preferred_element_type=f32)
                        for a in (-1, 0, 1)
                        for b in (-1, 0, 1)
                    ],
                )

            out[...] = flat_ref[0].astype(out.dtype)

        return body

    fields = [hidden_t, pre_t, x, x_inner, x_outer, g, g_inner, g_outer] + x_rims + g_rims
    flat_scratch = pltpu.VMEM((1, flat, LANES), f32)
    (send,) = call(
        kernel_gradient(lambda core: 1 - core),
        [shape_of((flat, LANES), bf16)],
        fields,
        [flat_scratch, sides],
        flops=9 * tap_flops,
        name="sibling_kernel_gradient",
    )
    received = [swapped(send, count, 1, 1)]
    (own,) = call(
        kernel_gradient(lambda core: core),
        [shape_of((flat, LANES), f32)],
        fields,
        [flat_scratch, sides],
        flops=9 * tap_flops,
        name="own_kernel_gradient",
    )

    def digit_of(stride, radix):
        return lax.rem(lax.axis_index("lon") // stride, radix)

    def combine(own, received, stride, radix):
        m = own.shape[0] // radix

        def body(own_ref, *refs):
            got, (mine, *sends) = refs[: len(received)], refs[len(received) :]
            digit = digit_of(stride, radix)
            for k, target in enumerate([mine] + sends):
                at = pl.ds(pl.multiple_of((digit ^ k) * m, m), m)
                value = own_ref[at, :]
                for ref in got:
                    value = value + ref[at, :].astype(f32)
                target[...] = value.astype(target.dtype)

        outs = [shape_of((m, LANES), f32)] + [shape_of((m, LANES), bf16)] * (radix - 1)
        return call(body, outs, [own] + received, name="combine")

    stride = 2
    for radix in stages[1:]:
        own, *sends = combine(own, received, stride, radix)
        received = [swapped(part, count, stride, k + 1) for k, part in enumerate(sends)]
        stride *= radix
    if lax.axis_size("lat") > 1:
        for part in received:
            own = own + part.astype(f32)
        held = lax.psum(own, "lat").astype(bf16)
    else:

        def last_body(own_ref, *refs):
            value = own_ref[...]
            for ref in refs[:-1]:
                value = value + ref[...].astype(f32)
            refs[-1][...] = value.astype(bf16)

        (held,) = call(last_body, [shape_of(own.shape, bf16)], [own] + received, name="combine_last")

    for radix in reversed(stages[2:]):
        stride //= radix
        held = jnp.concatenate([held] + [swapped(held, count, stride, k) for k in range(1, radix)], axis=0)
    group = stages[1]
    quarter = [held] + [swapped(held, count, 2, k) for k in range(1, group)]
    sibling = [swapped(q, count, 1, 1) for q in quarter]

    pre_field = pre_grad.reshape(height, width, channels)
    p_rims = rims_of(pre_field, FIRST_SPREAD)
    p_inner, p_outer = beside(pre_field, pre_packed, FIRST_SPREAD, pack_one)

    def input_body(p_ref, inner_ref, outer_ref, w_ref, *rest):
        rims, (out, se) = (rest[:3], rest[3:]) if rimmed else ((None,) * 3, rest)
        place_sides(se, inner_ref, outer_ref, rims[1:], FIRST_SPREAD)
        extend(se.at[1], p_ref[...], rims[0], width)
        for start, size in blocks:
            grad = conv_block([(se.at[1 + b], w_ref, b, True) for b in (-1, 0, 1)], start, size, width)
            out[start : start + size, :] = grad.astype(bf16)

    (input_gradient,) = call(
        input_body,
        [shape_of((rows, channels), bf16)],
        [pre_grad, p_inner, p_outer, first_weight] + p_rims,
        [sides],
        flops=9 * tap_flops,
        name="input_gradient",
    )

    unit = flat // pieces

    def final_body(*refs):
        quarters, (first_out, second_out, both) = refs[: 2 * group], refs[2 * group :]
        place = lax.axis_index("lon")
        mine = lax.rem(place, 2)
        for side in range(2):
            lead = mine if side == 0 else 1 - mine
            for k in range(group):
                stride, span = 2 * group, pieces // group
                walk = [((digit_of(2, group) ^ k) * span, 0)]
                for radix in stages[2:]:
                    digit = digit_of(stride, radix)
                    span //= radix
                    walk = [
                        (at + (digit ^ j) * span, order + j * span) for at, order in walk for j in range(radix)
                    ]
                    stride *= radix
                for at, order in walk:
                    both[lead, pl.ds(pl.multiple_of(at * unit, unit), unit), :] = quarters[side * group + k][
                        order * unit : (order + 1) * unit, :
                    ].astype(f32)
        second = load_flat(both, 0, channels)
        first = load_flat(both, 1, channels)
        for tap in range(9):
            second_out[tap // 3, tap % 3] = second[tap] * scale
            first_out[tap // 3, tap % 3] = first[tap].T * scale

    first_gradient, second_gradient = call(
        final_body,
        [shape_of((3, 3, channels, channels), f32)] * 2,
        quarter + sibling,
        [pltpu.VMEM((2, flat, LANES), f32)],
        name="unpack_gradients",
    )
    return (input_gradient.reshape(height, width, channels), first_gradient, second_gradient)


def solution(mesh):
    placed = (P("lat", "lon", None), P("lat", "lon", None), P(), P())
    return jax.shard_map(
        shards,
        mesh=mesh,
        in_specs=placed,
        out_specs=(P("lat", "lon", None), P(), P()),
        check_vma=False,
    )
```

```python
import math

import jax
import jax.numpy as jnp
from jax import lax
from jax.experimental import pallas as pl
from jax.experimental.pallas import tpu as pltpu
from jax.sharding import PartitionSpec as P

FIRST_SPREAD = 32
SECOND_SPREAD = 64
LANES = 128
ROW_TILE = 16
P_PARTS = 1
GROUPS = 1
VMEM_LIMIT = 48 * 1024 * 1024


def call(body, outs, args, scratch=(), flops=0, name=None, far_args=(), far_outs=()):
    moved = sum(a.size * a.dtype.itemsize for a in list(args) + list(outs))
    near, far = pl.BlockSpec(memory_space=pltpu.VMEM), pl.BlockSpec(memory_space=pltpu.HBM)
    return pl.pallas_call(
        body,
        out_shape=list(outs),
        in_specs=[far if i in far_args else near for i in range(len(args))],
        out_specs=[far if i in far_outs else near for i in range(len(outs))],
        scratch_shapes=list(scratch),
        compiler_params=pltpu.CompilerParams(vmem_limit_bytes=VMEM_LIMIT),
        cost_estimate=pl.CostEstimate(flops=flops, bytes_accessed=moved, transcendentals=0),
        name=name,
    )(*args)


def shape_of(shape, dtype):
    return jax.ShapeDtypeStruct(shape, dtype)


def packs(rows, channels):
    return channels % LANES * 2 == LANES and rows % (2 * ROW_TILE) == 0


def packed_shape(rows, channels):
    if not packs(rows, channels):
        return (rows, channels)
    full = channels // LANES
    return (rows * full + rows // 2, LANES)


def pack_into(refs, value):
    rows, channels = value.shape
    if packs(rows, channels):
        full = channels // LANES
        rest = value[:, full * LANES :]
        half = rows // 2
        tiles = [value[:, tile * LANES : (tile + 1) * LANES] for tile in range(full)]
        tiles.append(jnp.concatenate([rest[:half], rest[half:]], axis=1))
        value = jnp.concatenate(tiles, axis=0)
    size = value.shape[0] // len(refs)
    for part, ref in enumerate(refs):
        ref[...] = value[part * size : (part + 1) * size]


def unpacked(refs, rows, channels):
    parts = [ref[...] for ref in refs]
    ref = parts[0] if len(parts) == 1 else jnp.concatenate(parts, axis=0)
    if not packs(rows, channels):
        return ref
    full = channels // LANES
    rest = ref[full * rows :, :]
    width = channels - full * LANES
    tail = jnp.concatenate([rest[:, :width], rest[:, width:]], axis=0)
    return jnp.concatenate([ref[t * rows : (t + 1) * rows, :] for t in range(full)] + [tail], axis=1)


def extend(scratch, value, rim, width):
    rows = value.shape[0]
    scratch[width : width + rows, :] = value
    if rim is None:
        blank = jnp.zeros((width, value.shape[1]), value.dtype)
        scratch[:width, :] = blank
        scratch[width + rows :, :] = blank
    else:
        scratch[:width, :] = rim[:width, :]
        scratch[width + rows :, :] = rim[width:, :]


def row_blocks(rows):
    size = rows
    while size > 256 and size % 2 == 0 and size // 2 % ROW_TILE == 0:
        size //= 2
    return [(start, size) for start in range(0, rows, size)]


NT = (((1,), (1,)), ((), ()))
NN = (((1,), (0,)), ((), ()))


def conv_block(terms, start, size, width):
    total = None
    for ext, weight, b, flipped in terms:
        for a in (-1, 0, 1):
            tap = ext[start + (1 + a) * width : start + (1 + a) * width + size, :]
            kernel = weight[1 - a, 1 - b] if flipped else weight[1 + a, 1 + b]
            part = lax.dot_general(tap, kernel, NT if flipped else NN, preferred_element_type=jnp.float32)
            total = part if total is None else total + part
    return total


def flat_rows(channels, pieces):
    if channels % LANES * 2 != LANES:
        rows = 9 * channels * (-(-channels // LANES))
    else:
        rows = 9 * channels * channels // LANES
    unit = pieces * ROW_TILE
    return -(-rows // unit) * unit


def store_flat(ref, lead, blocks):
    channels = blocks[0].shape[0]
    full = channels // LANES
    row = 0
    for block in blocks:
        for tile in range(full):
            ref[lead, row : row + channels, :] = block[:, tile * LANES : (tile + 1) * LANES]
            row += channels
    width = channels - full * LANES
    if width == 0:
        return
    rests = [block[:, full * LANES :] for block in blocks]
    if width * 2 != LANES:
        for rest in rests:
            ref[lead, row : row + channels, :width] = rest
            row += channels
        return
    for pair in range(0, 8, 2):
        ref[lead, row : row + channels, :] = jnp.concatenate([rests[pair], rests[pair + 1]], axis=1)
        row += channels
    half = channels // 2
    ref[lead, row : row + half, :] = jnp.concatenate([rests[8][:half], rests[8][half:]], axis=1)


def load_flat(ref, lead, channels):
    full = channels // LANES
    row = 0
    parts = []
    for _ in range(9):
        tiles = []
        for _ in range(full):
            tiles.append(ref[lead, row : row + channels, :])
            row += channels
        parts.append(tiles)
    width = channels - full * LANES
    if width == 0:
        pass
    elif width * 2 != LANES:
        for tap in range(9):
            parts[tap].append(ref[lead, row : row + channels, :width])
            row += channels
    else:
        for pair in range(0, 8, 2):
            both = ref[lead, row : row + channels, :]
            parts[pair].append(both[:, :width])
            parts[pair + 1].append(both[:, width:])
            row += channels
        both = ref[lead, row : row + channels // 2, :]
        parts[8].append(jnp.concatenate([both[:, :width], both[:, width:]], axis=0))
    return [jnp.concatenate(p, axis=1) if len(p) > 1 else p[0] for p in parts]


def radices(count):
    found = []
    if count % 2 == 0:
        found.append(2)
        count //= 2
    while count % 4 == 0:
        found.append(4)
        count //= 4
    while count % 2 == 0:
        found.append(2)
        count //= 2
    return found if count == 1 else None


def swapped(value, count, stride, k):
    return lax.ppermute(value, "lon", [(i, i ^ (k * stride)) for i in range(count)])


def moved(value, steps):
    count = lax.axis_size("lon")
    if steps % count == 0:
        return value
    return lax.ppermute(value, "lon", [(i, (i + steps) % count) for i in range(count)])


def lat_rim(field):
    count = lax.axis_size("lat")
    if count == 1:
        return None
    north = lax.ppermute(field[-1], "lat", [(i, i + 1) for i in range(count - 1)])
    south = lax.ppermute(field[0], "lat", [(i + 1, i) for i in range(count - 1)])
    return jnp.stack([north, south])


def paired(spread, width):
    steps, rest = divmod(spread, width)
    return rest == 0 and lax.axis_size("lon") % (2 * steps) == 0


def side_of(spread, width):
    if not paired(spread, width):
        return 0
    return lax.rem(lax.axis_index("lon") // (spread // width), 2)


def inner_pairs(steps):
    return [(i, i + steps if i // steps % 2 == 0 else i - steps) for i in range(lax.axis_size("lon"))]


def outer_pairs(steps):
    count = lax.axis_size("lon")
    return [(i, (i - steps if i // steps % 2 == 0 else i + steps) % count) for i in range(count)]


def after(value, *others):
    return lax.optimization_barrier((value, *others))[0]


def beside(field, packed, spread, pack):
    width = field.shape[1]
    steps, rest = divmod(spread, width)
    if paired(spread, width):
        return (
            [lax.ppermute(packed, "lon", inner_pairs(steps))],
            [lax.ppermute(packed, "lon", outer_pairs(steps))],
        )
    if rest == 0:
        return [moved(packed, -steps)], [moved(packed, steps)]
    cut = width - rest
    west = jnp.concatenate([moved(field[:, cut:], steps + 1), moved(field[:, :cut], steps)], axis=1)
    east = jnp.concatenate([moved(field[:, rest:], -steps), moved(field[:, :rest], -steps - 1)], axis=1)
    return [pack(east)], [pack(west)]


def onward_pairs(steps):
    count = lax.axis_size("lon")
    return [(i, (i + 2 * steps if i // steps % 2 == 0 else i - 2 * steps) % count) for i in range(count)]


def shards(inputs, cotangent, first_weight, second_weight):
    height, width, channels = inputs.shape
    rows = height * width
    count = lax.axis_size("lon")
    scale = 1.0 / math.sqrt(rows * lax.axis_size("lat") * count)
    bf16, f32 = jnp.bfloat16, jnp.float32
    pshape = packed_shape(rows, channels)
    ext_rows = rows + 2 * width
    ext = pltpu.VMEM((ext_rows, channels), bf16)
    sides = pltpu.VMEM((3, ext_rows, channels), bf16)
    tap_flops = 2 * rows * channels * channels
    blocks = row_blocks(rows)

    def pack_body(source, *targets):
        pack_into(targets, source[...])

    def pack_one(field, parts=1):
        shape = (pshape[0] // parts, pshape[1])
        packed = call(
            pack_body, [shape_of(shape, bf16)] * parts, [field.reshape(rows, channels)], name="pack"
        )
        return packed if parts > 1 else packed[0]

    def rims_of(field, spread):
        rim = lat_rim(field)
        if rim is None:
            return []
        inner, outer = beside(rim, rim, spread, lambda r: r)
        return [r.reshape(2 * width, channels) for r in (rim, *inner, *outer)]

    def place_sides(scratch, refs, rims, spread):
        side = side_of(spread, width)
        half = len(refs) // 2
        extend(scratch.at[2 - 2 * side], unpacked(refs[:half], rows, channels), rims[0], width)
        extend(scratch.at[2 * side], unpacked(refs[half:], rows, channels), rims[1], width)

    def near_part(field, weight, inner, rims, spread, flipped, name):
        def body(x_ref, w_ref, *rest):
            refs, rest = rest[: len(inner)], rest[len(inner) :]
            (own_rim, inner_rim), (part, e0, e1) = (rest[:2], rest[2:]) if rimmed else ((None, None), rest)
            extend(e0, x_ref[...], own_rim, width)
            extend(e1, unpacked(refs, rows, channels), inner_rim, width)
            b = 1 - 2 * side_of(spread, width)
            for start, size in blocks:
                part[start : start + size, :] = conv_block(
                    [(e0, w_ref, 0, flipped), (e1, w_ref, b, flipped)], start, size, width
                )

        args = [field, weight] + inner + rims[:2]
        return call(body, [shape_of((rows, channels), f32)], args, [ext, ext], 6 * tap_flops, name)[0]

    def far_part(part_ref, scratch, w_ref, spread, flipped, start, size):
        b = 2 * side_of(spread, width) - 1
        return part_ref[start : start + size, :] + conv_block([(scratch, w_ref, b, flipped)], start, size, width)

    x = inputs.reshape(rows, channels)
    g = cotangent.reshape(rows, channels)
    x_rims = rims_of(inputs, FIRST_SPREAD)
    g_rims = rims_of(cotangent, SECOND_SPREAD)
    rimmed = bool(x_rims)

    if paired(SECOND_SPREAD, width):
        steps = SECOND_SPREAD // width
        g_packed = pack_one(cotangent, 2)
        g_inner = [lax.ppermute(part, "lon", inner_pairs(steps)) for part in g_packed]
        g_outer = [
            lax.ppermute(g_inner[0], "lon", onward_pairs(steps)),
            lax.ppermute(g_packed[1], "lon", outer_pairs(steps)),
        ]
    else:
        g_inner, g_outer = beside(cotangent, pack_one(cotangent), SECOND_SPREAD, pack_one)
    if paired(FIRST_SPREAD, width):
        steps = FIRST_SPREAD // width
        x_packed = pack_one(after(inputs, *g_packed), 2)
        x_inner = [lax.ppermute(part, "lon", inner_pairs(steps)) for part in x_packed]
        x_outer = [lax.ppermute(part, "lon", outer_pairs(steps)) for part in x_packed]
    else:
        x_inner, x_outer = beside(inputs, pack_one(inputs), FIRST_SPREAD, pack_one)
    part1 = near_part(x, first_weight, x_inner, x_rims, FIRST_SPREAD, False, "near_pre_act")
    part2 = near_part(g, second_weight, g_inner, g_rims, SECOND_SPREAD, True, "near_hidden_grad")
    x_sides, g_sides = x_inner + x_outer, g_inner + g_outer
    nx, ng = len(x_sides), len(g_sides)

    def hidden_body(part_ref, w_ref, *rest):
        side_refs, rest = rest[: len(x_outer)], rest[len(x_outer) :]
        (rim,), (hidden_t, slope, se, hid) = (rest[:1], rest[1:]) if rimmed else ((None,), rest)
        extend(se, unpacked(side_refs, rows, channels), rim, width)
        for start, size in blocks:
            act = far_part(part_ref, se, w_ref, FIRST_SPREAD, False, start, size)
            sigma = jax.nn.sigmoid(act)
            slope[start : start + size, :] = sigma * (1.0 + act * (1.0 - sigma))
            hid[start : start + size, :] = (act * sigma).astype(bf16).astype(f32)
        hidden_t[...] = hid[...].T.astype(bf16)

    hidden_t, slope = call(
        hidden_body,
        [shape_of((channels, rows), bf16), shape_of((rows, channels), f32)],
        [part1, first_weight] + x_outer + x_rims[2:],
        [ext, pltpu.VMEM((rows, channels), f32)],
        flops=3 * tap_flops,
        name="hidden",
    )

    def grad_body(part_ref, slope_ref, w_ref, *rest):
        side_refs, rest = rest[: len(g_outer)], rest[len(g_outer) :]
        (rim,), (pre_grad, packed, pre_t, se, pre) = (rest[:1], rest[1:]) if rimmed else ((None,), rest)
        extend(se, unpacked(side_refs, rows, channels), rim, width)
        for start, size in blocks:
            grad = far_part(part_ref, se, w_ref, SECOND_SPREAD, True, start, size)
            value = (grad * slope_ref[start : start + size, :]).astype(bf16)
            pre_grad[start : start + size, :] = value
            pre[start : start + size, :] = value.astype(f32)
        pack_into([packed], pre_grad[...])
        pre_t[...] = pre[...].T.astype(bf16)

    pre_grad, pre_packed, pre_t = call(
        grad_body,
        [shape_of((rows, channels), bf16), shape_of(pshape, bf16), shape_of((channels, rows), bf16)],
        [part2, slope, second_weight] + g_outer + g_rims[2:],
        [ext, pltpu.VMEM((rows, channels), f32)],
        flops=3 * tap_flops,
        name="pre_grad",
    )

    stages = radices(count)
    pieces = count // 2
    flat = flat_rows(channels, pieces)
    used = flat_rows(channels, 1)

    def kernel_gradient(which):
        def body(hid_ref, pre_ref, x_ref, g_ref, *rest):
            x_refs, g_refs, rest = rest[:nx], rest[nx : nx + ng], rest[nx + ng :]
            rims, (out, flat_ref, se) = (rest[:6], rest[6:]) if rimmed else ((None,) * 6, rest)

            def window(b, a):
                return se[1 + b, (1 + a) * width : (1 + a) * width + rows, :]

            if used < flat:
                flat_ref[0, used - ROW_TILE :, :] = jnp.zeros((flat - used + ROW_TILE, LANES), f32)
            chosen = which(lax.rem(lax.axis_index("lon"), 2))

            @pl.when(chosen == 0)
            def _():
                place_sides(se, g_refs, rims[4:6], SECOND_SPREAD)
                extend(se.at[1], g_ref[...], rims[3], width)
                store_flat(
                    flat_ref,
                    0,
                    [
                        jnp.dot(hid_ref[...], window(-b, -a), preferred_element_type=f32)
                        for a in (-1, 0, 1)
                        for b in (-1, 0, 1)
                    ],
                )

            @pl.when(chosen == 1)
            def _():
                place_sides(se, x_refs, rims[1:3], FIRST_SPREAD)
                extend(se.at[1], x_ref[...], rims[0], width)
                store_flat(
                    flat_ref,
                    0,
                    [
                        jnp.dot(pre_ref[...], window(b, a), preferred_element_type=f32)
                        for a in (-1, 0, 1)
                        for b in (-1, 0, 1)
                    ],
                )

            out[...] = flat_ref[0].astype(out.dtype)

        return body

    fields = [hidden_t, pre_t, x, g] + x_sides + g_sides + x_rims + g_rims
    flat_scratch = pltpu.VMEM((1, flat, LANES), f32)
    (send,) = call(
        kernel_gradient(lambda core: 1 - core),
        [shape_of((flat, LANES), bf16)],
        fields,
        [flat_scratch, sides],
        flops=9 * tap_flops,
        name="sibling_kernel_gradient",
    )
    received = [swapped(send, count, 1, 1)]
    (own,) = call(
        kernel_gradient(lambda core: core),
        [shape_of((flat, LANES), f32)],
        fields,
        [flat_scratch, sides],
        flops=9 * tap_flops,
        name="own_kernel_gradient",
    )

    def digit_of(stride, radix):
        return lax.rem(lax.axis_index("lon") // stride, radix)

    def combine(own, received, stride, radix, begin, size):
        m = size // radix

        def body(own_ref, *refs):
            got, (mine, *sends) = refs[: len(received)], refs[len(received) :]
            digit = digit_of(stride, radix)
            for k, target in enumerate([mine] + sends):
                at = pl.ds(pl.multiple_of(begin + (digit ^ k) * m, ROW_TILE), m)
                value = own_ref[at, :]
                for ref in got:
                    value = value + ref[at, :].astype(f32)
                target[...] = value.astype(target.dtype)

        outs = [shape_of((m, LANES), f32)] + [shape_of((m, LANES), bf16)] * (radix - 1)
        return call(body, outs, [own] + received, name="combine")

    unit = flat // pieces
    unit_rows = [unit]
    if GROUPS == 2 and unit > ROW_TILE:
        first_rows = -(-unit // (2 * ROW_TILE)) * ROW_TILE
        unit_rows = [first_rows, unit - first_rows]
    begins = [pieces * sum(unit_rows[:i]) for i in range(len(unit_rows))]
    groups = [(own, received, begin, pieces * rows_) for begin, rows_ in zip(begins, unit_rows)]
    stride = 2
    first_got = None
    for radix in stages[1:]:
        following = []
        for own, received, begin, size in groups:
            own, *sends = combine(own, received, stride, radix, begin, size)
            received = [swapped(part, count, stride, k + 1) for k, part in enumerate(sends)]
            following.append((own, received, 0, size // radix))
            first_got = received[0] if first_got is None else first_got
        groups = following
        stride *= radix
    pre_field = pre_grad.reshape(height, width, channels)
    p_rims = rims_of(pre_field, FIRST_SPREAD)
    if paired(FIRST_SPREAD, width):
        steps = FIRST_SPREAD // width
        p_inner = [lax.ppermute(pre_packed, "lon", inner_pairs(steps))]
        size = pshape[0] // P_PARTS
        pre_packed = after(pre_packed, first_got)
        p_outer = [
            lax.ppermute(pre_packed[i * size : (i + 1) * size], "lon", outer_pairs(steps)) for i in range(P_PARTS)
        ]
    else:
        p_inner, p_outer = beside(pre_field, pre_packed, FIRST_SPREAD, pack_one)
    part3 = near_part(pre_grad, first_weight, p_inner, p_rims, FIRST_SPREAD, True, "near_input_gradient")

    def input_body(part_ref, w_ref, *rest):
        side_refs, rest = rest[: len(p_outer)], rest[len(p_outer) :]
        (rim,), (out, se) = (rest[:1], rest[1:]) if rimmed else ((None,), rest)
        extend(se, unpacked(side_refs, rows, channels), rim, width)
        for start, size in blocks:
            out[start : start + size, :] = far_part(part_ref, se, w_ref, FIRST_SPREAD, True, start, size).astype(bf16)

    (input_gradient,) = call(
        input_body,
        [shape_of((rows, channels), bf16)],
        [part3, first_weight] + p_outer + p_rims[2:],
        [ext],
        flops=3 * tap_flops,
        name="input_gradient",
    )

    def finish(own, received):
        if lax.axis_size("lat") > 1:
            for part in received:
                own = own + part.astype(f32)
            return lax.psum(own, "lat").astype(bf16)

        def body(own_ref, *refs):
            value = own_ref[...]
            for ref in refs[:-1]:
                value = value + ref[...].astype(f32)
            refs[-1][...] = value.astype(bf16)

        return call(body, [shape_of(own.shape, bf16)], [own] + received, name="combine_last")[0]

    group = stages[1]
    arrived = []
    for own, received, _, _ in groups:
        held = finish(own, received)
        stride = count
        for radix in reversed(stages[2:]):
            stride //= radix
            held = jnp.concatenate([held] + [swapped(held, count, stride, k) for k in range(1, radix)], axis=0)
        quarter = [held] + [swapped(held, count, 2, k) for k in range(1, group)]
        sibling = [swapped(held, count, 1, 1)]
        sibling += [swapped(after(q, input_gradient), count, 1, 1) for q in quarter[1:]]
        arrived += quarter + sibling

    def final_body(*refs):
        (first_out, second_out, both, stage, sems) = refs[len(arrived) :]
        place = lax.axis_index("lon")
        mine = lax.rem(place, 2)
        for i, ref in enumerate(refs[: len(arrived)]):
            which, side, k = i // (2 * group), i // group % 2, i % group
            lead = mine if side == 0 else 1 - mine
            m = unit_rows[which]
            stride, span = 2 * group, pieces // group
            walk = [((digit_of(2, group) ^ k) * span, 0)]
            for radix in stages[2:]:
                digit = digit_of(stride, radix)
                span //= radix
                walk = [(at + (digit ^ j) * span, order + j * span) for at, order in walk for j in range(radix)]
                stride *= radix
            for at, order in walk:
                target = pl.ds(pl.multiple_of(begins[which] + at * m, ROW_TILE), m)
                both[lead, target, :] = ref[order * m : (order + 1) * m, :].astype(f32)
        copies = []
        for which, out in enumerate((second_out, first_out)):
            for tap, value in enumerate(load_flat(both, which, channels)):
                stage[which, tap] = (value.T if which else value) * scale
                copies.append(
                    pltpu.make_async_copy(
                        stage.at[which, tap], out.at[tap // 3, tap % 3], sems.at[9 * which + tap]
                    )
                )
                copies[-1].start()
        for copy in copies:
            copy.wait()

    first_gradient, second_gradient = call(
        final_body,
        [shape_of((3, 3, channels, channels), f32)] * 2,
        arrived,
        [
            pltpu.VMEM((2, flat, LANES), f32),
            pltpu.VMEM((2, 9, channels, channels), f32),
            pltpu.SemaphoreType.DMA((18,)),
        ],
        name="unpack_gradients",
        far_outs=(0, 1),
    )
    return (input_gradient.reshape(height, width, channels), first_gradient, second_gradient)


def solution(mesh):
    placed = (P("lat", "lon", None), P("lat", "lon", None), P(), P())
    return jax.shard_map(
        shards,
        mesh=mesh,
        in_specs=placed,
        out_specs=(P("lat", "lon", None), P(), P()),
        check_vma=False,
    )
```

```python
import math

import jax
import jax.numpy as jnp
from jax import lax
from jax.experimental import pallas as pl
from jax.experimental.pallas import tpu as pltpu
from jax.sharding import PartitionSpec as P

FIRST_SPREAD = 32
SECOND_SPREAD = 64
LANES = 128
ROW_TILE = 16
G_SHARE = 13 / 24
X_SHARE = 5 / 12
VMEM_LIMIT = 48 * 1024 * 1024


def call(body, outs, args, scratch=(), flops=0, name=None, far_args=(), far_outs=(), aliases={}):
    moved = sum(a.size * a.dtype.itemsize for a in list(args) + list(outs))
    near, far = pl.BlockSpec(memory_space=pltpu.VMEM), pl.BlockSpec(memory_space=pltpu.HBM)
    return pl.pallas_call(
        body,
        out_shape=list(outs),
        in_specs=[far if i in far_args else near for i in range(len(args))],
        out_specs=[far if i in far_outs else near for i in range(len(outs))],
        scratch_shapes=list(scratch),
        input_output_aliases=aliases,
        compiler_params=pltpu.CompilerParams(vmem_limit_bytes=VMEM_LIMIT),
        cost_estimate=pl.CostEstimate(flops=flops, bytes_accessed=moved, transcendentals=0),
        name=name,
    )(*args)


def shape_of(shape, dtype):
    return jax.ShapeDtypeStruct(shape, dtype)


def packs(rows, channels):
    return channels % LANES * 2 == LANES and rows % (2 * ROW_TILE) == 0


def packed_shape(rows, channels):
    if not packs(rows, channels):
        return (rows, channels)
    full = channels // LANES
    return (rows * full + rows // 2, LANES)


def pack_into(refs, value):
    rows, channels = value.shape
    if packs(rows, channels):
        full = channels // LANES
        rest = value[:, full * LANES :]
        half = rows // 2
        tiles = [value[:, tile * LANES : (tile + 1) * LANES] for tile in range(full)]
        tiles.append(jnp.concatenate([rest[:half], rest[half:]], axis=1))
        value = jnp.concatenate(tiles, axis=0)
    begin = 0
    for ref in refs:
        ref[...] = value[begin : begin + ref.shape[0]]
        begin += ref.shape[0]


def unpacked(refs, rows, channels):
    parts = [ref[...] for ref in refs]
    ref = parts[0] if len(parts) == 1 else jnp.concatenate(parts, axis=0)
    if not packs(rows, channels):
        return ref
    full = channels // LANES
    rest = ref[full * rows :, :]
    width = channels - full * LANES
    tail = jnp.concatenate([rest[:, :width], rest[:, width:]], axis=0)
    return jnp.concatenate([ref[t * rows : (t + 1) * rows, :] for t in range(full)] + [tail], axis=1)


def extend(scratch, value, rim, width):
    rows = value.shape[0]
    scratch[width : width + rows, :] = value
    if rim is None:
        blank = jnp.zeros((width, value.shape[1]), value.dtype)
        scratch[:width, :] = blank
        scratch[width + rows :, :] = blank
    else:
        scratch[:width, :] = rim[:width, :]
        scratch[width + rows :, :] = rim[width:, :]


def row_blocks(rows):
    size = rows
    while size > 256 and size % 2 == 0 and size // 2 % ROW_TILE == 0:
        size //= 2
    return [(start, size) for start in range(0, rows, size)]


NT = (((1,), (1,)), ((), ()))
NN = (((1,), (0,)), ((), ()))


def conv_block(terms, start, size, width):
    total = None
    for ext, weight, b, flipped in terms:
        for a in (-1, 0, 1):
            tap = ext[start + (1 + a) * width : start + (1 + a) * width + size, :]
            kernel = weight[1 - a, 1 - b] if flipped else weight[1 + a, 1 + b]
            part = lax.dot_general(tap, kernel, NT if flipped else NN, preferred_element_type=jnp.float32)
            total = part if total is None else total + part
    return total


def flat_rows(channels, pieces):
    if channels % LANES * 2 != LANES:
        rows = 9 * channels * (-(-channels // LANES))
    else:
        rows = 9 * channels * channels // LANES
    unit = pieces * ROW_TILE
    return -(-rows // unit) * unit


def store_flat(ref, lead, blocks):
    channels = blocks[0].shape[0]
    full = channels // LANES
    row = 0
    for block in blocks:
        for tile in range(full):
            ref[lead, row : row + channels, :] = block[:, tile * LANES : (tile + 1) * LANES]
            row += channels
    width = channels - full * LANES
    if width == 0:
        return
    rests = [block[:, full * LANES :] for block in blocks]
    if width * 2 != LANES:
        for rest in rests:
            ref[lead, row : row + channels, :width] = rest
            row += channels
        return
    for pair in range(0, 8, 2):
        ref[lead, row : row + channels, :] = jnp.concatenate([rests[pair], rests[pair + 1]], axis=1)
        row += channels
    half = channels // 2
    ref[lead, row : row + half, :] = jnp.concatenate([rests[8][:half], rests[8][half:]], axis=1)


def load_flat(ref, lead, channels):
    full = channels // LANES
    row = 0
    parts = []
    for _ in range(9):
        tiles = []
        for _ in range(full):
            tiles.append(ref[lead, row : row + channels, :])
            row += channels
        parts.append(tiles)
    width = channels - full * LANES
    if width == 0:
        pass
    elif width * 2 != LANES:
        for tap in range(9):
            parts[tap].append(ref[lead, row : row + channels, :width])
            row += channels
    else:
        for pair in range(0, 8, 2):
            both = ref[lead, row : row + channels, :]
            parts[pair].append(both[:, :width])
            parts[pair + 1].append(both[:, width:])
            row += channels
        both = ref[lead, row : row + channels // 2, :]
        parts[8].append(jnp.concatenate([both[:, :width], both[:, width:]], axis=0))
    return [jnp.concatenate(p, axis=1) if len(p) > 1 else p[0] for p in parts]


def radices(count):
    found = []
    if count % 2 == 0:
        found.append(2)
        count //= 2
    while count % 4 == 0:
        found.append(4)
        count //= 4
    while count % 2 == 0:
        found.append(2)
        count //= 2
    return found if count == 1 else None


def swapped(value, count, stride, k):
    return lax.ppermute(value, "lon", [(i, i ^ (k * stride)) for i in range(count)])


def moved(value, steps):
    count = lax.axis_size("lon")
    if steps % count == 0:
        return value
    return lax.ppermute(value, "lon", [(i, (i + steps) % count) for i in range(count)])


def lat_rim(field):
    count = lax.axis_size("lat")
    if count == 1:
        return None
    north = lax.ppermute(field[-1], "lat", [(i, i + 1) for i in range(count - 1)])
    south = lax.ppermute(field[0], "lat", [(i + 1, i) for i in range(count - 1)])
    return jnp.stack([north, south])


def paired(spread, width):
    steps, rest = divmod(spread, width)
    return rest == 0 and lax.axis_size("lon") % (2 * steps) == 0


def side_of(spread, width):
    if not paired(spread, width):
        return 0
    return lax.rem(lax.axis_index("lon") // (spread // width), 2)


def inner_pairs(steps):
    return [(i, i + steps if i // steps % 2 == 0 else i - steps) for i in range(lax.axis_size("lon"))]


def outer_pairs(steps):
    count = lax.axis_size("lon")
    return [(i, (i - steps if i // steps % 2 == 0 else i + steps) % count) for i in range(count)]


def after(value, *others):
    return lax.optimization_barrier((value, *others))[0]


def beside(field, packed, spread, pack):
    width = field.shape[1]
    steps, rest = divmod(spread, width)
    if paired(spread, width):
        return (
            [lax.ppermute(packed, "lon", inner_pairs(steps))],
            [lax.ppermute(packed, "lon", outer_pairs(steps))],
        )
    if rest == 0:
        return [moved(packed, -steps)], [moved(packed, steps)]
    cut = width - rest
    west = jnp.concatenate([moved(field[:, cut:], steps + 1), moved(field[:, :cut], steps)], axis=1)
    east = jnp.concatenate([moved(field[:, rest:], -steps), moved(field[:, :rest], -steps - 1)], axis=1)
    return [pack(east)], [pack(west)]


def onward_pairs(steps):
    count = lax.axis_size("lon")
    return [(i, (i + 2 * steps if i // steps % 2 == 0 else i - 2 * steps) % count) for i in range(count)]


def shards(inputs, cotangent, first_weight, second_weight):
    height, width, channels = inputs.shape
    rows = height * width
    count = lax.axis_size("lon")
    scale = 1.0 / math.sqrt(rows * lax.axis_size("lat") * count)
    bf16, f32 = jnp.bfloat16, jnp.float32
    pshape = packed_shape(rows, channels)
    ext_rows = rows + 2 * width
    ext = pltpu.VMEM((ext_rows, channels), bf16)
    sides = pltpu.VMEM((3, ext_rows, channels), bf16)
    tap_flops = 2 * rows * channels * channels
    blocks = row_blocks(rows)

    def pack_body(source, *targets):
        pack_into(targets, source[...])

    def pack_one(field, share=None):
        sizes = [pshape[0]]
        if share is not None:
            first = max(int(pshape[0] * share) // ROW_TILE, 1) * ROW_TILE
            sizes = [first, pshape[0] - first]
        shapes = [shape_of((size, pshape[1]), bf16) for size in sizes]
        packed = call(pack_body, shapes, [field.reshape(rows, channels)], name="pack")
        return packed[0] if share is None else packed

    def rims_of(field, spread):
        rim = lat_rim(field)
        if rim is None:
            return []
        inner, outer = beside(rim, rim, spread, lambda r: r)
        return [r.reshape(2 * width, channels) for r in (rim, *inner, *outer)]

    def place_sides(scratch, refs, rims, spread):
        side = side_of(spread, width)
        half = len(refs) // 2
        extend(scratch.at[2 - 2 * side], unpacked(refs[:half], rows, channels), rims[0], width)
        extend(scratch.at[2 * side], unpacked(refs[half:], rows, channels), rims[1], width)

    def near_part(field, weight, inner, rims, spread, flipped, name):
        def body(x_ref, w_ref, *rest):
            refs, rest = rest[: len(inner)], rest[len(inner) :]
            (own_rim, inner_rim), (part, e0, e1) = (rest[:2], rest[2:]) if rimmed else ((None, None), rest)
            extend(e0, x_ref[...], own_rim, width)
            extend(e1, unpacked(refs, rows, channels), inner_rim, width)
            b = 1 - 2 * side_of(spread, width)
            for start, size in blocks:
                part[start : start + size, :] = conv_block(
                    [(e0, w_ref, 0, flipped), (e1, w_ref, b, flipped)], start, size, width
                )

        args = [field, weight] + inner + rims[:2]
        return call(body, [shape_of((rows, channels), f32)], args, [ext, ext], 6 * tap_flops, name)[0]

    def far_part(part_ref, scratch, w_ref, spread, flipped, start, size):
        b = 2 * side_of(spread, width) - 1
        return part_ref[start : start + size, :] + conv_block([(scratch, w_ref, b, flipped)], start, size, width)

    x = inputs.reshape(rows, channels)
    g = cotangent.reshape(rows, channels)
    x_rims = rims_of(inputs, FIRST_SPREAD)
    g_rims = rims_of(cotangent, SECOND_SPREAD)
    rimmed = bool(x_rims)

    if paired(SECOND_SPREAD, width):
        steps = SECOND_SPREAD // width
        g_packed = pack_one(cotangent, G_SHARE)
        g_inner = [lax.ppermute(part, "lon", inner_pairs(steps)) for part in g_packed]
        g_outer = [
            lax.ppermute(g_inner[0], "lon", onward_pairs(steps)),
            lax.ppermute(g_packed[1], "lon", outer_pairs(steps)),
        ]
    else:
        g_inner, g_outer = beside(cotangent, pack_one(cotangent), SECOND_SPREAD, pack_one)
    if paired(FIRST_SPREAD, width):
        steps = FIRST_SPREAD // width
        x_packed = pack_one(after(inputs, *g_packed), X_SHARE)
        x_inner = [lax.ppermute(part, "lon", inner_pairs(steps)) for part in x_packed]
        x_outer = [lax.ppermute(part, "lon", outer_pairs(steps)) for part in x_packed]
    else:
        x_inner, x_outer = beside(inputs, pack_one(inputs), FIRST_SPREAD, pack_one)
    part1 = near_part(x, first_weight, x_inner, x_rims, FIRST_SPREAD, False, "near_pre_act")
    part2 = near_part(g, second_weight, g_inner, g_rims, SECOND_SPREAD, True, "near_hidden_grad")
    x_sides, g_sides = x_inner + x_outer, g_inner + g_outer
    nx, ng = len(x_sides), len(g_sides)

    def hidden_body(part_ref, w_ref, *rest):
        side_refs, rest = rest[: len(x_outer)], rest[len(x_outer) :]
        (rim,), (hidden_t, slope, se, hid) = (rest[:1], rest[1:]) if rimmed else ((None,), rest)
        extend(se, unpacked(side_refs, rows, channels), rim, width)
        for start, size in blocks:
            act = far_part(part_ref, se, w_ref, FIRST_SPREAD, False, start, size)
            sigma = jax.nn.sigmoid(act)
            slope[start : start + size, :] = sigma * (1.0 + act * (1.0 - sigma))
            hid[start : start + size, :] = (act * sigma).astype(bf16).astype(f32)
        hidden_t[...] = hid[...].T.astype(bf16)

    hidden_t, slope = call(
        hidden_body,
        [shape_of((channels, rows), bf16), shape_of((rows, channels), f32)],
        [part1, first_weight] + x_outer + x_rims[2:],
        [ext, pltpu.VMEM((rows, channels), f32)],
        flops=3 * tap_flops,
        name="hidden",
    )

    def grad_body(part_ref, slope_ref, w_ref, *rest):
        side_refs, rest = rest[: len(g_outer)], rest[len(g_outer) :]
        (rim,), (pre_grad, packed, pre_t, se, pre) = (rest[:1], rest[1:]) if rimmed else ((None,), rest)
        extend(se, unpacked(side_refs, rows, channels), rim, width)
        for start, size in blocks:
            grad = far_part(part_ref, se, w_ref, SECOND_SPREAD, True, start, size)
            value = (grad * slope_ref[start : start + size, :]).astype(bf16)
            pre_grad[start : start + size, :] = value
            pre[start : start + size, :] = value.astype(f32)
        pack_into([packed], pre_grad[...])
        pre_t[...] = pre[...].T.astype(bf16)

    pre_grad, pre_packed, pre_t = call(
        grad_body,
        [shape_of((rows, channels), bf16), shape_of(pshape, bf16), shape_of((channels, rows), bf16)],
        [part2, slope, second_weight] + g_outer + g_rims[2:],
        [ext, pltpu.VMEM((rows, channels), f32)],
        flops=3 * tap_flops,
        name="pre_grad",
    )

    stages = radices(count)
    pieces = count // 2
    flat = flat_rows(channels, pieces)
    used = flat_rows(channels, 1)

    def kernel_gradient(which):
        def body(hid_ref, pre_ref, x_ref, g_ref, *rest):
            x_refs, g_refs, rest = rest[:nx], rest[nx : nx + ng], rest[nx + ng :]
            rims, (out, flat_ref, se) = (rest[:6], rest[6:]) if rimmed else ((None,) * 6, rest)

            def window(b, a):
                return se[1 + b, (1 + a) * width : (1 + a) * width + rows, :]

            if used < flat:
                flat_ref[0, used - ROW_TILE :, :] = jnp.zeros((flat - used + ROW_TILE, LANES), f32)
            chosen = which(lax.rem(lax.axis_index("lon"), 2))

            @pl.when(chosen == 0)
            def _():
                place_sides(se, g_refs, rims[4:6], SECOND_SPREAD)
                extend(se.at[1], g_ref[...], rims[3], width)
                store_flat(
                    flat_ref,
                    0,
                    [
                        jnp.dot(hid_ref[...], window(-b, -a), preferred_element_type=f32)
                        for a in (-1, 0, 1)
                        for b in (-1, 0, 1)
                    ],
                )

            @pl.when(chosen == 1)
            def _():
                place_sides(se, x_refs, rims[1:3], FIRST_SPREAD)
                extend(se.at[1], x_ref[...], rims[0], width)
                store_flat(
                    flat_ref,
                    0,
                    [
                        jnp.dot(pre_ref[...], window(b, a), preferred_element_type=f32)
                        for a in (-1, 0, 1)
                        for b in (-1, 0, 1)
                    ],
                )

            out[...] = flat_ref[0].astype(out.dtype)

        return body

    fields = [hidden_t, pre_t, x, g] + x_sides + g_sides + x_rims + g_rims
    flat_scratch = pltpu.VMEM((1, flat, LANES), f32)
    (send,) = call(
        kernel_gradient(lambda core: 1 - core),
        [shape_of((flat, LANES), bf16)],
        fields,
        [flat_scratch, sides],
        flops=9 * tap_flops,
        name="sibling_kernel_gradient",
    )
    received = [swapped(send, count, 1, 1)]
    (own,) = call(
        kernel_gradient(lambda core: core),
        [shape_of((flat, LANES), f32)],
        fields,
        [flat_scratch, sides],
        flops=9 * tap_flops,
        name="own_kernel_gradient",
    )

    def digit_of(stride, radix):
        return lax.rem(lax.axis_index("lon") // stride, radix)

    def combine(own, received, stride, radix):
        m = own.shape[0] // radix

        def body(own_ref, *refs):
            got, (mine, *sends) = refs[: len(received)], refs[len(received) :]
            digit = digit_of(stride, radix)
            for k, target in enumerate([mine] + sends):
                at = pl.ds(pl.multiple_of((digit ^ k) * m, ROW_TILE), m)
                value = own_ref[at, :]
                for ref in got:
                    value = value + ref[at, :].astype(f32)
                target[...] = value.astype(target.dtype)

        outs = [shape_of((m, LANES), f32)] + [shape_of((m, LANES), bf16)] * (radix - 1)
        return call(body, outs, [own] + received, name="combine")

    stride = 2
    first_got = None
    for radix in stages[1:]:
        own, *sends = combine(own, received, stride, radix)
        received = [swapped(part, count, stride, k + 1) for k, part in enumerate(sends)]
        first_got = received[0] if first_got is None else first_got
        stride *= radix
    pre_field = pre_grad.reshape(height, width, channels)
    p_rims = rims_of(pre_field, FIRST_SPREAD)
    if paired(FIRST_SPREAD, width):
        steps = FIRST_SPREAD // width
        p_inner = [lax.ppermute(pre_packed, "lon", inner_pairs(steps))]
        p_outer = [lax.ppermute(after(pre_packed, first_got), "lon", outer_pairs(steps))]
    else:
        p_inner, p_outer = beside(pre_field, pre_packed, FIRST_SPREAD, pack_one)
    part3 = near_part(pre_grad, first_weight, p_inner, p_rims, FIRST_SPREAD, True, "near_input_gradient")

    def input_body(part_ref, w_ref, *rest):
        side_refs, rest = rest[: len(p_outer)], rest[len(p_outer) :]
        (rim,), (out, se) = (rest[:1], rest[1:]) if rimmed else ((None,), rest)
        extend(se, unpacked(side_refs, rows, channels), rim, width)
        for start, size in blocks:
            out[start : start + size, :] = far_part(part_ref, se, w_ref, FIRST_SPREAD, True, start, size).astype(bf16)

    (input_gradient,) = call(
        input_body,
        [shape_of((rows, channels), bf16)],
        [part3, first_weight] + p_outer + p_rims[2:],
        [ext],
        flops=3 * tap_flops,
        name="input_gradient",
    )

    def finish(own, received):
        if lax.axis_size("lat") > 1:
            for part in received:
                own = own + part.astype(f32)
            return lax.psum(own, "lat").astype(bf16)

        def body(own_ref, *refs):
            value = own_ref[...]
            for ref in refs[:-1]:
                value = value + ref[...].astype(f32)
            refs[-1][...] = value.astype(bf16)

        return call(body, [shape_of(own.shape, bf16)], [own] + received, name="combine_last")[0]

    group = stages[1]
    held = finish(own, received)
    stride = count
    for radix in reversed(stages[2:]):
        stride //= radix
        held = jnp.concatenate([held] + [swapped(held, count, stride, k) for k in range(1, radix)], axis=0)
    quarter = [held] + [swapped(held, count, 2, k) for k in range(1, group)]
    sibling = [swapped(held, count, 1, 1)]
    sibling += [swapped(after(q, input_gradient), count, 1, 1) for q in quarter[1:]]
    unit = flat // pieces

    def unpack(parts, which, previous):
        def body(*refs):
            second_out, first_out, flat_ref, stage, sems = refs[group + len(previous) :]
            for k, ref in enumerate(refs[:group]):
                stride, span = 2 * group, pieces // group
                walk = [((digit_of(2, group) ^ k) * span, 0)]
                for radix in stages[2:]:
                    digit = digit_of(stride, radix)
                    span //= radix
                    walk = [
                        (at + (digit ^ j) * span, order + j * span) for at, order in walk for j in range(radix)
                    ]
                    stride *= radix
                for at, order in walk:
                    target = pl.ds(pl.multiple_of(at * unit, ROW_TILE), unit)
                    flat_ref[0, target, :] = ref[order * unit : (order + 1) * unit, :].astype(f32)
            chosen = which(lax.rem(lax.axis_index("lon"), 2))

            def write(out, transposed):
                copies = []
                for tap, value in enumerate(load_flat(flat_ref, 0, channels)):
                    stage[tap] = (value.T if transposed else value) * scale
                    copies.append(pltpu.make_async_copy(stage.at[tap], out.at[tap // 3, tap % 3], sems.at[tap]))
                    copies[-1].start()
                for copy in copies:
                    copy.wait()

            @pl.when(chosen == 0)
            def _():
                write(second_out, False)

            @pl.when(chosen == 1)
            def _():
                write(first_out, True)

        return call(
            body,
            [shape_of((3, 3, channels, channels), f32)] * 2,
            parts + previous,
            [flat_scratch, pltpu.VMEM((9, channels, channels), f32), pltpu.SemaphoreType.DMA((9,))],
            name="unpack_gradient",
            far_args=tuple(range(group, group + len(previous))),
            far_outs=(0, 1),
            aliases={group + i: i for i in range(len(previous))},
        )

    own_written = unpack(quarter, lambda core: core, [])
    second_gradient, first_gradient = unpack(sibling, lambda core: 1 - core, list(own_written))
    return (input_gradient.reshape(height, width, channels), first_gradient, second_gradient)


def solution(mesh):
    placed = (P("lat", "lon", None), P("lat", "lon", None), P(), P())
    return jax.shard_map(
        shards,
        mesh=mesh,
        in_specs=placed,
        out_specs=(P("lat", "lon", None), P(), P()),
        check_vma=False,
    )
```

```python
import math

import jax
import jax.numpy as jnp
from jax import lax
from jax.experimental import pallas as pl
from jax.experimental.pallas import tpu as pltpu
from jax.sharding import PartitionSpec as P

FIRST_SPREAD = 32
SECOND_SPREAD = 64
LANES = 128
ROW_TILE = 16
G_SHARE = 5 / 8
X_SHARE = 1 / 2
VMEM_LIMIT = 20 * 1024 * 1024


def call(body, outs, args, scratch=(), flops=0, name=None, far_args=(), far_outs=(), aliases={}):
    moved = sum(a.size * a.dtype.itemsize for a in list(args) + list(outs))
    near, far = pl.BlockSpec(memory_space=pltpu.VMEM), pl.BlockSpec(memory_space=pltpu.HBM)
    return pl.pallas_call(
        body,
        out_shape=list(outs),
        in_specs=[far if i in far_args else near for i in range(len(args))],
        out_specs=[far if i in far_outs else near for i in range(len(outs))],
        scratch_shapes=list(scratch),
        input_output_aliases=aliases,
        compiler_params=pltpu.CompilerParams(vmem_limit_bytes=VMEM_LIMIT),
        cost_estimate=pl.CostEstimate(flops=flops, bytes_accessed=moved, transcendentals=0),
        name=name,
    )(*args)


def shape_of(shape, dtype):
    return jax.ShapeDtypeStruct(shape, dtype)


def packs(rows, channels):
    return channels % LANES * 2 == LANES and rows % (2 * ROW_TILE) == 0


def packed_shape(rows, channels):
    if not packs(rows, channels):
        return (rows, channels)
    full = channels // LANES
    return (rows * full + rows // 2, LANES)


def pack_into(refs, value):
    rows, channels = value.shape
    if packs(rows, channels):
        full = channels // LANES
        rest = value[:, full * LANES :]
        half = rows // 2
        tiles = [value[:, tile * LANES : (tile + 1) * LANES] for tile in range(full)]
        tiles.append(jnp.concatenate([rest[:half], rest[half:]], axis=1))
        value = jnp.concatenate(tiles, axis=0)
    begin = 0
    for ref in refs:
        ref[...] = value[begin : begin + ref.shape[0]]
        begin += ref.shape[0]


def unpacked(refs, rows, channels):
    parts = [ref[...] for ref in refs]
    ref = parts[0] if len(parts) == 1 else jnp.concatenate(parts, axis=0)
    if not packs(rows, channels):
        return ref
    full = channels // LANES
    rest = ref[full * rows :, :]
    width = channels - full * LANES
    tail = jnp.concatenate([rest[:, :width], rest[:, width:]], axis=0)
    return jnp.concatenate([ref[t * rows : (t + 1) * rows, :] for t in range(full)] + [tail], axis=1)


def extend(scratch, value, rim, width):
    rows = value.shape[0]
    scratch[width : width + rows, :] = value
    if rim is None:
        blank = jnp.zeros((width, value.shape[1]), value.dtype)
        scratch[:width, :] = blank
        scratch[width + rows :, :] = blank
    else:
        scratch[:width, :] = rim[:width, :]
        scratch[width + rows :, :] = rim[width:, :]


def row_blocks(rows):
    size = rows
    while size > 256 and size % 2 == 0 and size // 2 % ROW_TILE == 0:
        size //= 2
    return [(start, size) for start in range(0, rows, size)]


NT = (((1,), (1,)), ((), ()))
NN = (((1,), (0,)), ((), ()))


def conv_block(terms, start, size, width):
    total = None
    for ext, weight, b, flipped in terms:
        for a in (-1, 0, 1):
            tap = ext[start + (1 + a) * width : start + (1 + a) * width + size, :]
            kernel = weight[1 - a, 1 - b] if flipped else weight[1 + a, 1 + b]
            part = lax.dot_general(tap, kernel, NT if flipped else NN, preferred_element_type=jnp.float32)
            total = part if total is None else total + part
    return total


def part_rows(height, channels):
    full, width = divmod(channels, LANES)
    rows = 9 * height * full
    if width:
        rows += 9 * height // 2 if width * 2 == LANES else 9 * height
    return -(-rows // ROW_TILE) * ROW_TILE


def store_part(ref, start, end, blocks):
    height, channels = blocks[0].shape
    full, width = divmod(channels, LANES)
    row = start
    for block in blocks:
        for tile in range(full):
            ref[row : row + height, :] = block[:, tile * LANES : (tile + 1) * LANES]
            row += height
    rests = [block[:, full * LANES :] for block in blocks]
    if width and width * 2 != LANES:
        for rest in rests:
            ref[row : row + height, :width] = rest
            row += height
    elif width:
        for pair in range(0, 8, 2):
            ref[row : row + height, :] = jnp.concatenate([rests[pair], rests[pair + 1]], axis=1)
            row += height
        half = height // 2
        ref[row : row + half, :] = jnp.concatenate([rests[8][:half], rests[8][half:]], axis=1)
        row += half
    if row < end:
        ref[row:end, :] = jnp.zeros((end - row, LANES), ref.dtype)


def load_part(rows, height, channels):
    full, width = divmod(channels, LANES)
    parts = []
    for tap in range(9):
        at = tap * full * height
        parts.append([rows[at + t * height : at + (t + 1) * height] for t in range(full)])
    row = 9 * full * height
    if width and width * 2 != LANES:
        for tap in range(9):
            parts[tap].append(rows[row : row + height, :width])
            row += height
    elif width:
        for pair in range(0, 8, 2):
            both = rows[row : row + height]
            parts[pair].append(both[:, :width])
            parts[pair + 1].append(both[:, width:])
            row += height
        both = rows[row : row + height // 2]
        parts[8].append(jnp.concatenate([both[:, :width], both[:, width:]], axis=0))
    return [jnp.concatenate(p, axis=1) if len(p) > 1 else p[0] for p in parts]


def radices(count):
    found = []
    if count % 2 == 0:
        found.append(2)
        count //= 2
    while count % 4 == 0:
        found.append(4)
        count //= 4
    while count % 2 == 0:
        found.append(2)
        count //= 2
    return found if count == 1 else None


def swapped(value, count, stride, k):
    return lax.ppermute(value, "lon", [(i, i ^ (k * stride)) for i in range(count)])


def moved(value, steps):
    count = lax.axis_size("lon")
    if steps % count == 0:
        return value
    return lax.ppermute(value, "lon", [(i, (i + steps) % count) for i in range(count)])


def lat_rim(field):
    count = lax.axis_size("lat")
    if count == 1:
        return None
    north = lax.ppermute(field[-1], "lat", [(i, i + 1) for i in range(count - 1)])
    south = lax.ppermute(field[0], "lat", [(i + 1, i) for i in range(count - 1)])
    return jnp.stack([north, south])


def paired(spread, width):
    steps, rest = divmod(spread, width)
    return rest == 0 and lax.axis_size("lon") % (2 * steps) == 0


def side_of(spread, width):
    if not paired(spread, width):
        return 0
    return lax.rem(lax.axis_index("lon") // (spread // width), 2)


def inner_pairs(steps):
    return [(i, i + steps if i // steps % 2 == 0 else i - steps) for i in range(lax.axis_size("lon"))]


def outer_pairs(steps):
    count = lax.axis_size("lon")
    return [(i, (i - steps if i // steps % 2 == 0 else i + steps) % count) for i in range(count)]


def after(value, *others):
    return lax.optimization_barrier((value, *others))[0]


def beside(field, packed, spread, pack):
    width = field.shape[1]
    steps, rest = divmod(spread, width)
    if paired(spread, width):
        return (
            [lax.ppermute(packed, "lon", inner_pairs(steps))],
            [lax.ppermute(packed, "lon", outer_pairs(steps))],
        )
    if rest == 0:
        return [moved(packed, -steps)], [moved(packed, steps)]
    cut = width - rest
    west = jnp.concatenate([moved(field[:, cut:], steps + 1), moved(field[:, :cut], steps)], axis=1)
    east = jnp.concatenate([moved(field[:, rest:], -steps), moved(field[:, :rest], -steps - 1)], axis=1)
    return [pack(east)], [pack(west)]


def onward_pairs(steps):
    count = lax.axis_size("lon")
    return [(i, (i + 2 * steps if i // steps % 2 == 0 else i - 2 * steps) % count) for i in range(count)]


def shards(inputs, cotangent, first_weight, second_weight):
    height, width, channels = inputs.shape
    rows = height * width
    count = lax.axis_size("lon")
    scale = 1.0 / math.sqrt(rows * lax.axis_size("lat") * count)
    bf16, f32 = jnp.bfloat16, jnp.float32
    pshape = packed_shape(rows, channels)
    ext_rows = rows + 2 * width
    ext_shape, turned_shape = (ext_rows, channels), (3 * channels, rows)
    ext = pltpu.VMEM(ext_shape, bf16)
    tap_flops = 2 * rows * channels * channels
    blocks = row_blocks(rows)

    def pack_body(source, *targets):
        pack_into(targets, source[...])

    def pack_one(field, share=None):
        sizes = [pshape[0]]
        if share is not None:
            first = max(int(pshape[0] * share) // ROW_TILE, 1) * ROW_TILE
            sizes = [first, pshape[0] - first]
        shapes = [shape_of((size, pshape[1]), bf16) for size in sizes]
        packed = call(pack_body, shapes, [field.reshape(rows, channels)], name="pack")
        return packed[0] if share is None else packed

    def rims_of(field, spread):
        rim = lat_rim(field)
        if rim is None:
            return []
        inner, outer = beside(rim, rim, spread, lambda r: r)
        return [r.reshape(2 * width, channels) for r in (rim, *inner, *outer)]

    def turn(target, source):
        for a in range(3):
            value = source[a * width : a * width + rows, :].astype(f32).T
            target[a * channels : (a + 1) * channels, :] = value.astype(bf16)

    def near_part(field, weight, inner, rims, spread, flipped, name, keep=None):
        def body(x_ref, w_ref, *rest):
            refs, rest = rest[: len(inner)], rest[len(inner) :]
            (own_rim, inner_rim), (part, *rest) = (rest[:2], rest[2:]) if rimmed else ((None, None), rest)
            e0, e1 = rest[:2] if keep == "rims" else rest[-2:]
            extend(e0, x_ref[...], own_rim, width)
            extend(e1, unpacked(refs, rows, channels), inner_rim, width)
            b = 1 - 2 * side_of(spread, width)
            for start, size in blocks:
                part[start : start + size, :] = conv_block(
                    [(e0, w_ref, 0, flipped), (e1, w_ref, b, flipped)], start, size, width
                )
            if keep == "turned":
                turn(rest[0], e0)
                turn(rest[1], e1)

        args = [field, weight] + inner + rims[:2]
        kept = {"rims": ext_shape, "turned": turned_shape}
        outs = [shape_of((rows, channels), f32)] + ([shape_of(kept[keep], bf16)] * 2 if keep else [])
        return call(body, outs, args, [] if keep == "rims" else [ext, ext], 6 * tap_flops, name)

    def far_part(part_ref, scratch, w_ref, spread, flipped, start, size):
        b = 2 * side_of(spread, width) - 1
        return part_ref[start : start + size, :] + conv_block([(scratch, w_ref, b, flipped)], start, size, width)

    x = inputs.reshape(rows, channels)
    g = cotangent.reshape(rows, channels)
    x_rims = rims_of(inputs, FIRST_SPREAD)
    g_rims = rims_of(cotangent, SECOND_SPREAD)
    rimmed = bool(x_rims)

    if paired(SECOND_SPREAD, width):
        steps = SECOND_SPREAD // width
        g_packed = pack_one(cotangent, G_SHARE)
        g_inner = [lax.ppermute(part, "lon", inner_pairs(steps)) for part in g_packed]
        g_outer = [
            lax.ppermute(g_inner[0], "lon", onward_pairs(steps)),
            lax.ppermute(g_packed[1], "lon", outer_pairs(steps)),
        ]
    else:
        g_inner, g_outer = beside(cotangent, pack_one(cotangent), SECOND_SPREAD, pack_one)
    if paired(FIRST_SPREAD, width):
        steps = FIRST_SPREAD // width
        x_packed = pack_one(after(inputs, *g_packed), X_SHARE)
        x_inner = [lax.ppermute(part, "lon", inner_pairs(steps)) for part in x_packed]
        x_outer = [lax.ppermute(part, "lon", outer_pairs(steps)) for part in x_packed]
    else:
        x_inner, x_outer = beside(inputs, pack_one(inputs), FIRST_SPREAD, pack_one)
    part1, x_own, x_near = near_part(
        x, first_weight, x_inner, x_rims, FIRST_SPREAD, False, "near_pre_act", "turned"
    )
    part2, g_own, g_near = near_part(
        g, second_weight, g_inner, g_rims, SECOND_SPREAD, True, "near_hidden_grad", "rims"
    )

    def hidden_body(part_ref, w_ref, *rest):
        side_refs, rest = rest[: len(x_outer)], rest[len(x_outer) :]
        (rim,), (hidden_t, slope, turned, se, hid) = (rest[:1], rest[1:]) if rimmed else ((None,), rest)
        extend(se, unpacked(side_refs, rows, channels), rim, width)
        for start, size in blocks:
            act = far_part(part_ref, se, w_ref, FIRST_SPREAD, False, start, size)
            sigma = jax.nn.sigmoid(act)
            slope[start : start + size, :] = sigma * (1.0 + act * (1.0 - sigma))
            hid[start : start + size, :] = (act * sigma).astype(bf16).astype(f32)
        hidden_t[...] = hid[...].T.astype(bf16)
        turn(turned, se)

    hidden_t, slope, x_far = call(
        hidden_body,
        [shape_of((channels, rows), bf16), shape_of((rows, channels), f32), shape_of(turned_shape, bf16)],
        [part1, first_weight] + x_outer + x_rims[2:],
        [ext, pltpu.VMEM((rows, channels), f32)],
        flops=3 * tap_flops,
        name="hidden",
    )

    def second_sums(hid_ref, field):
        return [
            jnp.dot(hid_ref[...], field[(1 - a) * width : (1 - a) * width + rows, :], preferred_element_type=f32)
            for a in (-1, 0, 1)
        ]

    def grad_body(part_ref, slope_ref, w_ref, *rest):
        side_refs, rest = rest[: len(g_outer)], rest[len(g_outer) :]
        (rim,), (pre_grad, packed, se) = (rest[:1], rest[1:]) if rimmed else ((None,), rest)
        extend(se, unpacked(side_refs, rows, channels), rim, width)
        for start, size in blocks:
            grad = far_part(part_ref, se, w_ref, SECOND_SPREAD, True, start, size)
            pre_grad[start : start + size, :] = (grad * slope_ref[start : start + size, :]).astype(bf16)
        pack_into([packed], pre_grad[...])

    pre_grad, pre_packed, g_far = call(
        grad_body,
        [shape_of((rows, channels), bf16), shape_of(pshape, bf16), shape_of(ext_shape, bf16)],
        [part2, slope, second_weight] + g_outer + g_rims[2:],
        flops=3 * tap_flops,
        name="pre_grad",
    )

    stages = radices(count)
    group = stages[1]
    later = stages[2:]
    height_of_part = channels // group
    part_size = part_rows(height_of_part, channels)
    sizes = []
    for radix in later:
        size = -(-part_size // (radix * ROW_TILE)) * ROW_TILE
        step = (part_size - size) // (radix - 1)
        if len(later) > 1 or step % ROW_TILE or step * (radix - 1) + size != part_size:
            part_size = -(-part_size // (math.prod(later) * ROW_TILE)) * math.prod(later) * ROW_TILE
            break
        sizes = [(size, step)]
    if len(sizes) < len(later):
        sizes, size = [], part_size
        for radix in later:
            size //= radix
            sizes.append((size, size))
    flat = group * part_size

    def kernel_gradient(which):
        def body(hid_ref, g0, g1, g2, pre_ref, x0, x1, x2, out, flat_ref):
            chosen = which(lax.rem(lax.axis_index("lon"), 2))

            def put(mid, inner, outer, spread, sign):
                east_first = side_of(spread, width) == 0
                nine = []
                for at in range(3):
                    east = jnp.where(east_first, inner[at], outer[at])
                    west = jnp.where(east_first, outer[at], inner[at])
                    nine += [west, mid[at], east][::sign]
                for c in range(group):
                    rows_of = slice(c * height_of_part, (c + 1) * height_of_part)
                    store_part(flat_ref, c * part_size, (c + 1) * part_size, [block[rows_of] for block in nine])

            @pl.when(chosen == 0)
            def _():
                put(*(second_sums(hid_ref, ref) for ref in (g0, g1, g2)), SECOND_SPREAD, -1)

            @pl.when(chosen == 1)
            def _():
                sums = [jnp.dot(ref[...], pre_ref[...], preferred_element_type=f32) for ref in (x0, x1, x2)]
                put(*([t[a * channels : (a + 1) * channels] for a in range(3)] for t in sums), FIRST_SPREAD, 1)

            out[...] = flat_ref[...].astype(out.dtype)

        return body

    fields = [hidden_t, g_own, g_near, g_far, pre_grad, x_own, x_near, x_far]
    flat_scratch = pltpu.VMEM((flat, LANES), f32)
    (send,) = call(
        kernel_gradient(lambda core: 1 - core),
        [shape_of((flat, LANES), bf16)],
        fields,
        [flat_scratch],
        flops=9 * tap_flops,
        name="sibling_kernel_gradient",
    )
    received = [swapped(send, count, 1, 1)]
    (own,) = call(
        kernel_gradient(lambda core: core),
        [shape_of((flat, LANES), f32)],
        fields,
        [flat_scratch],
        flops=9 * tap_flops,
        name="own_kernel_gradient",
    )

    def digit_of(stride, radix):
        return lax.rem(lax.axis_index("lon") // stride, radix)

    def combine(own, received, stride, radix, size, step):
        def body(own_ref, *refs):
            got, (mine, *sends) = refs[: len(received)], refs[len(received) :]
            digit = digit_of(stride, radix)
            for k, target in enumerate([mine] + sends):
                at = pl.ds(pl.multiple_of((digit ^ k) * step, ROW_TILE), size)
                value = own_ref[at, :]
                for ref in got:
                    value = value + ref[at, :].astype(f32)
                target[...] = value.astype(target.dtype)

        outs = [shape_of((size, LANES), f32)] + [shape_of((size, LANES), bf16)] * (radix - 1)
        return call(body, outs, [own] + received, name="combine")

    stride = 2
    plane_got = None
    for radix, (size, step) in zip(stages[1:], [(part_size, part_size)] + sizes):
        own, *sends = combine(own, received, stride, radix, size, step)
        received = [swapped(part, count, stride, k + 1) for k, part in enumerate(sends)]
        plane_got = received[-1] if plane_got is None else plane_got
        stride *= radix
    pre_field = pre_grad.reshape(height, width, channels)
    p_rims = rims_of(pre_field, FIRST_SPREAD)
    if paired(FIRST_SPREAD, width):
        steps = FIRST_SPREAD // width
        p_inner = [lax.ppermute(pre_packed, "lon", inner_pairs(steps))]
        p_outer = [lax.ppermute(after(pre_packed, plane_got), "lon", outer_pairs(steps))]
    else:
        p_inner, p_outer = beside(pre_field, pre_packed, FIRST_SPREAD, pack_one)
    (part3,) = near_part(pre_grad, first_weight, p_inner, p_rims, FIRST_SPREAD, True, "near_input_gradient")

    def input_body(part_ref, w_ref, *rest):
        side_refs, rest = rest[: len(p_outer)], rest[len(p_outer) :]
        (rim,), (out, se) = (rest[:1], rest[1:]) if rimmed else ((None,), rest)
        extend(se, unpacked(side_refs, rows, channels), rim, width)
        for start, size in blocks:
            out[start : start + size, :] = far_part(part_ref, se, w_ref, FIRST_SPREAD, True, start, size).astype(bf16)

    (input_gradient,) = call(
        input_body,
        [shape_of((rows, channels), bf16)],
        [part3, first_weight] + p_outer + p_rims[2:],
        [ext],
        flops=3 * tap_flops,
        name="input_gradient",
    )

    def finish(own, received):
        if lax.axis_size("lat") > 1:
            for part in received:
                own = own + part.astype(f32)
            return lax.psum(own, "lat").astype(bf16)

        def body(own_ref, *refs):
            value = own_ref[...]
            for ref in refs[:-1]:
                value = value + ref[...].astype(f32)
            refs[-1][...] = value.astype(bf16)

        return call(body, [shape_of(own.shape, bf16)], [own] + received, name="combine_last")[0]

    def assemble(pieces, stride, radix, size, step):
        def body(*refs):
            digit = digit_of(stride, radix)
            for k, ref in enumerate(refs[:-1]):
                place = digit ^ k
                refs[-1][pl.ds(pl.multiple_of(place * step, ROW_TILE), step), :] = ref[:step, :]
                if step < size:

                    @pl.when(place == radix - 1)
                    def _():
                        refs[-1][radix * step :, :] = ref[step:, :]

        total = step * (radix - 1) + size
        return call(body, [shape_of((total, LANES), bf16)], pieces, name="assemble")[0]

    held = finish(own, received)
    stride = count
    for radix, (size, step) in reversed(list(zip(later, sizes))):
        stride //= radix
        pieces = [held] + [swapped(held, count, stride, k) for k in range(1, radix)]
        held = assemble(pieces, stride, radix, size, step)
    def unpack(parts, previous):
        def body(*refs):
            second_out, first_out, stage, sems = refs[len(parts) + len(previous) :]
            core = lax.rem(lax.axis_index("lon"), 2)
            for i, (_, k, side) in enumerate(parts):
                for tap, value in enumerate(load_part(refs[i][...].astype(f32), height_of_part, channels)):
                    stage[i, tap] = value * scale
                start = pl.multiple_of((digit_of(2, group) ^ k) * height_of_part, height_of_part)
                for which, out in enumerate((second_out, first_out)):

                    @pl.when((core + side) % 2 == which)
                    def _():
                        for tap in range(9):
                            target = out.at[tap // 3, tap % 3, pl.ds(start, height_of_part)]
                            pltpu.make_async_copy(stage.at[i, tap], target, sems.at[9 * i + tap]).start()

            for i in range(len(parts)):
                for tap in range(9):
                    target = second_out.at[tap // 3, tap % 3, pl.ds(0, height_of_part)]
                    pltpu.make_async_copy(stage.at[i, tap], target, sems.at[9 * i + tap]).wait()

        count_in = len(parts)
        return list(
            call(
                body,
                [shape_of((3, 3, channels, channels), f32)] * 2,
                [array for array, _, _ in parts] + previous,
                [
                    pltpu.VMEM((count_in, 9, height_of_part, channels), f32),
                    pltpu.SemaphoreType.DMA((9 * count_in,)),
                ],
                name="unpack_gradients",
                far_args=tuple(range(count_in, count_in + len(previous))),
                far_outs=(0, 1),
                aliases={count_in + i: i for i in range(len(previous))},
            )
        )

    quarter = [held] + [swapped(held, count, 2, k) for k in range(1, group)]
    sibling = [swapped(held, count, 1, 1)]
    sibling += [swapped(after(q, input_gradient), count, 1, 1) for q in quarter[1:]]
    written = unpack([(part, k, 0) for k, part in enumerate(quarter)], [])
    written = unpack([(part, k, 1) for k, part in enumerate(sibling)], written)
    second_gradient, first_gradient = written
    return (input_gradient.reshape(height, width, channels), first_gradient, second_gradient)


def solution(mesh):
    placed = (P("lat", "lon", None), P("lat", "lon", None), P(), P())
    return jax.shard_map(
        shards,
        mesh=mesh,
        in_specs=placed,
        out_specs=(P("lat", "lon", None), P(), P()),
        check_vma=False,
    )
```

```python
import math

import jax
import jax.numpy as jnp
from jax import lax
from jax.experimental import pallas as pl
from jax.experimental.pallas import tpu as pltpu
from jax.sharding import PartitionSpec as P

FIRST_SPREAD = 32
SECOND_SPREAD = 64
LANES = 128
ROW_TILE = 16
G_SHARE = (7, 12)
X_SHARE = (49, 96)
VMEM_LIMIT = 20 * 1024 * 1024


def call(body, outs, args, scratch=(), flops=0, name=None, far_args=(), far_outs=(), aliases={}):
    moved = sum(a.size * a.dtype.itemsize for a in list(args) + list(outs))
    near, far = pl.BlockSpec(memory_space=pltpu.VMEM), pl.BlockSpec(memory_space=pltpu.HBM)
    return pl.pallas_call(
        body,
        out_shape=list(outs),
        in_specs=[far if i in far_args else near for i in range(len(args))],
        out_specs=[far if i in far_outs else near for i in range(len(outs))],
        scratch_shapes=list(scratch),
        input_output_aliases=aliases,
        compiler_params=pltpu.CompilerParams(vmem_limit_bytes=VMEM_LIMIT),
        cost_estimate=pl.CostEstimate(flops=flops, bytes_accessed=moved, transcendentals=0),
        name=name,
    )(*args)


def shape_of(shape, dtype):
    return jax.ShapeDtypeStruct(shape, dtype)


def packs(rows, channels):
    return channels % LANES * 2 == LANES and rows % (2 * ROW_TILE) == 0


def packed_shape(rows, channels):
    if not packs(rows, channels):
        return (rows, channels)
    full = channels // LANES
    return (rows * full + rows // 2, LANES)


def pack_into(refs, value):
    rows, channels = value.shape
    if packs(rows, channels):
        full = channels // LANES
        rest = value[:, full * LANES :]
        half = rows // 2
        tiles = [value[:, tile * LANES : (tile + 1) * LANES] for tile in range(full)]
        tiles.append(jnp.concatenate([rest[:half], rest[half:]], axis=1))
        value = jnp.concatenate(tiles, axis=0)
    begin = 0
    for ref in refs:
        ref[...] = value[begin : begin + ref.shape[0]]
        begin += ref.shape[0]


def unpacked(refs, rows, channels):
    parts = [ref[...] for ref in refs]
    ref = parts[0] if len(parts) == 1 else jnp.concatenate(parts, axis=0)
    if not packs(rows, channels):
        return ref
    full = channels // LANES
    rest = ref[full * rows :, :]
    width = channels - full * LANES
    tail = jnp.concatenate([rest[:, :width], rest[:, width:]], axis=0)
    return jnp.concatenate([ref[t * rows : (t + 1) * rows, :] for t in range(full)] + [tail], axis=1)


def extend(scratch, value, rim, width):
    rows = value.shape[0]
    scratch[width : width + rows, :] = value
    if rim is None:
        blank = jnp.zeros((width, value.shape[1]), value.dtype)
        scratch[:width, :] = blank
        scratch[width + rows :, :] = blank
    else:
        scratch[:width, :] = rim[:width, :]
        scratch[width + rows :, :] = rim[width:, :]


def row_blocks(rows):
    size = rows
    while size > 256 and size % 2 == 0 and size // 2 % ROW_TILE == 0:
        size //= 2
    return [(start, size) for start in range(0, rows, size)]


NT = (((1,), (1,)), ((), ()))
NN = (((1,), (0,)), ((), ()))


def conv_block(terms, start, size, width):
    total = None
    for ext, weight, b, flipped in terms:
        for a in (-1, 0, 1):
            tap = ext[start + (1 + a) * width : start + (1 + a) * width + size, :]
            kernel = weight[1 - a, 1 - b] if flipped else weight[1 + a, 1 + b]
            part = lax.dot_general(tap, kernel, NT if flipped else NN, preferred_element_type=jnp.float32)
            total = part if total is None else total + part
    return total


def part_rows(height, channels):
    full, width = divmod(channels, LANES)
    rows = 9 * height * full
    if width:
        rows += 9 * height // 2 if width * 2 == LANES else 9 * height
    return -(-rows // ROW_TILE) * ROW_TILE


def store_part(ref, start, end, blocks):
    height, channels = blocks[0].shape
    full, width = divmod(channels, LANES)
    row = start
    for block in blocks:
        for tile in range(full):
            ref[row : row + height, :] = block[:, tile * LANES : (tile + 1) * LANES]
            row += height
    rests = [block[:, full * LANES :] for block in blocks]
    if width and width * 2 != LANES:
        for rest in rests:
            ref[row : row + height, :width] = rest
            row += height
    elif width:
        for pair in range(0, 8, 2):
            ref[row : row + height, :] = jnp.concatenate([rests[pair], rests[pair + 1]], axis=1)
            row += height
        half = height // 2
        ref[row : row + half, :] = jnp.concatenate([rests[8][:half], rests[8][half:]], axis=1)
        row += half
    if row < end:
        ref[row:end, :] = jnp.zeros((end - row, LANES), ref.dtype)


def load_part(rows, height, channels):
    full, width = divmod(channels, LANES)
    parts = []
    for tap in range(9):
        at = tap * full * height
        parts.append([rows[at + t * height : at + (t + 1) * height] for t in range(full)])
    row = 9 * full * height
    if width and width * 2 != LANES:
        for tap in range(9):
            parts[tap].append(rows[row : row + height, :width])
            row += height
    elif width:
        for pair in range(0, 8, 2):
            both = rows[row : row + height]
            parts[pair].append(both[:, :width])
            parts[pair + 1].append(both[:, width:])
            row += height
        both = rows[row : row + height // 2]
        parts[8].append(jnp.concatenate([both[:, :width], both[:, width:]], axis=0))
    return [jnp.concatenate(p, axis=1) if len(p) > 1 else p[0] for p in parts]


def radices(count):
    found = []
    if count % 2 == 0:
        found.append(2)
        count //= 2
    while count % 4 == 0:
        found.append(4)
        count //= 4
    while count % 2 == 0:
        found.append(2)
        count //= 2
    return found if count == 1 else None


def swapped(value, count, stride, k):
    return lax.ppermute(value, "lon", [(i, i ^ (k * stride)) for i in range(count)])


def moved(value, steps):
    count = lax.axis_size("lon")
    if steps % count == 0:
        return value
    return lax.ppermute(value, "lon", [(i, (i + steps) % count) for i in range(count)])


def lat_rim(field):
    count = lax.axis_size("lat")
    if count == 1:
        return None
    north = lax.ppermute(field[-1], "lat", [(i, i + 1) for i in range(count - 1)])
    south = lax.ppermute(field[0], "lat", [(i + 1, i) for i in range(count - 1)])
    return jnp.stack([north, south])


def paired(spread, width):
    steps, rest = divmod(spread, width)
    return rest == 0 and lax.axis_size("lon") % (2 * steps) == 0


def side_of(spread, width):
    if not paired(spread, width):
        return 0
    return lax.rem(lax.axis_index("lon") // (spread // width), 2)


def inner_pairs(steps):
    return [(i, i + steps if i // steps % 2 == 0 else i - steps) for i in range(lax.axis_size("lon"))]


def outer_pairs(steps):
    count = lax.axis_size("lon")
    return [(i, (i - steps if i // steps % 2 == 0 else i + steps) % count) for i in range(count)]


def after(value, *others):
    return lax.optimization_barrier((value, *others))[0]


def beside(field, packed, spread, pack):
    width = field.shape[1]
    steps, rest = divmod(spread, width)
    if paired(spread, width):
        return (
            [lax.ppermute(packed, "lon", inner_pairs(steps))],
            [lax.ppermute(packed, "lon", outer_pairs(steps))],
        )
    if rest == 0:
        return [moved(packed, -steps)], [moved(packed, steps)]
    cut = width - rest
    west = jnp.concatenate([moved(field[:, cut:], steps + 1), moved(field[:, :cut], steps)], axis=1)
    east = jnp.concatenate([moved(field[:, rest:], -steps), moved(field[:, :rest], -steps - 1)], axis=1)
    return [pack(east)], [pack(west)]


def onward_pairs(steps):
    count = lax.axis_size("lon")
    return [(i, (i + 2 * steps if i // steps % 2 == 0 else i - 2 * steps) % count) for i in range(count)]


def shards(inputs, cotangent, first_weight, second_weight):
    height, width, channels = inputs.shape
    rows = height * width
    count = lax.axis_size("lon")
    scale = 1.0 / math.sqrt(rows * lax.axis_size("lat") * count)
    bf16, f32 = jnp.bfloat16, jnp.float32
    pshape = packed_shape(rows, channels)
    ext_rows = rows + 2 * width
    ext_shape, turned_shape = (ext_rows, channels), (3 * channels, rows)
    ext = pltpu.VMEM(ext_shape, bf16)
    tap_flops = 2 * rows * channels * channels
    blocks = row_blocks(rows)

    def pack_body(source, *targets):
        pack_into(targets, source[...])

    def pack_one(field, share=None):
        sizes = [pshape[0]]
        if share is not None:
            first = max(pshape[0] * share[0] // share[1] // ROW_TILE, 1) * ROW_TILE
            sizes = [first, pshape[0] - first]
        shapes = [shape_of((size, pshape[1]), bf16) for size in sizes]
        packed = call(pack_body, shapes, [field.reshape(rows, channels)], name="pack")
        return packed[0] if share is None else packed

    def rims_of(field, spread):
        rim = lat_rim(field)
        if rim is None:
            return []
        inner, outer = beside(rim, rim, spread, lambda r: r)
        return [r.reshape(2 * width, channels) for r in (rim, *inner, *outer)]

    def turn(target, source):
        for a in range(3):
            value = source[a * width : a * width + rows, :].astype(f32).T
            target[a * channels : (a + 1) * channels, :] = value.astype(bf16)

    def near_part(field, weight, inner, rims, spread, flipped, name, keep=None):
        def body(x_ref, w_ref, *rest):
            refs, rest = rest[: len(inner)], rest[len(inner) :]
            (own_rim, inner_rim), (part, *rest) = (rest[:2], rest[2:]) if rimmed else ((None, None), rest)
            e0, e1 = rest[:2] if keep == "rims" else rest[-2:]
            extend(e0, x_ref[...], own_rim, width)
            extend(e1, unpacked(refs, rows, channels), inner_rim, width)
            b = 1 - 2 * side_of(spread, width)
            for start, size in blocks:
                part[start : start + size, :] = conv_block(
                    [(e0, w_ref, 0, flipped), (e1, w_ref, b, flipped)], start, size, width
                )
            if keep == "turned":
                turn(rest[0], e0)
                turn(rest[1], e1)

        args = [field, weight] + inner + rims[:2]
        kept = {"rims": ext_shape, "turned": turned_shape}
        outs = [shape_of((rows, channels), f32)] + ([shape_of(kept[keep], bf16)] * 2 if keep else [])
        return call(body, outs, args, [] if keep == "rims" else [ext, ext], 6 * tap_flops, name)

    def far_part(part_ref, scratch, w_ref, spread, flipped, start, size):
        b = 2 * side_of(spread, width) - 1
        return part_ref[start : start + size, :] + conv_block([(scratch, w_ref, b, flipped)], start, size, width)

    x = inputs.reshape(rows, channels)
    g = cotangent.reshape(rows, channels)
    x_rims = rims_of(inputs, FIRST_SPREAD)
    g_rims = rims_of(cotangent, SECOND_SPREAD)
    rimmed = bool(x_rims)

    if paired(SECOND_SPREAD, width):
        steps = SECOND_SPREAD // width
        g_packed = pack_one(cotangent, G_SHARE)
        g_inner = [lax.ppermute(part, "lon", inner_pairs(steps)) for part in g_packed]
        g_outer = [
            lax.ppermute(g_inner[0], "lon", onward_pairs(steps)),
            lax.ppermute(g_packed[1], "lon", outer_pairs(steps)),
        ]
    else:
        g_inner, g_outer = beside(cotangent, pack_one(cotangent), SECOND_SPREAD, pack_one)
    if paired(FIRST_SPREAD, width):
        steps = FIRST_SPREAD // width
        x_packed = pack_one(after(inputs, *g_packed), X_SHARE)
        x_inner = [lax.ppermute(part, "lon", inner_pairs(steps)) for part in x_packed]
        x_outer = [lax.ppermute(part, "lon", outer_pairs(steps)) for part in x_packed]
    else:
        x_inner, x_outer = beside(inputs, pack_one(inputs), FIRST_SPREAD, pack_one)
    part1, x_own, x_near = near_part(
        x, first_weight, x_inner, x_rims, FIRST_SPREAD, False, "near_pre_act", "turned"
    )
    part2, g_own, g_near = near_part(
        g, second_weight, g_inner, g_rims, SECOND_SPREAD, True, "near_hidden_grad", "rims"
    )

    def hidden_body(part_ref, w_ref, *rest):
        side_refs, rest = rest[: len(x_outer)], rest[len(x_outer) :]
        (rim,), (hidden_t, slope, turned, se, hid) = (rest[:1], rest[1:]) if rimmed else ((None,), rest)
        extend(se, unpacked(side_refs, rows, channels), rim, width)
        for start, size in blocks:
            act = far_part(part_ref, se, w_ref, FIRST_SPREAD, False, start, size)
            sigma = jax.nn.sigmoid(act)
            slope[start : start + size, :] = sigma * (1.0 + act * (1.0 - sigma))
            hid[start : start + size, :] = (act * sigma).astype(bf16).astype(f32)
        hidden_t[...] = hid[...].T.astype(bf16)
        turn(turned, se)

    hidden_t, slope, x_far = call(
        hidden_body,
        [shape_of((channels, rows), bf16), shape_of((rows, channels), f32), shape_of(turned_shape, bf16)],
        [part1, first_weight] + x_outer + x_rims[2:],
        [ext, pltpu.VMEM((rows, channels), f32)],
        flops=3 * tap_flops,
        name="hidden",
    )

    def second_sums(hid_ref, field):
        return [
            jnp.dot(hid_ref[...], field[(1 - a) * width : (1 - a) * width + rows, :], preferred_element_type=f32)
            for a in (-1, 0, 1)
        ]

    def grad_body(part_ref, slope_ref, w_ref, *rest):
        side_refs, rest = rest[: len(g_outer)], rest[len(g_outer) :]
        (rim,), (pre_grad, packed, se) = (rest[:1], rest[1:]) if rimmed else ((None,), rest)
        extend(se, unpacked(side_refs, rows, channels), rim, width)
        for start, size in blocks:
            grad = far_part(part_ref, se, w_ref, SECOND_SPREAD, True, start, size)
            pre_grad[start : start + size, :] = (grad * slope_ref[start : start + size, :]).astype(bf16)
        pack_into([packed], pre_grad[...])

    pre_grad, pre_packed, g_far = call(
        grad_body,
        [shape_of((rows, channels), bf16), shape_of(pshape, bf16), shape_of(ext_shape, bf16)],
        [part2, slope, second_weight] + g_outer + g_rims[2:],
        flops=3 * tap_flops,
        name="pre_grad",
    )

    stages = radices(count)
    group = stages[1]
    later = stages[2:]
    height_of_part = channels // group
    part_size = part_rows(height_of_part, channels)
    sizes = []
    for radix in later:
        size = -(-part_size // (radix * ROW_TILE)) * ROW_TILE
        step = (part_size - size) // (radix - 1)
        if len(later) > 1 or step % ROW_TILE or step * (radix - 1) + size != part_size:
            part_size = -(-part_size // (math.prod(later) * ROW_TILE)) * math.prod(later) * ROW_TILE
            break
        sizes = [(size, step)]
    if len(sizes) < len(later):
        sizes, size = [], part_size
        for radix in later:
            size //= radix
            sizes.append((size, size))
    flat = group * part_size

    def kernel_gradient(which):
        def body(hid_ref, g0, g1, g2, pre_ref, x0, x1, x2, out, flat_ref):
            chosen = which(lax.rem(lax.axis_index("lon"), 2))

            def put(mid, inner, outer, spread, sign):
                east_first = side_of(spread, width) == 0
                nine = []
                for at in range(3):
                    east = jnp.where(east_first, inner[at], outer[at])
                    west = jnp.where(east_first, outer[at], inner[at])
                    nine += [west, mid[at], east][::sign]
                for c in range(group):
                    rows_of = slice(c * height_of_part, (c + 1) * height_of_part)
                    store_part(flat_ref, c * part_size, (c + 1) * part_size, [block[rows_of] for block in nine])

            @pl.when(chosen == 0)
            def _():
                put(*(second_sums(hid_ref, ref) for ref in (g0, g1, g2)), SECOND_SPREAD, -1)

            @pl.when(chosen == 1)
            def _():
                sums = [jnp.dot(ref[...], pre_ref[...], preferred_element_type=f32) for ref in (x0, x1, x2)]
                put(*([t[a * channels : (a + 1) * channels] for a in range(3)] for t in sums), FIRST_SPREAD, 1)

            out[...] = flat_ref[...].astype(out.dtype)

        return body

    fields = [hidden_t, g_own, g_near, g_far, pre_grad, x_own, x_near, x_far]
    flat_scratch = pltpu.VMEM((flat, LANES), f32)
    (send,) = call(
        kernel_gradient(lambda core: 1 - core),
        [shape_of((flat, LANES), bf16)],
        fields,
        [flat_scratch],
        flops=9 * tap_flops,
        name="sibling_kernel_gradient",
    )
    received = [swapped(send, count, 1, 1)]
    (own,) = call(
        kernel_gradient(lambda core: core),
        [shape_of((flat, LANES), f32)],
        fields,
        [flat_scratch],
        flops=9 * tap_flops,
        name="own_kernel_gradient",
    )

    def digit_of(stride, radix):
        return lax.rem(lax.axis_index("lon") // stride, radix)

    def combine(own, received, stride, radix, size, step):
        def body(own_ref, *refs):
            got, (mine, *sends) = refs[: len(received)], refs[len(received) :]
            digit = digit_of(stride, radix)
            for k, target in enumerate([mine] + sends):
                at = pl.ds(pl.multiple_of((digit ^ k) * step, ROW_TILE), size)
                value = own_ref[at, :]
                for ref in got:
                    value = value + ref[at, :].astype(f32)
                target[...] = value.astype(target.dtype)

        outs = [shape_of((size, LANES), f32)] + [shape_of((size, LANES), bf16)] * (radix - 1)
        return call(body, outs, [own] + received, name="combine")

    stride = 2
    plane_got = None
    for radix, (size, step) in zip(stages[1:], [(part_size, part_size)] + sizes):
        own, *sends = combine(own, received, stride, radix, size, step)
        received = [swapped(part, count, stride, k + 1) for k, part in enumerate(sends)]
        plane_got = received[-1] if plane_got is None else plane_got
        stride *= radix
    pre_field = pre_grad.reshape(height, width, channels)
    p_rims = rims_of(pre_field, FIRST_SPREAD)
    if paired(FIRST_SPREAD, width):
        steps = FIRST_SPREAD // width
        p_inner = [lax.ppermute(pre_packed, "lon", inner_pairs(steps))]
        p_outer = [lax.ppermute(after(pre_packed, plane_got), "lon", outer_pairs(steps))]
    else:
        p_inner, p_outer = beside(pre_field, pre_packed, FIRST_SPREAD, pack_one)
    (part3,) = near_part(pre_grad, first_weight, p_inner, p_rims, FIRST_SPREAD, True, "near_input_gradient")

    def input_body(part_ref, w_ref, *rest):
        side_refs, rest = rest[: len(p_outer)], rest[len(p_outer) :]
        (rim,), (out, se) = (rest[:1], rest[1:]) if rimmed else ((None,), rest)
        extend(se, unpacked(side_refs, rows, channels), rim, width)
        for start, size in blocks:
            out[start : start + size, :] = far_part(part_ref, se, w_ref, FIRST_SPREAD, True, start, size).astype(bf16)

    (input_gradient,) = call(
        input_body,
        [shape_of((rows, channels), bf16)],
        [part3, first_weight] + p_outer + p_rims[2:],
        [ext],
        flops=3 * tap_flops,
        name="input_gradient",
    )

    def finish(own, received):
        if lax.axis_size("lat") > 1:
            for part in received:
                own = own + part.astype(f32)
            return lax.psum(own, "lat").astype(bf16)

        def body(own_ref, *refs):
            value = own_ref[...]
            for ref in refs[:-1]:
                value = value + ref[...].astype(f32)
            refs[-1][...] = value.astype(bf16)

        return call(body, [shape_of(own.shape, bf16)], [own] + received, name="combine_last")[0]

    def assemble(pieces, stride, radix, size, step):
        def body(*refs):
            digit = digit_of(stride, radix)
            for k, ref in enumerate(refs[:-1]):
                place = digit ^ k
                refs[-1][pl.ds(pl.multiple_of(place * step, ROW_TILE), step), :] = ref[:step, :]
                if step < size:

                    @pl.when(place == radix - 1)
                    def _():
                        refs[-1][radix * step :, :] = ref[step:, :]

        total = step * (radix - 1) + size
        return call(body, [shape_of((total, LANES), bf16)], pieces, name="assemble")[0]

    held = finish(own, received)
    stride = count
    for radix, (size, step) in reversed(list(zip(later, sizes))):
        stride //= radix
        pieces = [held] + [swapped(held, count, stride, k) for k in range(1, radix)]
        held = assemble(pieces, stride, radix, size, step)
    def unpack(parts, previous):
        def body(*refs):
            second_out, first_out, stage, sems = refs[len(parts) + len(previous) :]
            core = lax.rem(lax.axis_index("lon"), 2)
            for i, (_, k, side) in enumerate(parts):
                for tap, value in enumerate(load_part(refs[i][...].astype(f32), height_of_part, channels)):
                    stage[i, tap] = value * scale
                start = pl.multiple_of((digit_of(2, group) ^ k) * height_of_part, height_of_part)
                for which, out in enumerate((second_out, first_out)):

                    @pl.when((core + side) % 2 == which)
                    def _():
                        for tap in range(9):
                            target = out.at[tap // 3, tap % 3, pl.ds(start, height_of_part)]
                            pltpu.make_async_copy(stage.at[i, tap], target, sems.at[9 * i + tap]).start()

            for i in range(len(parts)):
                for tap in range(9):
                    target = second_out.at[tap // 3, tap % 3, pl.ds(0, height_of_part)]
                    pltpu.make_async_copy(stage.at[i, tap], target, sems.at[9 * i + tap]).wait()

        count_in = len(parts)
        return list(
            call(
                body,
                [shape_of((3, 3, channels, channels), f32)] * 2,
                [array for array, _, _ in parts] + previous,
                [
                    pltpu.VMEM((count_in, 9, height_of_part, channels), f32),
                    pltpu.SemaphoreType.DMA((9 * count_in,)),
                ],
                name="unpack_gradients",
                far_args=tuple(range(count_in, count_in + len(previous))),
                far_outs=(0, 1),
                aliases={count_in + i: i for i in range(len(previous))},
            )
        )

    quarter = [held] + [swapped(held, count, 2, k) for k in range(1, group)]
    sibling = [swapped(held, count, 1, 1)]
    sibling += [swapped(after(q, input_gradient), count, 1, 1) for q in quarter[1:]]
    written = unpack([(part, k, 0) for k, part in enumerate(quarter)], [])
    written = unpack([(part, k, 1) for k, part in enumerate(sibling)], written)
    second_gradient, first_gradient = written
    return (input_gradient.reshape(height, width, channels), first_gradient, second_gradient)


def solution(mesh):
    placed = (P("lat", "lon", None), P("lat", "lon", None), P(), P())
    return jax.shard_map(
        shards,
        mesh=mesh,
        in_specs=placed,
        out_specs=(P("lat", "lon", None), P(), P()),
        check_vma=False,
    )
```

```python
import math

import jax
import jax.numpy as jnp
from jax import lax
from jax.experimental import pallas as pl
from jax.experimental.pallas import tpu as pltpu
from jax.sharding import PartitionSpec as P

FIRST_SPREAD = 32
SECOND_SPREAD = 64
LANES = 128
ROW_TILE = 16
G_SHARE = (7, 12)
X_SHARE = (49, 96)
VMEM_LIMIT = 20 * 1024 * 1024


def call(body, outs, args, scratch=(), flops=0, name=None, far_args=(), far_outs=(), aliases={}):
    moved = sum(a.size * a.dtype.itemsize for a in list(args) + list(outs))
    near, far = pl.BlockSpec(memory_space=pltpu.VMEM), pl.BlockSpec(memory_space=pltpu.HBM)
    return pl.pallas_call(
        body,
        out_shape=list(outs),
        in_specs=[far if i in far_args else near for i in range(len(args))],
        out_specs=[far if i in far_outs else near for i in range(len(outs))],
        scratch_shapes=list(scratch),
        input_output_aliases=aliases,
        compiler_params=pltpu.CompilerParams(vmem_limit_bytes=VMEM_LIMIT),
        cost_estimate=pl.CostEstimate(flops=flops, bytes_accessed=moved, transcendentals=0),
        name=name,
    )(*args)


def shape_of(shape, dtype):
    return jax.ShapeDtypeStruct(shape, dtype)


def packs(rows, channels):
    return channels % LANES * 2 == LANES and rows % (2 * ROW_TILE) == 0


def packed_shape(rows, channels):
    if not packs(rows, channels):
        return (rows, channels)
    full = channels // LANES
    return (rows * full + rows // 2, LANES)


def pack_into(refs, value):
    rows, channels = value.shape
    if packs(rows, channels):
        full = channels // LANES
        rest = value[:, full * LANES :]
        half = rows // 2
        tiles = [value[:, tile * LANES : (tile + 1) * LANES] for tile in range(full)]
        tiles.append(jnp.concatenate([rest[:half], rest[half:]], axis=1))
        value = jnp.concatenate(tiles, axis=0)
    begin = 0
    for ref in refs:
        ref[...] = value[begin : begin + ref.shape[0]]
        begin += ref.shape[0]


def unpacked(refs, rows, channels):
    parts = [ref[...] for ref in refs]
    ref = parts[0] if len(parts) == 1 else jnp.concatenate(parts, axis=0)
    if not packs(rows, channels):
        return ref
    full = channels // LANES
    rest = ref[full * rows :, :]
    width = channels - full * LANES
    tail = jnp.concatenate([rest[:, :width], rest[:, width:]], axis=0)
    return jnp.concatenate([ref[t * rows : (t + 1) * rows, :] for t in range(full)] + [tail], axis=1)


def extend(scratch, value, rim, width):
    rows = value.shape[0]
    scratch[width : width + rows, :] = value
    if rim is None:
        blank = jnp.zeros((width, value.shape[1]), value.dtype)
        scratch[:width, :] = blank
        scratch[width + rows :, :] = blank
    else:
        scratch[:width, :] = rim[:width, :]
        scratch[width + rows :, :] = rim[width:, :]


def row_blocks(rows):
    size = rows
    while size > 256 and size % 2 == 0 and size // 2 % ROW_TILE == 0:
        size //= 2
    return [(start, size) for start in range(0, rows, size)]


NT = (((1,), (1,)), ((), ()))
NN = (((1,), (0,)), ((), ()))


def conv_block(terms, start, size, width):
    total = None
    for ext, weight, b, flipped in terms:
        for a in (-1, 0, 1):
            tap = ext[start + (1 + a) * width : start + (1 + a) * width + size, :]
            kernel = weight[1 - a, 1 - b] if flipped else weight[1 + a, 1 + b]
            part = lax.dot_general(tap, kernel, NT if flipped else NN, preferred_element_type=jnp.float32)
            total = part if total is None else total + part
    return total


def part_rows(height, channels):
    full, width = divmod(channels, LANES)
    rows = 9 * height * full
    if width:
        rows += 9 * height // 2 if width * 2 == LANES else 9 * height
    return -(-rows // ROW_TILE) * ROW_TILE


def store_part(ref, start, end, blocks):
    height, channels = blocks[0].shape
    full, width = divmod(channels, LANES)
    row = start
    for block in blocks:
        for tile in range(full):
            ref[row : row + height, :] = block[:, tile * LANES : (tile + 1) * LANES]
            row += height
    rests = [block[:, full * LANES :] for block in blocks]
    if width and width * 2 != LANES:
        for rest in rests:
            ref[row : row + height, :width] = rest
            row += height
    elif width:
        for pair in range(0, 8, 2):
            ref[row : row + height, :] = jnp.concatenate([rests[pair], rests[pair + 1]], axis=1)
            row += height
        half = height // 2
        ref[row : row + half, :] = jnp.concatenate([rests[8][:half], rests[8][half:]], axis=1)
        row += half
    if row < end:
        ref[row:end, :] = jnp.zeros((end - row, LANES), ref.dtype)


def load_part(rows, height, channels):
    full, width = divmod(channels, LANES)
    parts = []
    for tap in range(9):
        at = tap * full * height
        parts.append([rows[at + t * height : at + (t + 1) * height] for t in range(full)])
    row = 9 * full * height
    if width and width * 2 != LANES:
        for tap in range(9):
            parts[tap].append(rows[row : row + height, :width])
            row += height
    elif width:
        for pair in range(0, 8, 2):
            both = rows[row : row + height]
            parts[pair].append(both[:, :width])
            parts[pair + 1].append(both[:, width:])
            row += height
        both = rows[row : row + height // 2]
        parts[8].append(jnp.concatenate([both[:, :width], both[:, width:]], axis=0))
    return [jnp.concatenate(p, axis=1) if len(p) > 1 else p[0] for p in parts]


def radices(count):
    found = []
    if count % 2 == 0:
        found.append(2)
        count //= 2
    while count % 4 == 0:
        found.append(4)
        count //= 4
    while count % 2 == 0:
        found.append(2)
        count //= 2
    return found if count == 1 else None


def swapped(value, count, stride, k):
    return lax.ppermute(value, "lon", [(i, i ^ (k * stride)) for i in range(count)])


def moved(value, steps):
    count = lax.axis_size("lon")
    if steps % count == 0:
        return value
    return lax.ppermute(value, "lon", [(i, (i + steps) % count) for i in range(count)])


def lat_rim(field):
    count = lax.axis_size("lat")
    if count == 1:
        return None
    north = lax.ppermute(field[-1], "lat", [(i, i + 1) for i in range(count - 1)])
    south = lax.ppermute(field[0], "lat", [(i + 1, i) for i in range(count - 1)])
    return jnp.stack([north, south])


def paired(spread, width):
    steps, rest = divmod(spread, width)
    return rest == 0 and lax.axis_size("lon") % (2 * steps) == 0


def side_of(spread, width):
    if not paired(spread, width):
        return 0
    return lax.rem(lax.axis_index("lon") // (spread // width), 2)


def inner_pairs(steps):
    return [(i, i + steps if i // steps % 2 == 0 else i - steps) for i in range(lax.axis_size("lon"))]


def outer_pairs(steps):
    count = lax.axis_size("lon")
    return [(i, (i - steps if i // steps % 2 == 0 else i + steps) % count) for i in range(count)]


def after(value, *others):
    return lax.optimization_barrier((value, *others))[0]


def beside(field, packed, spread, pack):
    width = field.shape[1]
    steps, rest = divmod(spread, width)
    if paired(spread, width):
        return (
            [lax.ppermute(packed, "lon", inner_pairs(steps))],
            [lax.ppermute(packed, "lon", outer_pairs(steps))],
        )
    if rest == 0:
        return [moved(packed, -steps)], [moved(packed, steps)]
    cut = width - rest
    west = jnp.concatenate([moved(field[:, cut:], steps + 1), moved(field[:, :cut], steps)], axis=1)
    east = jnp.concatenate([moved(field[:, rest:], -steps), moved(field[:, :rest], -steps - 1)], axis=1)
    return [pack(east)], [pack(west)]


def onward_pairs(steps):
    count = lax.axis_size("lon")
    return [(i, (i + 2 * steps if i // steps % 2 == 0 else i - 2 * steps) % count) for i in range(count)]


def shards(inputs, cotangent, first_weight, second_weight):
    height, width, channels = inputs.shape
    rows = height * width
    count = lax.axis_size("lon")
    scale = 1.0 / math.sqrt(rows * lax.axis_size("lat") * count)
    bf16, f32 = jnp.bfloat16, jnp.float32
    pshape = packed_shape(rows, channels)
    ext_rows = rows + 2 * width
    ext_shape, turned_shape = (ext_rows, channels), (3 * channels, rows)
    ext = pltpu.VMEM(ext_shape, bf16)
    tap_flops = 2 * rows * channels * channels
    blocks = row_blocks(rows)

    def pack_body(source, *targets):
        pack_into(targets, source[...])

    def pack_one(field, share=None):
        sizes = [pshape[0]]
        if share is not None:
            first = max(pshape[0] * share[0] // share[1] // ROW_TILE, 1) * ROW_TILE
            sizes = [first, pshape[0] - first]
        shapes = [shape_of((size, pshape[1]), bf16) for size in sizes]
        packed = call(pack_body, shapes, [field.reshape(rows, channels)], name="pack")
        return packed[0] if share is None else packed

    def rims_of(field, spread):
        rim = lat_rim(field)
        if rim is None:
            return []
        inner, outer = beside(rim, rim, spread, lambda r: r)
        return [r.reshape(2 * width, channels) for r in (rim, *inner, *outer)]

    def turn(target, source):
        for a in range(3):
            value = source[a * width : a * width + rows, :].astype(f32).T
            target[a * channels : (a + 1) * channels, :] = value.astype(bf16)

    def near_part(field, weight, inner, rims, spread, flipped, name, keep=None):
        def body(x_ref, w_ref, *rest):
            refs, rest = rest[: len(inner)], rest[len(inner) :]
            (own_rim, inner_rim), (part, *rest) = (rest[:2], rest[2:]) if rimmed else ((None, None), rest)
            e0, e1 = rest[:2] if keep == "rims" else rest[-2:]
            extend(e0, x_ref[...], own_rim, width)
            extend(e1, unpacked(refs, rows, channels), inner_rim, width)
            b = 1 - 2 * side_of(spread, width)
            for start, size in blocks:
                part[start : start + size, :] = conv_block(
                    [(e0, w_ref, 0, flipped), (e1, w_ref, b, flipped)], start, size, width
                )
            if keep == "turned":
                turn(rest[0], e0)
                turn(rest[1], e1)

        args = [field, weight] + inner + rims[:2]
        kept = {"rims": ext_shape, "turned": turned_shape}
        outs = [shape_of((rows, channels), f32)] + ([shape_of(kept[keep], bf16)] * 2 if keep else [])
        return call(body, outs, args, [] if keep == "rims" else [ext, ext], 6 * tap_flops, name)

    def far_part(part_ref, scratch, w_ref, spread, flipped, start, size):
        b = 2 * side_of(spread, width) - 1
        return part_ref[start : start + size, :] + conv_block([(scratch, w_ref, b, flipped)], start, size, width)

    x = inputs.reshape(rows, channels)
    g = cotangent.reshape(rows, channels)
    x_rims = rims_of(inputs, FIRST_SPREAD)
    g_rims = rims_of(cotangent, SECOND_SPREAD)
    rimmed = bool(x_rims)

    if paired(SECOND_SPREAD, width):
        steps = SECOND_SPREAD // width
        g_packed = pack_one(cotangent, G_SHARE)
        g_inner = [lax.ppermute(part, "lon", inner_pairs(steps)) for part in g_packed]
        g_outer = [
            lax.ppermute(g_inner[0], "lon", onward_pairs(steps)),
            lax.ppermute(g_packed[1], "lon", outer_pairs(steps)),
        ]
    else:
        g_inner, g_outer = beside(cotangent, pack_one(cotangent), SECOND_SPREAD, pack_one)
    if paired(FIRST_SPREAD, width):
        steps = FIRST_SPREAD // width
        x_packed = pack_one(after(inputs, *g_packed), X_SHARE)
        x_inner = [lax.ppermute(part, "lon", inner_pairs(steps)) for part in x_packed]
        x_outer = [lax.ppermute(part, "lon", outer_pairs(steps)) for part in x_packed]
    else:
        x_inner, x_outer = beside(inputs, pack_one(inputs), FIRST_SPREAD, pack_one)
    part1, x_own, x_near = near_part(
        x, first_weight, x_inner, x_rims, FIRST_SPREAD, False, "near_pre_act", "turned"
    )
    part2, g_own, g_near = near_part(
        g, second_weight, g_inner, g_rims, SECOND_SPREAD, True, "near_hidden_grad", "rims"
    )

    def hidden_body(part_ref, w_ref, *rest):
        side_refs, rest = rest[: len(x_outer)], rest[len(x_outer) :]
        (rim,), (hidden_t, slope, turned, se, hid) = (rest[:1], rest[1:]) if rimmed else ((None,), rest)
        extend(se, unpacked(side_refs, rows, channels), rim, width)
        for start, size in blocks:
            act = far_part(part_ref, se, w_ref, FIRST_SPREAD, False, start, size)
            sigma = jax.nn.sigmoid(act)
            slope[start : start + size, :] = sigma * (1.0 + act * (1.0 - sigma))
            hid[start : start + size, :] = (act * sigma).astype(bf16).astype(f32)
        hidden_t[...] = hid[...].T.astype(bf16)
        turn(turned, se)

    hidden_t, slope, x_far = call(
        hidden_body,
        [shape_of((channels, rows), bf16), shape_of((rows, channels), f32), shape_of(turned_shape, bf16)],
        [part1, first_weight] + x_outer + x_rims[2:],
        [ext, pltpu.VMEM((rows, channels), f32)],
        flops=3 * tap_flops,
        name="hidden",
    )

    def second_sums(hid_ref, field):
        return [
            jnp.dot(hid_ref[...], field[(1 - a) * width : (1 - a) * width + rows, :], preferred_element_type=f32)
            for a in (-1, 0, 1)
        ]

    def grad_body(part_ref, slope_ref, w_ref, *rest):
        side_refs, rest = rest[: len(g_outer)], rest[len(g_outer) :]
        (rim,), (pre_grad, packed, se) = (rest[:1], rest[1:]) if rimmed else ((None,), rest)
        extend(se, unpacked(side_refs, rows, channels), rim, width)
        for start, size in blocks:
            grad = far_part(part_ref, se, w_ref, SECOND_SPREAD, True, start, size)
            pre_grad[start : start + size, :] = (grad * slope_ref[start : start + size, :]).astype(bf16)
        pack_into([packed], pre_grad[...])

    pre_grad, pre_packed, g_far = call(
        grad_body,
        [shape_of((rows, channels), bf16), shape_of(pshape, bf16), shape_of(ext_shape, bf16)],
        [part2, slope, second_weight] + g_outer + g_rims[2:],
        flops=3 * tap_flops,
        name="pre_grad",
    )

    stages = radices(count)
    group = stages[1]
    later = stages[2:]
    height_of_part = channels // group
    part_size = part_rows(height_of_part, channels)
    sizes = []
    for radix in later:
        size = -(-part_size // (radix * ROW_TILE)) * ROW_TILE
        step = (part_size - size) // (radix - 1)
        if len(later) > 1 or step % ROW_TILE or step * (radix - 1) + size != part_size:
            part_size = -(-part_size // (math.prod(later) * ROW_TILE)) * math.prod(later) * ROW_TILE
            break
        sizes = [(size, step)]
    if len(sizes) < len(later):
        sizes, size = [], part_size
        for radix in later:
            size //= radix
            sizes.append((size, size))
    flat = group * part_size

    def kernel_gradient(which):
        def body(hid_ref, g0, g1, g2, pre_ref, x0, x1, x2, out, *scratch):
            flat_ref = scratch[0] if scratch else out
            chosen = which(lax.rem(lax.axis_index("lon"), 2))

            def put(mid, inner, outer, spread, sign):
                east_first = side_of(spread, width) == 0
                nine = []
                for at in range(3):
                    east = jnp.where(east_first, inner[at], outer[at])
                    west = jnp.where(east_first, outer[at], inner[at])
                    nine += [west, mid[at], east][::sign]
                for c in range(group):
                    rows_of = slice(c * height_of_part, (c + 1) * height_of_part)
                    store_part(flat_ref, c * part_size, (c + 1) * part_size, [block[rows_of] for block in nine])

            @pl.when(chosen == 0)
            def _():
                put(*(second_sums(hid_ref, ref) for ref in (g0, g1, g2)), SECOND_SPREAD, -1)

            @pl.when(chosen == 1)
            def _():
                sums = [jnp.dot(ref[...], pre_ref[...], preferred_element_type=f32) for ref in (x0, x1, x2)]
                put(*([t[a * channels : (a + 1) * channels] for a in range(3)] for t in sums), FIRST_SPREAD, 1)

            if scratch:
                out[...] = flat_ref[...].astype(out.dtype)

        return body

    fields = [hidden_t, g_own, g_near, g_far, pre_grad, x_own, x_near, x_far]
    flat_scratch = pltpu.VMEM((flat, LANES), f32)
    (send,) = call(
        kernel_gradient(lambda core: 1 - core),
        [shape_of((flat, LANES), bf16)],
        fields,
        [flat_scratch],
        flops=9 * tap_flops,
        name="sibling_kernel_gradient",
    )
    received = [swapped(send, count, 1, 1)]
    (own,) = call(
        kernel_gradient(lambda core: core),
        [shape_of((flat, LANES), f32)],
        fields,
        flops=9 * tap_flops,
        name="own_kernel_gradient",
    )

    def digit_of(stride, radix):
        return lax.rem(lax.axis_index("lon") // stride, radix)

    def combine(own, received, stride, radix, size, step):
        def body(own_ref, *refs):
            got, (mine, *sends) = refs[: len(received)], refs[len(received) :]
            digit = digit_of(stride, radix)
            for k, target in enumerate([mine] + sends):
                at = pl.ds(pl.multiple_of((digit ^ k) * step, ROW_TILE), size)
                value = own_ref[at, :]
                for ref in got:
                    value = value + ref[at, :].astype(f32)
                target[...] = value.astype(target.dtype)

        outs = [shape_of((size, LANES), f32)] + [shape_of((size, LANES), bf16)] * (radix - 1)
        return call(body, outs, [own] + received, name="combine")

    stride = 2
    plane_got = None
    for radix, (size, step) in zip(stages[1:], [(part_size, part_size)] + sizes):
        own, *sends = combine(own, received, stride, radix, size, step)
        received = [swapped(part, count, stride, k + 1) for k, part in enumerate(sends)]
        plane_got = received[-1] if plane_got is None else plane_got
        stride *= radix
    pre_field = pre_grad.reshape(height, width, channels)
    p_rims = rims_of(pre_field, FIRST_SPREAD)
    if paired(FIRST_SPREAD, width):
        steps = FIRST_SPREAD // width
        p_inner = [lax.ppermute(pre_packed, "lon", inner_pairs(steps))]
        p_outer = [lax.ppermute(after(pre_packed, plane_got), "lon", outer_pairs(steps))]
    else:
        p_inner, p_outer = beside(pre_field, pre_packed, FIRST_SPREAD, pack_one)
    (part3,) = near_part(pre_grad, first_weight, p_inner, p_rims, FIRST_SPREAD, True, "near_input_gradient")

    def input_body(part_ref, w_ref, *rest):
        side_refs, rest = rest[: len(p_outer)], rest[len(p_outer) :]
        (rim,), (out, se) = (rest[:1], rest[1:]) if rimmed else ((None,), rest)
        extend(se, unpacked(side_refs, rows, channels), rim, width)
        for start, size in blocks:
            out[start : start + size, :] = far_part(part_ref, se, w_ref, FIRST_SPREAD, True, start, size).astype(bf16)

    (input_gradient,) = call(
        input_body,
        [shape_of((rows, channels), bf16)],
        [part3, first_weight] + p_outer + p_rims[2:],
        [ext],
        flops=3 * tap_flops,
        name="input_gradient",
    )

    def finish(own, received):
        if lax.axis_size("lat") > 1:
            for part in received:
                own = own + part.astype(f32)
            return lax.psum(own, "lat").astype(bf16)

        def body(own_ref, *refs):
            value = own_ref[...]
            for ref in refs[:-1]:
                value = value + ref[...].astype(f32)
            refs[-1][...] = value.astype(bf16)

        return call(body, [shape_of(own.shape, bf16)], [own] + received, name="combine_last")[0]

    def assemble(pieces, stride, radix, size, step):
        def body(*refs):
            digit = digit_of(stride, radix)
            for k, ref in enumerate(refs[:-1]):
                place = digit ^ k
                refs[-1][pl.ds(pl.multiple_of(place * step, ROW_TILE), step), :] = ref[:step, :]
                if step < size:

                    @pl.when(place == radix - 1)
                    def _():
                        refs[-1][radix * step :, :] = ref[step:, :]

        total = step * (radix - 1) + size
        return call(body, [shape_of((total, LANES), bf16)], pieces, name="assemble")[0]

    held = finish(own, received)
    stride = count
    for radix, (size, step) in reversed(list(zip(later, sizes))):
        stride //= radix
        pieces = [held] + [swapped(held, count, stride, k) for k in range(1, radix)]
        held = assemble(pieces, stride, radix, size, step)
    def unpack(parts, previous):
        def body(*refs):
            second_out, first_out, stage, sems = refs[len(parts) + len(previous) :]
            core = lax.rem(lax.axis_index("lon"), 2)
            for i, (_, k, side) in enumerate(parts):
                for tap, value in enumerate(load_part(refs[i][...].astype(f32), height_of_part, channels)):
                    stage[i, tap // 3, tap % 3] = value * scale
                start = pl.multiple_of((digit_of(2, group) ^ k) * height_of_part, height_of_part)
                for which, out in enumerate((second_out, first_out)):

                    @pl.when((core + side) % 2 == which)
                    def _():
                        target = out.at[:, :, pl.ds(start, height_of_part)]
                        pltpu.make_async_copy(stage.at[i], target, sems.at[i]).start()

            for i in range(len(parts)):
                target = second_out.at[:, :, pl.ds(0, height_of_part)]
                pltpu.make_async_copy(stage.at[i], target, sems.at[i]).wait()

        count_in = len(parts)
        return list(
            call(
                body,
                [shape_of((3, 3, channels, channels), f32)] * 2,
                [array for array, _, _ in parts] + previous,
                [
                    pltpu.VMEM((count_in, 3, 3, height_of_part, channels), f32),
                    pltpu.SemaphoreType.DMA((count_in,)),
                ],
                name="unpack_gradients",
                far_args=tuple(range(count_in, count_in + len(previous))),
                far_outs=(0, 1),
                aliases={count_in + i: i for i in range(len(previous))},
            )
        )

    quarter = [held] + [swapped(held, count, 2, k) for k in range(1, group)]
    sibling = [swapped(held, count, 1, 1)]
    sibling += [swapped(after(q, input_gradient), count, 1, 1) for q in quarter[1:]]
    written = unpack([(part, k, 0) for k, part in enumerate(quarter)], [])
    written = unpack([(part, k, 1) for k, part in enumerate(sibling)], written)
    second_gradient, first_gradient = written
    return (input_gradient.reshape(height, width, channels), first_gradient, second_gradient)


def solution(mesh):
    placed = (P("lat", "lon", None), P("lat", "lon", None), P(), P())
    return jax.shard_map(
        shards,
        mesh=mesh,
        in_specs=placed,
        out_specs=(P("lat", "lon", None), P(), P()),
        check_vma=False,
    )
```

```python
import math

import jax
import jax.numpy as jnp
from jax import lax
from jax.experimental import pallas as pl
from jax.experimental.pallas import tpu as pltpu
from jax.sharding import PartitionSpec as P

FIRST_SPREAD = 32
SECOND_SPREAD = 64
LANES = 128
ROW_TILE = 16
G_SHARE = (7, 12)
X_SHARE = (49, 96)
VMEM_LIMIT = 20 * 1024 * 1024


def call(body, outs, args, scratch=(), flops=0, name=None, far_args=(), far_outs=(), aliases={}):
    moved = sum(a.size * a.dtype.itemsize for a in list(args) + list(outs))
    near, far = pl.BlockSpec(memory_space=pltpu.VMEM), pl.BlockSpec(memory_space=pltpu.HBM)
    return pl.pallas_call(
        body,
        out_shape=list(outs),
        in_specs=[far if i in far_args else near for i in range(len(args))],
        out_specs=[far if i in far_outs else near for i in range(len(outs))],
        scratch_shapes=list(scratch),
        input_output_aliases=aliases,
        compiler_params=pltpu.CompilerParams(vmem_limit_bytes=VMEM_LIMIT),
        cost_estimate=pl.CostEstimate(flops=flops, bytes_accessed=moved, transcendentals=0),
        name=name,
    )(*args)


def shape_of(shape, dtype):
    return jax.ShapeDtypeStruct(shape, dtype)


def packs(rows, channels):
    return channels % LANES * 2 == LANES and rows % (2 * ROW_TILE) == 0


def packed_shape(rows, channels):
    if not packs(rows, channels):
        return (rows, channels)
    full = channels // LANES
    return (rows * full + rows // 2, LANES)


def pack_into(refs, value):
    rows, channels = value.shape
    if packs(rows, channels):
        full = channels // LANES
        rest = value[:, full * LANES :]
        half = rows // 2
        tiles = [value[:, tile * LANES : (tile + 1) * LANES] for tile in range(full)]
        tiles.append(jnp.concatenate([rest[:half], rest[half:]], axis=1))
        value = jnp.concatenate(tiles, axis=0)
    begin = 0
    for ref in refs:
        ref[...] = value[begin : begin + ref.shape[0]]
        begin += ref.shape[0]


def unpacked(refs, rows, channels):
    parts = [ref[...] for ref in refs]
    ref = parts[0] if len(parts) == 1 else jnp.concatenate(parts, axis=0)
    if not packs(rows, channels):
        return ref
    full = channels // LANES
    rest = ref[full * rows :, :]
    width = channels - full * LANES
    tail = jnp.concatenate([rest[:, :width], rest[:, width:]], axis=0)
    return jnp.concatenate([ref[t * rows : (t + 1) * rows, :] for t in range(full)] + [tail], axis=1)


def extend(scratch, value, rim, width):
    rows = value.shape[0]
    scratch[width : width + rows, :] = value
    if rim is None:
        blank = jnp.zeros((width, value.shape[1]), value.dtype)
        scratch[:width, :] = blank
        scratch[width + rows :, :] = blank
    else:
        scratch[:width, :] = rim[:width, :]
        scratch[width + rows :, :] = rim[width:, :]


def row_blocks(rows):
    size = rows
    while size > 256 and size % 2 == 0 and size // 2 % ROW_TILE == 0:
        size //= 2
    return [(start, size) for start in range(0, rows, size)]


NT = (((1,), (1,)), ((), ()))
NN = (((1,), (0,)), ((), ()))


def conv_block(terms, start, size, width):
    total = None
    for ext, weight, b, flipped in terms:
        for a in (-1, 0, 1):
            tap = ext[start + (1 + a) * width : start + (1 + a) * width + size, :]
            kernel = weight[1 - a, 1 - b] if flipped else weight[1 + a, 1 + b]
            part = lax.dot_general(tap, kernel, NT if flipped else NN, preferred_element_type=jnp.float32)
            total = part if total is None else total + part
    return total


def part_rows(height, channels):
    full, width = divmod(channels, LANES)
    rows = 9 * height * full
    if width:
        rows += 9 * height // 2 if width * 2 == LANES else 9 * height
    return -(-rows // ROW_TILE) * ROW_TILE


def store_part(ref, start, end, blocks):
    height, channels = blocks[0].shape
    full, width = divmod(channels, LANES)
    row = start
    for block in blocks:
        for tile in range(full):
            ref[row : row + height, :] = block[:, tile * LANES : (tile + 1) * LANES]
            row += height
    rests = [block[:, full * LANES :] for block in blocks]
    if width and width * 2 != LANES:
        for rest in rests:
            ref[row : row + height, :width] = rest
            row += height
    elif width:
        for pair in range(0, 8, 2):
            ref[row : row + height, :] = jnp.concatenate([rests[pair], rests[pair + 1]], axis=1)
            row += height
        half = height // 2
        ref[row : row + half, :] = jnp.concatenate([rests[8][:half], rests[8][half:]], axis=1)
        row += half
    if row < end:
        ref[row:end, :] = jnp.zeros((end - row, LANES), ref.dtype)


def load_part(rows, height, channels):
    full, width = divmod(channels, LANES)
    parts = []
    for tap in range(9):
        at = tap * full * height
        parts.append([rows[at + t * height : at + (t + 1) * height] for t in range(full)])
    row = 9 * full * height
    if width and width * 2 != LANES:
        for tap in range(9):
            parts[tap].append(rows[row : row + height, :width])
            row += height
    elif width:
        for pair in range(0, 8, 2):
            both = rows[row : row + height]
            parts[pair].append(both[:, :width])
            parts[pair + 1].append(both[:, width:])
            row += height
        both = rows[row : row + height // 2]
        parts[8].append(jnp.concatenate([both[:, :width], both[:, width:]], axis=0))
    return [jnp.concatenate(p, axis=1) if len(p) > 1 else p[0] for p in parts]


def radices(count):
    found = []
    if count % 2 == 0:
        found.append(2)
        count //= 2
    while count % 4 == 0:
        found.append(4)
        count //= 4
    while count % 2 == 0:
        found.append(2)
        count //= 2
    return found if count == 1 else None


def swapped(value, count, stride, k):
    return lax.ppermute(value, "lon", [(i, i ^ (k * stride)) for i in range(count)])


def moved(value, steps):
    count = lax.axis_size("lon")
    if steps % count == 0:
        return value
    return lax.ppermute(value, "lon", [(i, (i + steps) % count) for i in range(count)])


def lat_rim(field):
    count = lax.axis_size("lat")
    if count == 1:
        return None
    north = lax.ppermute(field[-1], "lat", [(i, i + 1) for i in range(count - 1)])
    south = lax.ppermute(field[0], "lat", [(i + 1, i) for i in range(count - 1)])
    return jnp.stack([north, south])


def paired(spread, width):
    steps, rest = divmod(spread, width)
    return rest == 0 and lax.axis_size("lon") % (2 * steps) == 0


def side_of(spread, width):
    if not paired(spread, width):
        return 0
    return lax.rem(lax.axis_index("lon") // (spread // width), 2)


def inner_pairs(steps):
    return [(i, i + steps if i // steps % 2 == 0 else i - steps) for i in range(lax.axis_size("lon"))]


def outer_pairs(steps):
    count = lax.axis_size("lon")
    return [(i, (i - steps if i // steps % 2 == 0 else i + steps) % count) for i in range(count)]


def after(value, *others):
    return lax.optimization_barrier((value, *others))[0]


def beside(field, packed, spread, pack):
    width = field.shape[1]
    steps, rest = divmod(spread, width)
    if paired(spread, width):
        return (
            [lax.ppermute(packed, "lon", inner_pairs(steps))],
            [lax.ppermute(packed, "lon", outer_pairs(steps))],
        )
    if rest == 0:
        return [moved(packed, -steps)], [moved(packed, steps)]
    cut = width - rest
    west = jnp.concatenate([moved(field[:, cut:], steps + 1), moved(field[:, :cut], steps)], axis=1)
    east = jnp.concatenate([moved(field[:, rest:], -steps), moved(field[:, :rest], -steps - 1)], axis=1)
    return [pack(east)], [pack(west)]


def onward_pairs(steps):
    count = lax.axis_size("lon")
    return [(i, (i + 2 * steps if i // steps % 2 == 0 else i - 2 * steps) % count) for i in range(count)]


def shards(inputs, cotangent, first_weight, second_weight):
    height, width, channels = inputs.shape
    rows = height * width
    count = lax.axis_size("lon")
    scale = 1.0 / math.sqrt(rows * lax.axis_size("lat") * count)
    bf16, f32 = jnp.bfloat16, jnp.float32
    pshape = packed_shape(rows, channels)
    ext_rows = rows + 2 * width
    ext_shape, turned_shape = (ext_rows, channels), (3 * channels, rows)
    ext = pltpu.VMEM(ext_shape, bf16)
    tap_flops = 2 * rows * channels * channels
    blocks = row_blocks(rows)

    def pack_body(source, *targets):
        pack_into(targets, source[...])

    def pack_one(field, share=None):
        sizes = [pshape[0]]
        if share is not None:
            first = max(pshape[0] * share[0] // share[1] // ROW_TILE, 1) * ROW_TILE
            sizes = [first, pshape[0] - first]
        shapes = [shape_of((size, pshape[1]), bf16) for size in sizes]
        packed = call(pack_body, shapes, [field.reshape(rows, channels)], name="pack")
        return packed[0] if share is None else packed

    def rims_of(field, spread):
        rim = lat_rim(field)
        if rim is None:
            return []
        inner, outer = beside(rim, rim, spread, lambda r: r)
        return [r.reshape(2 * width, channels) for r in (rim, *inner, *outer)]

    def turn(target, source):
        for a in range(3):
            value = source[a * width : a * width + rows, :].astype(f32).T
            target[a * channels : (a + 1) * channels, :] = value.astype(bf16)

    def near_part(field, weight, inner, rims, spread, flipped, name, keep=None):
        def body(x_ref, w_ref, *rest):
            refs, rest = rest[: len(inner)], rest[len(inner) :]
            (own_rim, inner_rim), (part, *rest) = (rest[:2], rest[2:]) if rimmed else ((None, None), rest)
            e0, e1 = rest[:2] if keep == "rims" else rest[-2:]
            extend(e0, x_ref[...], own_rim, width)
            extend(e1, unpacked(refs, rows, channels), inner_rim, width)
            b = 1 - 2 * side_of(spread, width)
            for start, size in blocks:
                part[start : start + size, :] = conv_block(
                    [(e0, w_ref, 0, flipped), (e1, w_ref, b, flipped)], start, size, width
                )
            if keep == "turned":
                turn(rest[0], e0)
                turn(rest[1], e1)

        args = [field, weight] + inner + rims[:2]
        kept = {"rims": ext_shape, "turned": turned_shape}
        outs = [shape_of((rows, channels), f32)] + ([shape_of(kept[keep], bf16)] * 2 if keep else [])
        return call(body, outs, args, [] if keep == "rims" else [ext, ext], 6 * tap_flops, name)

    def far_part(part_ref, scratch, w_ref, spread, flipped, start, size):
        b = 2 * side_of(spread, width) - 1
        return part_ref[start : start + size, :] + conv_block([(scratch, w_ref, b, flipped)], start, size, width)

    x = inputs.reshape(rows, channels)
    g = cotangent.reshape(rows, channels)
    x_rims = rims_of(inputs, FIRST_SPREAD)
    g_rims = rims_of(cotangent, SECOND_SPREAD)
    rimmed = bool(x_rims)

    if paired(SECOND_SPREAD, width):
        steps = SECOND_SPREAD // width
        g_packed = pack_one(cotangent, G_SHARE)
        g_inner = [lax.ppermute(part, "lon", inner_pairs(steps)) for part in g_packed]
        g_outer = [
            lax.ppermute(g_inner[0], "lon", onward_pairs(steps)),
            lax.ppermute(g_packed[1], "lon", outer_pairs(steps)),
        ]
    else:
        g_inner, g_outer = beside(cotangent, pack_one(cotangent), SECOND_SPREAD, pack_one)
    if paired(FIRST_SPREAD, width):
        steps = FIRST_SPREAD // width
        x_packed = pack_one(after(inputs, *g_packed), X_SHARE)
        x_inner = [lax.ppermute(part, "lon", inner_pairs(steps)) for part in x_packed]
        x_outer = [lax.ppermute(part, "lon", outer_pairs(steps)) for part in x_packed]
    else:
        x_inner, x_outer = beside(inputs, pack_one(inputs), FIRST_SPREAD, pack_one)
    part1, x_own, x_near = near_part(
        x, first_weight, x_inner, x_rims, FIRST_SPREAD, False, "near_pre_act", "turned"
    )
    part2, g_own, g_near = near_part(
        g, second_weight, g_inner, g_rims, SECOND_SPREAD, True, "near_hidden_grad", "rims"
    )

    def hidden_body(part_ref, w_ref, *rest):
        side_refs, rest = rest[: len(x_outer)], rest[len(x_outer) :]
        (rim,), (hidden_t, slope, turned, se, hid) = (rest[:1], rest[1:]) if rimmed else ((None,), rest)
        extend(se, unpacked(side_refs, rows, channels), rim, width)
        for start, size in blocks:
            act = far_part(part_ref, se, w_ref, FIRST_SPREAD, False, start, size)
            sigma = jax.nn.sigmoid(act)
            slope[start : start + size, :] = sigma * (1.0 + act * (1.0 - sigma))
            hid[start : start + size, :] = (act * sigma).astype(bf16).astype(f32)
        hidden_t[...] = hid[...].T.astype(bf16)
        turn(turned, se)

    hidden_t, slope, x_far = call(
        hidden_body,
        [shape_of((channels, rows), bf16), shape_of((rows, channels), f32), shape_of(turned_shape, bf16)],
        [part1, first_weight] + x_outer + x_rims[2:],
        [ext, pltpu.VMEM((rows, channels), f32)],
        flops=3 * tap_flops,
        name="hidden",
    )

    def second_sums(hid_ref, field):
        return [
            jnp.dot(hid_ref[...], field[(1 - a) * width : (1 - a) * width + rows, :], preferred_element_type=f32)
            for a in (-1, 0, 1)
        ]

    def grad_body(part_ref, slope_ref, w_ref, *rest):
        side_refs, rest = rest[: len(g_outer)], rest[len(g_outer) :]
        (rim,), (pre_grad, se) = (rest[:1], rest[1:]) if rimmed else ((None,), rest)
        extend(se, unpacked(side_refs, rows, channels), rim, width)
        for start, size in blocks:
            grad = far_part(part_ref, se, w_ref, SECOND_SPREAD, True, start, size)
            pre_grad[start : start + size, :] = (grad * slope_ref[start : start + size, :]).astype(bf16)

    pre_grad, g_far = call(
        grad_body,
        [shape_of((rows, channels), bf16), shape_of(ext_shape, bf16)],
        [part2, slope, second_weight] + g_outer + g_rims[2:],
        flops=3 * tap_flops,
        name="pre_grad",
    )

    stages = radices(count)
    group = stages[1]
    later = stages[2:]
    height_of_part = channels // group
    part_size = part_rows(height_of_part, channels)
    sizes = []
    for radix in later:
        size = -(-part_size // (radix * ROW_TILE)) * ROW_TILE
        step = (part_size - size) // (radix - 1)
        if len(later) > 1 or step % ROW_TILE or step * (radix - 1) + size != part_size:
            part_size = -(-part_size // (math.prod(later) * ROW_TILE)) * math.prod(later) * ROW_TILE
            break
        sizes = [(size, step)]
    if len(sizes) < len(later):
        sizes, size = [], part_size
        for radix in later:
            size //= radix
            sizes.append((size, size))
    flat = group * part_size

    def kernel_gradient(which):
        def body(hid_ref, g0, g1, g2, pre_ref, x0, x1, x2, out, *scratch):
            flat_ref = scratch[0] if scratch else out
            chosen = which(lax.rem(lax.axis_index("lon"), 2))

            def put(mid, inner, outer, spread, sign):
                east_first = side_of(spread, width) == 0
                nine = []
                for at in range(3):
                    east = jnp.where(east_first, inner[at], outer[at])
                    west = jnp.where(east_first, outer[at], inner[at])
                    nine += [west, mid[at], east][::sign]
                for c in range(group):
                    rows_of = slice(c * height_of_part, (c + 1) * height_of_part)
                    store_part(flat_ref, c * part_size, (c + 1) * part_size, [block[rows_of] for block in nine])

            @pl.when(chosen == 0)
            def _():
                put(*(second_sums(hid_ref, ref) for ref in (g0, g1, g2)), SECOND_SPREAD, -1)

            @pl.when(chosen == 1)
            def _():
                sums = [jnp.dot(ref[...], pre_ref[...], preferred_element_type=f32) for ref in (x0, x1, x2)]
                put(*([t[a * channels : (a + 1) * channels] for a in range(3)] for t in sums), FIRST_SPREAD, 1)

            if scratch:
                out[...] = flat_ref[...].astype(out.dtype)

        return body

    fields = [hidden_t, g_own, g_near, g_far, pre_grad, x_own, x_near, x_far]
    flat_scratch = pltpu.VMEM((flat, LANES), f32)
    (send,) = call(
        kernel_gradient(lambda core: 1 - core),
        [shape_of((flat, LANES), bf16)],
        fields,
        [flat_scratch],
        flops=9 * tap_flops,
        name="sibling_kernel_gradient",
    )
    received = [swapped(send, count, 1, 1)]
    (own,) = call(
        kernel_gradient(lambda core: core),
        [shape_of((flat, LANES), f32)],
        fields,
        flops=9 * tap_flops,
        name="own_kernel_gradient",
    )

    def digit_of(stride, radix):
        return lax.rem(lax.axis_index("lon") // stride, radix)

    def combine(own, received, stride, radix, size, step):
        def body(own_ref, *refs):
            got, (mine, *sends) = refs[: len(received)], refs[len(received) :]
            digit = digit_of(stride, radix)
            for k, target in enumerate([mine] + sends):
                at = pl.ds(pl.multiple_of((digit ^ k) * step, ROW_TILE), size)
                value = own_ref[at, :]
                for ref in got:
                    value = value + ref[at, :].astype(f32)
                target[...] = value.astype(target.dtype)

        outs = [shape_of((size, LANES), f32)] + [shape_of((size, LANES), bf16)] * (radix - 1)
        return call(body, outs, [own] + received, name="combine")

    stride = 2
    plane_got = None
    for radix, (size, step) in zip(stages[1:], [(part_size, part_size)] + sizes):
        own, *sends = combine(own, received, stride, radix, size, step)
        received = [swapped(part, count, stride, k + 1) for k, part in enumerate(sends)]
        plane_got = received[-1] if plane_got is None else plane_got
        stride *= radix
    pre_field = pre_grad.reshape(height, width, channels)
    pre_packed = pack_one(pre_field)
    p_rims = rims_of(pre_field, FIRST_SPREAD)
    if paired(FIRST_SPREAD, width):
        steps = FIRST_SPREAD // width
        p_inner = [lax.ppermute(pre_packed, "lon", inner_pairs(steps))]
        p_outer = [lax.ppermute(after(pre_packed, plane_got), "lon", outer_pairs(steps))]
    else:
        p_inner, p_outer = beside(pre_field, pre_packed, FIRST_SPREAD, pack_one)
    (part3,) = near_part(pre_grad, first_weight, p_inner, p_rims, FIRST_SPREAD, True, "near_input_gradient")

    def input_body(part_ref, w_ref, *rest):
        side_refs, rest = rest[: len(p_outer)], rest[len(p_outer) :]
        (rim,), (out, se) = (rest[:1], rest[1:]) if rimmed else ((None,), rest)
        extend(se, unpacked(side_refs, rows, channels), rim, width)
        for start, size in blocks:
            out[start : start + size, :] = far_part(part_ref, se, w_ref, FIRST_SPREAD, True, start, size).astype(bf16)

    (input_gradient,) = call(
        input_body,
        [shape_of((rows, channels), bf16)],
        [part3, first_weight] + p_outer + p_rims[2:],
        [ext],
        flops=3 * tap_flops,
        name="input_gradient",
    )

    def finish(own, received):
        if lax.axis_size("lat") > 1:
            for part in received:
                own = own + part.astype(f32)
            return lax.psum(own, "lat").astype(bf16)

        def body(own_ref, *refs):
            value = own_ref[...]
            for ref in refs[:-1]:
                value = value + ref[...].astype(f32)
            refs[-1][...] = value.astype(bf16)

        return call(body, [shape_of(own.shape, bf16)], [own] + received, name="combine_last")[0]

    def assemble(pieces, stride, radix, size, step):
        def body(*refs):
            digit = digit_of(stride, radix)
            for k, ref in enumerate(refs[:-1]):
                place = digit ^ k
                refs[-1][pl.ds(pl.multiple_of(place * step, ROW_TILE), step), :] = ref[:step, :]
                if step < size:

                    @pl.when(place == radix - 1)
                    def _():
                        refs[-1][radix * step :, :] = ref[step:, :]

        total = step * (radix - 1) + size
        return call(body, [shape_of((total, LANES), bf16)], pieces, name="assemble")[0]

    held = finish(own, received)
    stride = count
    for radix, (size, step) in reversed(list(zip(later, sizes))):
        stride //= radix
        pieces = [held] + [swapped(held, count, stride, k) for k in range(1, radix)]
        held = assemble(pieces, stride, radix, size, step)
    def unpack(parts, previous):
        def body(*refs):
            second_out, first_out, stage, sems = refs[len(parts) + len(previous) :]
            core = lax.rem(lax.axis_index("lon"), 2)
            for i, (_, k, side) in enumerate(parts):
                for tap, value in enumerate(load_part(refs[i][...].astype(f32), height_of_part, channels)):
                    stage[i, tap // 3, tap % 3] = value * scale
                start = pl.multiple_of((digit_of(2, group) ^ k) * height_of_part, height_of_part)
                for which, out in enumerate((second_out, first_out)):

                    @pl.when((core + side) % 2 == which)
                    def _():
                        target = out.at[:, :, pl.ds(start, height_of_part)]
                        pltpu.make_async_copy(stage.at[i], target, sems.at[i]).start()

            for i in range(len(parts)):
                target = second_out.at[:, :, pl.ds(0, height_of_part)]
                pltpu.make_async_copy(stage.at[i], target, sems.at[i]).wait()

        count_in = len(parts)
        return list(
            call(
                body,
                [shape_of((3, 3, channels, channels), f32)] * 2,
                [array for array, _, _ in parts] + previous,
                [
                    pltpu.VMEM((count_in, 3, 3, height_of_part, channels), f32),
                    pltpu.SemaphoreType.DMA((count_in,)),
                ],
                name="unpack_gradients",
                far_args=tuple(range(count_in, count_in + len(previous))),
                far_outs=(0, 1),
                aliases={count_in + i: i for i in range(len(previous))},
            )
        )

    quarter = [held] + [swapped(held, count, 2, k) for k in range(1, group)]
    sibling = [swapped(held, count, 1, 1)]
    sibling += [swapped(after(q, input_gradient), count, 1, 1) for q in quarter[1:]]
    written = unpack([(part, k, 0) for k, part in enumerate(quarter)], [])
    written = unpack([(part, k, 1) for k, part in enumerate(sibling)], written)
    second_gradient, first_gradient = written
    return (input_gradient.reshape(height, width, channels), first_gradient, second_gradient)


def solution(mesh):
    placed = (P("lat", "lon", None), P("lat", "lon", None), P(), P())
    return jax.shard_map(
        shards,
        mesh=mesh,
        in_specs=placed,
        out_specs=(P("lat", "lon", None), P(), P()),
        check_vma=False,
    )
```

```python
import math

import jax
import jax.numpy as jnp
from jax import lax
from jax.experimental import pallas as pl
from jax.experimental.pallas import tpu as pltpu
from jax.sharding import PartitionSpec as P

FIRST_SPREAD = 32
SECOND_SPREAD = 64
LANES = 128
ROW_TILE = 16
G_SHARE = (7, 12)
X_SHARE = (49, 96)
VMEM_LIMIT = 20 * 1024 * 1024


def call(body, outs, args, scratch=(), flops=0, name=None, far_args=(), far_outs=(), aliases={}):
    moved = sum(a.size * a.dtype.itemsize for a in list(args) + list(outs))
    near, far = pl.BlockSpec(memory_space=pltpu.VMEM), pl.BlockSpec(memory_space=pltpu.HBM)
    return pl.pallas_call(
        body,
        out_shape=list(outs),
        in_specs=[far if i in far_args else near for i in range(len(args))],
        out_specs=[far if i in far_outs else near for i in range(len(outs))],
        scratch_shapes=list(scratch),
        input_output_aliases=aliases,
        compiler_params=pltpu.CompilerParams(vmem_limit_bytes=VMEM_LIMIT),
        cost_estimate=pl.CostEstimate(flops=flops, bytes_accessed=moved, transcendentals=0),
        name=name,
    )(*args)


def shape_of(shape, dtype):
    return jax.ShapeDtypeStruct(shape, dtype)


def packs(rows, channels):
    return channels % LANES * 2 == LANES and rows % (2 * ROW_TILE) == 0


def packed_shape(rows, channels):
    if not packs(rows, channels):
        return (rows, channels)
    full = channels // LANES
    return (rows * full + rows // 2, LANES)


def pack_into(refs, value):
    rows, channels = value.shape
    if packs(rows, channels):
        full = channels // LANES
        rest = value[:, full * LANES :]
        half = rows // 2
        tiles = [value[:, tile * LANES : (tile + 1) * LANES] for tile in range(full)]
        tiles.append(jnp.concatenate([rest[:half], rest[half:]], axis=1))
        value = jnp.concatenate(tiles, axis=0)
    begin = 0
    for ref in refs:
        ref[...] = value[begin : begin + ref.shape[0]]
        begin += ref.shape[0]


def unpacked(refs, rows, channels):
    parts = [ref[...] for ref in refs]
    ref = parts[0] if len(parts) == 1 else jnp.concatenate(parts, axis=0)
    if not packs(rows, channels):
        return ref
    full = channels // LANES
    rest = ref[full * rows :, :]
    width = channels - full * LANES
    tail = jnp.concatenate([rest[:, :width], rest[:, width:]], axis=0)
    return jnp.concatenate([ref[t * rows : (t + 1) * rows, :] for t in range(full)] + [tail], axis=1)


def extend(scratch, value, rim, width):
    rows = value.shape[0]
    scratch[width : width + rows, :] = value
    if rim is None:
        blank = jnp.zeros((width, value.shape[1]), value.dtype)
        scratch[:width, :] = blank
        scratch[width + rows :, :] = blank
    else:
        scratch[:width, :] = rim[:width, :]
        scratch[width + rows :, :] = rim[width:, :]


def row_blocks(rows):
    size = rows
    while size > 512 and size % 2 == 0 and size // 2 % ROW_TILE == 0:
        size //= 2
    return [(start, size) for start in range(0, rows, size)]


NT = (((1,), (1,)), ((), ()))
NN = (((1,), (0,)), ((), ()))


def conv_block(terms, start, size, width):
    total = None
    for ext, weight, b, flipped in terms:
        for a in (-1, 0, 1):
            tap = ext[start + (1 + a) * width : start + (1 + a) * width + size, :]
            kernel = weight[1 - a, 1 - b] if flipped else weight[1 + a, 1 + b]
            part = lax.dot_general(tap, kernel, NT if flipped else NN, preferred_element_type=jnp.float32)
            total = part if total is None else total + part
    return total


def part_rows(height, channels):
    full, width = divmod(channels, LANES)
    rows = 9 * height * full
    if width:
        rows += 9 * height // 2 if width * 2 == LANES else 9 * height
    return -(-rows // ROW_TILE) * ROW_TILE


def store_part(ref, start, end, blocks):
    height, channels = blocks[0].shape
    full, width = divmod(channels, LANES)
    row = start
    for block in blocks:
        for tile in range(full):
            ref[row : row + height, :] = block[:, tile * LANES : (tile + 1) * LANES]
            row += height
    rests = [block[:, full * LANES :] for block in blocks]
    if width and width * 2 != LANES:
        for rest in rests:
            ref[row : row + height, :width] = rest
            row += height
    elif width:
        for pair in range(0, 8, 2):
            ref[row : row + height, :] = jnp.concatenate([rests[pair], rests[pair + 1]], axis=1)
            row += height
        half = height // 2
        ref[row : row + half, :] = jnp.concatenate([rests[8][:half], rests[8][half:]], axis=1)
        row += half
    if row < end:
        ref[row:end, :] = jnp.zeros((end - row, LANES), ref.dtype)


def load_part(rows, height, channels):
    full, width = divmod(channels, LANES)
    parts = []
    for tap in range(9):
        at = tap * full * height
        parts.append([rows[at + t * height : at + (t + 1) * height] for t in range(full)])
    row = 9 * full * height
    if width and width * 2 != LANES:
        for tap in range(9):
            parts[tap].append(rows[row : row + height, :width])
            row += height
    elif width:
        for pair in range(0, 8, 2):
            both = rows[row : row + height]
            parts[pair].append(both[:, :width])
            parts[pair + 1].append(both[:, width:])
            row += height
        both = rows[row : row + height // 2]
        parts[8].append(jnp.concatenate([both[:, :width], both[:, width:]], axis=0))
    return [jnp.concatenate(p, axis=1) if len(p) > 1 else p[0] for p in parts]


def radices(count):
    found = []
    if count % 2 == 0:
        found.append(2)
        count //= 2
    while count % 4 == 0:
        found.append(4)
        count //= 4
    while count % 2 == 0:
        found.append(2)
        count //= 2
    return found if count == 1 else None


def swapped(value, count, stride, k):
    return lax.ppermute(value, "lon", [(i, i ^ (k * stride)) for i in range(count)])


def moved(value, steps):
    count = lax.axis_size("lon")
    if steps % count == 0:
        return value
    return lax.ppermute(value, "lon", [(i, (i + steps) % count) for i in range(count)])


def lat_rim(field):
    count = lax.axis_size("lat")
    if count == 1:
        return None
    north = lax.ppermute(field[-1], "lat", [(i, i + 1) for i in range(count - 1)])
    south = lax.ppermute(field[0], "lat", [(i + 1, i) for i in range(count - 1)])
    return jnp.stack([north, south])


def paired(spread, width):
    steps, rest = divmod(spread, width)
    return rest == 0 and lax.axis_size("lon") % (2 * steps) == 0


def side_of(spread, width):
    if not paired(spread, width):
        return 0
    return lax.rem(lax.axis_index("lon") // (spread // width), 2)


def inner_pairs(steps):
    return [(i, i + steps if i // steps % 2 == 0 else i - steps) for i in range(lax.axis_size("lon"))]


def outer_pairs(steps):
    count = lax.axis_size("lon")
    return [(i, (i - steps if i // steps % 2 == 0 else i + steps) % count) for i in range(count)]


def after(value, *others):
    return lax.optimization_barrier((value, *others))[0]


def beside(field, packed, spread, pack):
    width = field.shape[1]
    steps, rest = divmod(spread, width)
    if paired(spread, width):
        return (
            [lax.ppermute(packed, "lon", inner_pairs(steps))],
            [lax.ppermute(packed, "lon", outer_pairs(steps))],
        )
    if rest == 0:
        return [moved(packed, -steps)], [moved(packed, steps)]
    cut = width - rest
    west = jnp.concatenate([moved(field[:, cut:], steps + 1), moved(field[:, :cut], steps)], axis=1)
    east = jnp.concatenate([moved(field[:, rest:], -steps), moved(field[:, :rest], -steps - 1)], axis=1)
    return [pack(east)], [pack(west)]


def onward_pairs(steps):
    count = lax.axis_size("lon")
    return [(i, (i + 2 * steps if i // steps % 2 == 0 else i - 2 * steps) % count) for i in range(count)]


def shards(inputs, cotangent, first_weight, second_weight):
    height, width, channels = inputs.shape
    rows = height * width
    count = lax.axis_size("lon")
    scale = 1.0 / math.sqrt(rows * lax.axis_size("lat") * count)
    bf16, f32 = jnp.bfloat16, jnp.float32
    pshape = packed_shape(rows, channels)
    ext_rows = rows + 2 * width
    ext_shape, turned_shape = (ext_rows, channels), (3 * channels, rows)
    ext = pltpu.VMEM(ext_shape, bf16)
    tap_flops = 2 * rows * channels * channels
    blocks = row_blocks(rows)

    def pack_body(source, *targets):
        pack_into(targets, source[...])

    def pack_one(field, share=None):
        sizes = [pshape[0]]
        if share is not None:
            first = max(pshape[0] * share[0] // share[1] // ROW_TILE, 1) * ROW_TILE
            sizes = [first, pshape[0] - first]
        shapes = [shape_of((size, pshape[1]), bf16) for size in sizes]
        packed = call(pack_body, shapes, [field.reshape(rows, channels)], name="pack")
        return packed[0] if share is None else packed

    def rims_of(field, spread):
        rim = lat_rim(field)
        if rim is None:
            return []
        inner, outer = beside(rim, rim, spread, lambda r: r)
        return [r.reshape(2 * width, channels) for r in (rim, *inner, *outer)]

    def turn(target, source):
        for a in range(3):
            value = source[a * width : a * width + rows, :].astype(f32).T
            target[a * channels : (a + 1) * channels, :] = value.astype(bf16)

    def near_part(field, weight, inner, rims, spread, flipped, name, keep=None):
        def body(x_ref, w_ref, *rest):
            refs, rest = rest[: len(inner)], rest[len(inner) :]
            (own_rim, inner_rim), (part, *rest) = (rest[:2], rest[2:]) if rimmed else ((None, None), rest)
            e0, e1 = rest[:2] if keep == "rims" else rest[-2:]
            extend(e0, x_ref[...], own_rim, width)
            extend(e1, unpacked(refs, rows, channels), inner_rim, width)
            b = 1 - 2 * side_of(spread, width)
            for start, size in blocks:
                part[start : start + size, :] = conv_block(
                    [(e0, w_ref, 0, flipped), (e1, w_ref, b, flipped)], start, size, width
                )
            if keep == "turned":
                turn(rest[0], e0)
                turn(rest[1], e1)

        args = [field, weight] + inner + rims[:2]
        kept = {"rims": ext_shape, "turned": turned_shape}
        outs = [shape_of((rows, channels), f32)] + ([shape_of(kept[keep], bf16)] * 2 if keep else [])
        return call(body, outs, args, [] if keep == "rims" else [ext, ext], 6 * tap_flops, name)

    def far_part(part_ref, scratch, w_ref, spread, flipped, start, size):
        b = 2 * side_of(spread, width) - 1
        return part_ref[start : start + size, :] + conv_block([(scratch, w_ref, b, flipped)], start, size, width)

    x = inputs.reshape(rows, channels)
    g = cotangent.reshape(rows, channels)
    x_rims = rims_of(inputs, FIRST_SPREAD)
    g_rims = rims_of(cotangent, SECOND_SPREAD)
    rimmed = bool(x_rims)

    if paired(SECOND_SPREAD, width):
        steps = SECOND_SPREAD // width
        g_packed = pack_one(cotangent, G_SHARE)
        g_inner = [lax.ppermute(part, "lon", inner_pairs(steps)) for part in g_packed]
        g_outer = [
            lax.ppermute(g_inner[0], "lon", onward_pairs(steps)),
            lax.ppermute(g_packed[1], "lon", outer_pairs(steps)),
        ]
    else:
        g_inner, g_outer = beside(cotangent, pack_one(cotangent), SECOND_SPREAD, pack_one)
    if paired(FIRST_SPREAD, width):
        steps = FIRST_SPREAD // width
        x_packed = pack_one(after(inputs, *g_packed), X_SHARE)
        x_inner = [lax.ppermute(part, "lon", inner_pairs(steps)) for part in x_packed]
        x_outer = [lax.ppermute(part, "lon", outer_pairs(steps)) for part in x_packed]
    else:
        x_inner, x_outer = beside(inputs, pack_one(inputs), FIRST_SPREAD, pack_one)
    part1, x_own, x_near = near_part(
        x, first_weight, x_inner, x_rims, FIRST_SPREAD, False, "near_pre_act", "turned"
    )
    part2, g_own, g_near = near_part(
        g, second_weight, g_inner, g_rims, SECOND_SPREAD, True, "near_hidden_grad", "rims"
    )

    def hidden_body(part_ref, w_ref, *rest):
        side_refs, rest = rest[: len(x_outer)], rest[len(x_outer) :]
        (rim,), (hidden_t, slope, turned, se, hid) = (rest[:1], rest[1:]) if rimmed else ((None,), rest)
        extend(se, unpacked(side_refs, rows, channels), rim, width)
        for start, size in blocks:
            act = far_part(part_ref, se, w_ref, FIRST_SPREAD, False, start, size)
            sigma = jax.nn.sigmoid(act)
            slope[start : start + size, :] = sigma * (1.0 + act * (1.0 - sigma))
            hid[start : start + size, :] = (act * sigma).astype(bf16).astype(f32)
        hidden_t[...] = hid[...].T.astype(bf16)
        turn(turned, se)

    hidden_t, slope, x_far = call(
        hidden_body,
        [shape_of((channels, rows), bf16), shape_of((rows, channels), f32), shape_of(turned_shape, bf16)],
        [part1, first_weight] + x_outer + x_rims[2:],
        [ext, pltpu.VMEM((rows, channels), f32)],
        flops=3 * tap_flops,
        name="hidden",
    )

    def second_sums(hid_ref, field):
        return [
            jnp.dot(hid_ref[...], field[(1 - a) * width : (1 - a) * width + rows, :], preferred_element_type=f32)
            for a in (-1, 0, 1)
        ]

    def grad_body(part_ref, slope_ref, w_ref, *rest):
        side_refs, rest = rest[: len(g_outer)], rest[len(g_outer) :]
        (rim,), (pre_grad, se) = (rest[:1], rest[1:]) if rimmed else ((None,), rest)
        extend(se, unpacked(side_refs, rows, channels), rim, width)
        for start, size in blocks:
            grad = far_part(part_ref, se, w_ref, SECOND_SPREAD, True, start, size)
            pre_grad[start : start + size, :] = (grad * slope_ref[start : start + size, :]).astype(bf16)

    pre_grad, g_far = call(
        grad_body,
        [shape_of((rows, channels), bf16), shape_of(ext_shape, bf16)],
        [part2, slope, second_weight] + g_outer + g_rims[2:],
        flops=3 * tap_flops,
        name="pre_grad",
    )

    stages = radices(count)
    group = stages[1]
    later = stages[2:]
    height_of_part = channels // group
    part_size = part_rows(height_of_part, channels)
    sizes = []
    for radix in later:
        size = -(-part_size // (radix * ROW_TILE)) * ROW_TILE
        step = (part_size - size) // (radix - 1)
        if len(later) > 1 or step % ROW_TILE or step * (radix - 1) + size != part_size:
            part_size = -(-part_size // (math.prod(later) * ROW_TILE)) * math.prod(later) * ROW_TILE
            break
        sizes = [(size, step)]
    if len(sizes) < len(later):
        sizes, size = [], part_size
        for radix in later:
            size //= radix
            sizes.append((size, size))
    flat = group * part_size

    def kernel_gradient(which):
        def body(hid_ref, g0, g1, g2, pre_ref, x0, x1, x2, out, *scratch):
            flat_ref = scratch[0] if scratch else out
            chosen = which(lax.rem(lax.axis_index("lon"), 2))

            def put(mid, inner, outer, spread, sign):
                east_first = side_of(spread, width) == 0
                nine = []
                for at in range(3):
                    east = jnp.where(east_first, inner[at], outer[at])
                    west = jnp.where(east_first, outer[at], inner[at])
                    nine += [west, mid[at], east][::sign]
                for c in range(group):
                    rows_of = slice(c * height_of_part, (c + 1) * height_of_part)
                    store_part(flat_ref, c * part_size, (c + 1) * part_size, [block[rows_of] for block in nine])

            @pl.when(chosen == 0)
            def _():
                put(*(second_sums(hid_ref, ref) for ref in (g0, g1, g2)), SECOND_SPREAD, -1)

            @pl.when(chosen == 1)
            def _():
                sums = [jnp.dot(ref[...], pre_ref[...], preferred_element_type=f32) for ref in (x0, x1, x2)]
                put(*([t[a * channels : (a + 1) * channels] for a in range(3)] for t in sums), FIRST_SPREAD, 1)

            if scratch:
                out[...] = flat_ref[...].astype(out.dtype)

        return body

    fields = [hidden_t, g_own, g_near, g_far, pre_grad, x_own, x_near, x_far]
    flat_scratch = pltpu.VMEM((flat, LANES), f32)
    (send,) = call(
        kernel_gradient(lambda core: 1 - core),
        [shape_of((flat, LANES), bf16)],
        fields,
        [flat_scratch],
        flops=9 * tap_flops,
        name="sibling_kernel_gradient",
    )
    received = [swapped(send, count, 1, 1)]
    (own,) = call(
        kernel_gradient(lambda core: core),
        [shape_of((flat, LANES), f32)],
        fields,
        flops=9 * tap_flops,
        name="own_kernel_gradient",
    )

    def digit_of(stride, radix):
        return lax.rem(lax.axis_index("lon") // stride, radix)

    def combine(own, received, stride, radix, size, step):
        def body(own_ref, *refs):
            got, (mine, *sends) = refs[: len(received)], refs[len(received) :]
            digit = digit_of(stride, radix)
            for k, target in enumerate([mine] + sends):
                at = pl.ds(pl.multiple_of((digit ^ k) * step, ROW_TILE), size)
                value = own_ref[at, :]
                for ref in got:
                    value = value + ref[at, :].astype(f32)
                target[...] = value.astype(target.dtype)

        outs = [shape_of((size, LANES), f32)] + [shape_of((size, LANES), bf16)] * (radix - 1)
        return call(body, outs, [own] + received, name="combine")

    stride = 2
    plane_got = None
    for radix, (size, step) in zip(stages[1:], [(part_size, part_size)] + sizes):
        own, *sends = combine(own, received, stride, radix, size, step)
        received = [swapped(part, count, stride, k + 1) for k, part in enumerate(sends)]
        plane_got = received[-1] if plane_got is None else plane_got
        stride *= radix
    pre_field = pre_grad.reshape(height, width, channels)
    pre_packed = pack_one(pre_field)
    p_rims = rims_of(pre_field, FIRST_SPREAD)
    if paired(FIRST_SPREAD, width):
        steps = FIRST_SPREAD // width
        p_inner = [lax.ppermute(pre_packed, "lon", inner_pairs(steps))]
        p_outer = [lax.ppermute(after(pre_packed, plane_got), "lon", outer_pairs(steps))]
    else:
        p_inner, p_outer = beside(pre_field, pre_packed, FIRST_SPREAD, pack_one)
    (part3,) = near_part(pre_grad, first_weight, p_inner, p_rims, FIRST_SPREAD, True, "near_input_gradient")

    def input_body(part_ref, w_ref, *rest):
        side_refs, rest = rest[: len(p_outer)], rest[len(p_outer) :]
        (rim,), (out, se) = (rest[:1], rest[1:]) if rimmed else ((None,), rest)
        extend(se, unpacked(side_refs, rows, channels), rim, width)
        for start, size in blocks:
            out[start : start + size, :] = far_part(part_ref, se, w_ref, FIRST_SPREAD, True, start, size).astype(bf16)

    (input_gradient,) = call(
        input_body,
        [shape_of((rows, channels), bf16)],
        [part3, first_weight] + p_outer + p_rims[2:],
        [ext],
        flops=3 * tap_flops,
        name="input_gradient",
    )

    def finish(own, received):
        if lax.axis_size("lat") > 1:
            for part in received:
                own = own + part.astype(f32)
            return lax.psum(own, "lat").astype(bf16)

        def body(own_ref, *refs):
            value = own_ref[...]
            for ref in refs[:-1]:
                value = value + ref[...].astype(f32)
            refs[-1][...] = value.astype(bf16)

        return call(body, [shape_of(own.shape, bf16)], [own] + received, name="combine_last")[0]

    def assemble(pieces, stride, radix, size, step):
        def body(*refs):
            digit = digit_of(stride, radix)
            for k, ref in enumerate(refs[:-1]):
                place = digit ^ k
                refs[-1][pl.ds(pl.multiple_of(place * step, ROW_TILE), step), :] = ref[:step, :]
                if step < size:

                    @pl.when(place == radix - 1)
                    def _():
                        refs[-1][radix * step :, :] = ref[step:, :]

        total = step * (radix - 1) + size
        return call(body, [shape_of((total, LANES), bf16)], pieces, name="assemble")[0]

    held = finish(own, received)
    stride = count
    for radix, (size, step) in reversed(list(zip(later, sizes))):
        stride //= radix
        pieces = [held] + [swapped(held, count, stride, k) for k in range(1, radix)]
        held = assemble(pieces, stride, radix, size, step)
    def unpack(parts, previous):
        def body(*refs):
            second_out, first_out, stage, sems = refs[len(parts) + len(previous) :]
            core = lax.rem(lax.axis_index("lon"), 2)
            for i, (_, k, side) in enumerate(parts):
                for tap, value in enumerate(load_part(refs[i][...].astype(f32), height_of_part, channels)):
                    stage[i, tap // 3, tap % 3] = value * scale
                start = pl.multiple_of((digit_of(2, group) ^ k) * height_of_part, height_of_part)
                for which, out in enumerate((second_out, first_out)):

                    @pl.when((core + side) % 2 == which)
                    def _():
                        target = out.at[:, :, pl.ds(start, height_of_part)]
                        pltpu.make_async_copy(stage.at[i], target, sems.at[i]).start()

            for i in range(len(parts)):
                target = second_out.at[:, :, pl.ds(0, height_of_part)]
                pltpu.make_async_copy(stage.at[i], target, sems.at[i]).wait()

        count_in = len(parts)
        return list(
            call(
                body,
                [shape_of((3, 3, channels, channels), f32)] * 2,
                [array for array, _, _ in parts] + previous,
                [
                    pltpu.VMEM((count_in, 3, 3, height_of_part, channels), f32),
                    pltpu.SemaphoreType.DMA((count_in,)),
                ],
                name="unpack_gradients",
                far_args=tuple(range(count_in, count_in + len(previous))),
                far_outs=(0, 1),
                aliases={count_in + i: i for i in range(len(previous))},
            )
        )

    quarter = [held] + [swapped(held, count, 2, k) for k in range(1, group)]
    sibling = [swapped(held, count, 1, 1)]
    sibling += [swapped(after(q, input_gradient), count, 1, 1) for q in quarter[1:]]
    written = unpack([(part, k, 0) for k, part in enumerate(quarter)], [])
    written = unpack([(part, k, 1) for k, part in enumerate(sibling)], written)
    second_gradient, first_gradient = written
    return (input_gradient.reshape(height, width, channels), first_gradient, second_gradient)


def solution(mesh):
    placed = (P("lat", "lon", None), P("lat", "lon", None), P(), P())
    return jax.shard_map(
        shards,
        mesh=mesh,
        in_specs=placed,
        out_specs=(P("lat", "lon", None), P(), P()),
        check_vma=False,
    )
```
